128 devices in a mesh: dp: 8 (over x, z_lo), seq: 8 (over y, core), tensor: 2 (over z_hi).
Axes of the slice: x: 4, y: 4, z: 4 (z_hi: 2, z_lo: 2; z = z_hi * 2 + z_lo), core: 2. Of those that a mesh axis runs over, the one named last changes fastest.
Arguments:
- tokens: bfloat16 [8, 2048, 1024], P('dp', 'seq'), may hold values from -6 to 6
- cotangent: bfloat16 [8, 2048, 1024], P('dp', 'seq'), may hold values from -6 to 6
- positions: int32 [8, 2048], P('dp', 'seq'), may hold values from 0 to 2047, as said below
- segments: int32 [8, 2048], P('dp', 'seq'), may hold values from 0 to 3, as said below
- attention_gain: bfloat16 [1024], replicated, may hold values from 0.5 to 1.5
- query_weight: bfloat16 [1024, 2048], P(None, 'tensor'), may hold values from -0.1875 to 0.1875
- key_weight: bfloat16 [1024, 1024], P(None, 'tensor'), may hold values from -0.1875 to 0.1875
- value_weight: bfloat16 [1024, 1024], P(None, 'tensor'), may hold values from -0.1875 to 0.1875
- query_gain: bfloat16 [128], replicated, may hold values from 0.796875 to 1.796875
- key_gain: bfloat16 [128], replicated, may hold values from 0.796875 to 1.796875
- out_weight: bfloat16 [2048, 1024], P('tensor'), may hold values from -0.75 to 0.75
- mlp_gain: bfloat16 [1024], replicated, may hold values from 0.5 to 1.5
- gate_weight: bfloat16 [1024, 3072], P(None, 'tensor'), may hold values from -0.1875 to 0.1875
- up_weight: bfloat16 [1024, 3072], P(None, 'tensor'), may hold values from -0.1875 to 0.1875
- down_weight: bfloat16 [3072, 1024], P('tensor'), may hold values from -0.109375 to 0.109375
Outputs:
- output: bfloat16 [8, 2048, 1024], P('dp', 'seq')
- input_grad: bfloat16 [8, 2048, 1024], P('dp', 'seq')
- grad_query: float32 [1024, 2048], P(('dp', 'seq'), 'tensor')
- grad_key: float32 [1024, 1024], P(('dp', 'seq'), 'tensor')
- grad_value: float32 [1024, 1024], P(('dp', 'seq'), 'tensor')
- grad_out: float32 [2048, 1024], P('tensor', ('dp', 'seq'))
- grad_gate: float32 [1024, 3072], P(('dp', 'seq'), 'tensor')
- grad_up: float32 [1024, 3072], P(('dp', 'seq'), 'tensor')
- grad_down: float32 [3072, 1024], P('tensor', ('dp', 'seq'))
- grad_attention_gain: float32 [1024], P(('dp', 'seq'))
- grad_mlp_gain: float32 [1024], P(('dp', 'seq'))
- grad_query_gain: float32 [128], P(('dp', 'seq'))
- grad_key_gain: float32 [128], P(('dp', 'seq'))
The draws below stay inside these ranges and needn't reach their ends.
Inputs may be any that keep to these rules, and one draw needn't show every extreme that they name: In each sequence the positions are a permutation of 0 to 2047; the rows of the device at index j of seq are two runs of 128 consecutive positions, the runs numbered c and 2 n - 1 - c of the sequence's 2 n runs, with n the devices of seq and c depending on j. `segments`: document numbers never fall along increasing positions and rise by at most one from one position to the next; every sequence holds four documents.
All inputs are finite; a program needn't handle non-finite values.
Results may differ from the reference program's by a relative error of at most 0.03.
Values may be sent and summed in bfloat16 or wider, within the bound.
A program may use at most 128 MiB of HBM per device.

```python
import math
import jax
import jax.numpy as jnp
from jax import lax

D = 1024
HEAD_DIM = 128
FF = 3072
TOK_DEV = 256
LENGTH = 2048
SEQS = 8
Q_WIDTH = 2048
KV_WIDTH = 1024


def token_layout(key):
    devices = LENGTH // TOK_DEV
    piece_rows = TOK_DEV // 2
    order_key, first_key, start_key = jax.random.split(key, 3)
    order = jax.vmap(lambda subkey: jax.random.permutation(subkey, devices))(jax.random.split(order_key, SEQS))
    row_index = jnp.arange(LENGTH, dtype=jnp.int32)
    device = row_index // TOK_DEV
    upper_half = row_index % TOK_DEV // piece_rows
    within = row_index % piece_rows
    picked = order[:, device]
    piece_index = jnp.where(upper_half[None, :] == 0, picked, 2 * devices - 1 - picked)
    token_place = (piece_index * piece_rows + within[None, :]).astype(jnp.int32)
    first_length = jax.random.randint(first_key, (SEQS, 1), LENGTH // 2 + piece_rows, 3 * LENGTH // 4 + piece_rows + 1)
    remaining = LENGTH - first_length
    second_start = first_length + remaining // 3
    third_start = first_length + 2 * remaining // 3
    place_index = jnp.arange(LENGTH, dtype=jnp.int32)[None, :]
    spacing = max(LENGTH // 8, 2)
    starts = jax.random.randint(start_key, (SEQS, LENGTH), 0, spacing) == 0
    begins = (place_index == first_length) | (place_index == second_start) | (place_index == third_start) | (place_index > first_length) & starts
    by_place = jnp.minimum(jnp.cumsum(begins.astype(jnp.int32), axis=1), 3).astype(jnp.int32)
    segment = jnp.take_along_axis(by_place, token_place, axis=1)
    return (token_place, segment.astype(jnp.int32))


def draw_positions(key, part):
    shared = token_layout(key)
    return shared[0]


def draw_segments(key, part):
    shared = token_layout(key)
    return shared[1]


def with_spikes(values, own_key, source, target, shards_of, factor):
    def block_of(axis_at):
        return (jnp.arange(values.shape[axis_at]) // (values.shape[axis_at] // shards_of)).reshape((-1,) + (1,) * (values.ndim - 1 - axis_at))

    one_side = jax.random.permutation(own_key, shards_of)[block_of(target)]
    far = (block_of(target) + shards_of // 2) % shards_of
    return jnp.where((block_of(source) == one_side) | (block_of(source) == far), factor * values, values)


def levels(rng, extent, cuts, low, high):
    def one(dim, shards_of):
        steps = jax.random.uniform(jax.random.fold_in(jax.random.fold_in(rng, 6), dim), (shards_of,), jnp.float32, low / len(cuts), high / len(cuts))
        return jnp.repeat(jnp.exp(steps), extent[dim] // shards_of).reshape((-1,) + (1,) * (len(extent) - dim - 1))

    gain = one(*cuts[0])
    for cut in cuts[1:]:
        gain = gain * one(*cut)
    return gain


def scatter_about(rng, shape, spread, most, cuts=(), kind=jnp.bfloat16):
    gain = levels(rng, shape, cuts, -0.22, 0.18) if cuts else 1.0
    array = jax.random.normal(rng, shape, jnp.float32) * spread * gain
    return jnp.minimum(jnp.maximum(array, -most), most).astype(kind)


def heavy_noise(stream_key, dims, scale, most, cuts, heavy, kind=jnp.bfloat16):
    values = scale * jax.random.normal(stream_key, dims, jnp.float32)
    if cuts:
        values = values * levels(stream_key, dims, cuts, -0.22, 0.18)
    return jnp.clip(with_spikes(values, jax.random.fold_in(stream_key, 3), *heavy), -most, most).astype(kind)


def setup_inputs(seed: int = 0) -> dict:
    arg_keys = jax.random.split(jax.random.key(seed), 16)
    tokens = scatter_about(arg_keys[0], (SEQS, LENGTH, D), 1.0, 6.0, ((0, 8), (1, 8)))
    cotangent = heavy_noise(arg_keys[1], (SEQS, LENGTH, D), 1.0, 6.0, ((0, 8), (1, 8)), (1, 2, 8, 2.0))
    positions = draw_positions(jax.random.fold_in(arg_keys[15], 71), 0)
    segments = draw_segments(jax.random.fold_in(arg_keys[15], 71), 0)
    attention_gain = jnp.clip(1.0 + 0.1 * jax.random.normal(arg_keys[4], (D,), jnp.float32), 0.5, 1.5).astype(jnp.bfloat16)
    query_weight = scatter_about(arg_keys[5], (D, Q_WIDTH), D ** -0.5, 0.1875, ((1, 2),))
    key_weight = scatter_about(arg_keys[6], (D, KV_WIDTH), D ** -0.5, 0.1875, ((1, 2),))
    value_weight = scatter_about(arg_keys[7], (D, KV_WIDTH), D ** -0.5, 0.1875, ((1, 2),))
    query_gain = jnp.clip(jax.random.uniform(arg_keys[8], (HEAD_DIM,), jnp.float32, 0.796875, 1.796875), 0.796875, 1.796875).astype(jnp.bfloat16)
    key_gain = jnp.clip(jax.random.uniform(arg_keys[9], (HEAD_DIM,), jnp.float32, 0.796875, 1.796875), 0.796875, 1.796875).astype(jnp.bfloat16)
    out_weight = scatter_about(arg_keys[10], (Q_WIDTH, D), (Q_WIDTH // 32) ** -0.5, 0.75, ((0, 2),))
    mlp_gain = jnp.clip(1.0 + 0.1 * jax.random.normal(arg_keys[11], (D,), jnp.float32), 0.5, 1.5).astype(jnp.bfloat16)
    gate_weight = scatter_about(arg_keys[12], (D, FF), D ** -0.5, 0.1875, ((1, 2),))
    up_weight = scatter_about(arg_keys[13], (D, FF), D ** -0.5, 0.1875, ((1, 2),))
    down_weight = scatter_about(arg_keys[14], (FF, D), FF ** -0.5, 0.109375, ((0, 2),))
    return dict(tokens=tokens, cotangent=cotangent, positions=positions, segments=segments, attention_gain=attention_gain, query_weight=query_weight, key_weight=key_weight, value_weight=value_weight, query_gain=query_gain, key_gain=key_gain, out_weight=out_weight, mlp_gain=mlp_gain, gate_weight=gate_weight, up_weight=up_weight, down_weight=down_weight)


EPS = 1e-06
ROPE_BASE = 1000000.0
NEGATIVE = -1e+30
HIGHEST = lax.Precision.HIGHEST

@jax.custom_vjp
def low(v):
    return lax.optimization_barrier(v.astype(jnp.bfloat16)).astype(jnp.float32)

@jax.custom_vjp
def low_back(v):
    return v

def low_keep(v):
    return (low(v), None)

def low_pass(kept, grad):
    return (grad,)

def back_keep(v):
    return (v, None)

def back_low(kept, grad):
    return (low(grad),)
low.defvjp(low_keep, low_pass)
low_back.defvjp(back_keep, back_low)

def matmul(left, right):
    return jnp.dot(left, right, precision=HIGHEST, preferred_element_type=jnp.float32)

def rms_norm(entries, gain_vec):
    return entries * lax.rsqrt(lax.optimization_barrier(jnp.mean(entries * entries, axis=-1, keepdims=True)) + EPS) * gain_vec

def rope_tables(token_place, head_dim):
    half_dim = head_dim // 2
    inverse = 1.0 / ROPE_BASE ** (jnp.arange(half_dim, dtype=jnp.float32) * 2.0 / head_dim)
    angles = token_place.astype(jnp.float32)[:, None] * inverse[None, :]
    return (jnp.cos(angles), jnp.sin(angles))

def rotate(entries, cosine_table, sine_table):
    half_dim = entries.shape[-1] // 2
    front_half = entries[..., :half_dim]
    back_half = entries[..., half_dim:]
    cosine = cosine_table[:, None, :]
    sine = sine_table[:, None, :]
    return jnp.concatenate([front_half * cosine - back_half * sine, back_half * cosine + front_half * sine], axis=-1)

def attention(query_all, key_all, value_all, token_place, segment):
    length = query_all.shape[0]
    key_heads = query_all.shape[1]
    groups = query_all.shape[2]
    head_dim = query_all.shape[3]
    block_rows = min(512, length)
    block_count = length // block_rows
    score_scale = 1.0 / math.sqrt(head_dim)

    def one_block(element):
        query_block, query_place, query_segment = element
        scores = jnp.einsum('bkgd,tkd->kgbt', query_block, key_all, precision=HIGHEST, preferred_element_type=jnp.float32) * score_scale
        scores = low_back(scores)
        allowed = (token_place[None, :] <= query_place[:, None]) & (segment[None, :] == query_segment[:, None])
        scores = jnp.where(allowed[None, None], scores, NEGATIVE)
        attend = low(jax.nn.softmax(scores, axis=-1))
        return jnp.einsum('kgbt,tkd->bkgd', attend, value_all, precision=HIGHEST, preferred_element_type=jnp.float32)
    pieces = (query_all.reshape(block_count, block_rows, key_heads, groups, head_dim), token_place.reshape(block_count, block_rows), segment.reshape(block_count, block_rows))
    result = lax.map(jax.checkpoint(one_block), pieces)
    return result.reshape(length, key_heads * groups * head_dim)

def layer(tokens_in, query_weight, key_weight, value_weight, out_weight, gate_weight, up_weight, down_weight, attention_gain, mlp_gain, query_gain, key_gain, token_place, segment):
    length = tokens_in.shape[0]
    head_dim = query_gain.shape[0]
    cosine_table, sine_table = rope_tables(token_place, head_dim)
    normed = low(rms_norm(tokens_in, attention_gain))
    query_raw = low_back(matmul(normed, query_weight)).reshape(length, -1, head_dim)
    key_raw = low_back(matmul(normed, key_weight)).reshape(length, -1, head_dim)
    value_all = low(low_back(matmul(normed, value_weight))).reshape(length, -1, head_dim)
    query_all = low(rotate(rms_norm(query_raw, query_gain), cosine_table, sine_table))
    key_all = low(rotate(rms_norm(key_raw, key_gain), cosine_table, sine_table))
    key_heads = key_all.shape[1]
    query_all = query_all.reshape(length, key_heads, -1, head_dim)
    attended = low(low_back(attention(query_all, key_all, value_all, token_place, segment)))
    middle = tokens_in + low_back(matmul(attended, out_weight))
    normed_mlp = low(rms_norm(middle, mlp_gain))
    gate_value = low_back(matmul(normed_mlp, gate_weight))
    up_value = low_back(matmul(normed_mlp, up_weight))
    activated = low(jax.nn.silu(gate_value) * up_value)
    return middle + matmul(activated, down_weight)

def reference(tokens, cotangent, positions, segments, attention_gain, query_weight, key_weight, value_weight, query_gain, key_gain, out_weight, mlp_gain, gate_weight, up_weight, down_weight):
    weights = tuple((entry.astype(jnp.float32) for entry in (query_weight, key_weight, value_weight, out_weight, gate_weight, up_weight, down_weight, attention_gain, mlp_gain, query_gain, key_gain)))

    def step(carried, element):
        tokens_seq, cotangent_seq, place_seq, segment_seq = element

        def forward(tokens_in, *weights_in):
            return layer(tokens_in, *weights_in, place_seq, segment_seq)
        result, pullback = jax.vjp(forward, tokens_seq.astype(jnp.float32), *weights)
        gradients = pullback(cotangent_seq.astype(jnp.float32))
        updated = tuple((left + right for left, right in zip(carried, gradients[1:])))
        return (updated, (result.astype(jnp.bfloat16), gradients[0].astype(jnp.bfloat16)))
    initial = tuple((jnp.zeros(entry.shape, jnp.float32) for entry in weights))
    totals, (output, input_grad) = lax.scan(step, initial, (tokens, cotangent, positions, segments))
    return (output, input_grad, totals[0], totals[1], totals[2], totals[3], totals[4], totals[5], totals[6], totals[7], totals[8], totals[9], totals[10])
```

```python
import functools
import math

import jax
import jax.numpy as jnp
from jax import lax
from jax.experimental import pallas as pl
from jax.experimental.pallas import tpu as pltpu
from jax.sharding import PartitionSpec as P

EPS = 1e-06
ROPE_BASE = 1000000.0
NEGATIVE = -1e30


MESH = pl.DeviceIdType.MESH
CHUNK = 16
DIMS = ("x3", "x1", "y3", "y1", "z")
LOW = jnp.bfloat16


def place():
    dp = lax.axis_index("dp")
    seq = lax.axis_index("seq")
    tensor = lax.axis_index("tensor")
    x, z = dp // 2, dp % 2
    y, core = seq // 2, seq % 2
    x_near = x + 1 - 2 * (x % 2)
    y_near = y + 1 - 2 * (y % 2)
    bits = {
        "core": core,
        "x3": x // 2,
        "x1": (x // 2 + x % 2) % 2,
        "y3": y // 2,
        "y1": (y // 2 + y % 2) % 2,
        "z": z,
    }
    partners = {
        "core": (dp, seq + 1 - 2 * core, tensor),
        "x3": ((3 - x) * 2 + z, seq, tensor),
        "x1": (x_near * 2 + z, seq, tensor),
        "y3": (dp, (3 - y) * 2 + core, tensor),
        "y1": (dp, y_near * 2 + core, tensor),
        "z": (dp + 1 - 2 * z, seq, tensor),
        "tensor": (dp, seq, 1 - tensor),
    }
    return bits, partners


def greet(partners):
    barrier = pltpu.get_barrier_semaphore()
    for partner in partners:
        pl.semaphore_signal(barrier, inc=1, device_id=partner, device_id_type=MESH)
    pl.semaphore_wait(barrier, len(partners))


def stream_order(stream):
    return ("core",) + tuple(DIMS[(stream + i) % len(DIMS)] for i in range(len(DIMS)))


def slot_chunks(order):
    chunks = []
    for slot in range(2 ** len(order)):
        bit = {d: (slot >> (len(order) - 1 - i)) & 1 for i, d in enumerate(order)}
        x = 2 * bit["x3"] + (bit["x3"] ^ bit["x1"])
        y = 2 * bit["y3"] + (bit["y3"] ^ bit["y1"])
        chunks.append(((x * 2 + bit["z"]) * 4 + y) * 2 + bit["core"])
    return chunks


def scatter_kernel(pieces, n_lhs, n_rhs, *refs):
    streams = len(pieces)
    lhs = refs[:n_lhs]
    rhs = refs[n_lhs : n_lhs + n_rhs]
    gains_in, partial_in = refs[n_lhs + n_rhs : n_lhs + n_rhs + 2]
    refs = refs[n_lhs + n_rhs + 2 :]
    outs = refs[:streams]
    gains_out, partial_out = refs[streams : streams + 2]
    refs = refs[streams + 2 :]
    turned, sent, held = refs[:3]
    landed = refs[3:9]
    gains_held = refs[9]
    gains_landed = refs[10:16]
    gains_last, gains_sum, send_sem, recv_sem, gains_send, gains_recv, pair_send, pair_recv = refs[16:]
    bits, partners = place()
    greet(list(partners.values()))

    def exchange(source, target, out_sem, in_sem, partner):
        return pltpu.make_async_remote_copy(
            src_ref=source,
            dst_ref=target,
            send_sem=out_sem,
            recv_sem=in_sem,
            device_id=partner,
            device_id_type=MESH,
        )

    partial_copy = exchange(
        partial_in, partial_out, pair_send.at[0], pair_recv.at[0], partners["tensor"]
    )
    partial_copy.start()
    orders = [stream_order(s) for s in range(streams)]
    features = lhs[0].shape[1]
    half = features // 2
    core = bits["core"]
    block = 128
    copies = {}
    used = []
    for s in range(streams):
        for left, right, first, columns in pieces[s]:
            flipped = lhs[left][...].T
            index = len(used)
            used.append((s, left, right, first, columns))
            for slot, chunk in enumerate(slot_chunks(orders[s])):
                turned[index, slot * CHUNK : (slot + 1) * CHUNK, :] = flipped[
                    chunk * CHUNK : (chunk + 1) * CHUNK, :
                ]

    def product(s, target, offset):
        for index, (stream, _, right, first, columns) in enumerate(used):
            if stream != s:
                continue

            def rows(i, _, index=index, right=right, first=first, columns=columns):
                start = pl.multiple_of(i * block, block)
                from_row = pl.multiple_of(offset + start, block)
                target[s, pl.ds(start, block), first : first + columns] = jnp.dot(
                    turned[index, pl.ds(from_row, block), :],
                    rhs[right][...],
                    preferred_element_type=jnp.float32,
                ).astype(LOW)
                return 0

            lax.fori_loop(0, half // block, rows, 0)

    for s in range(streams):
        product(s, sent, (1 - core) * half)
        copies[s, 0] = exchange(
            sent.at[s], landed[0].at[s], send_sem.at[s, 0], recv_sem.at[s, 0], partners["core"]
        )
        copies[s, 0].start()
    gain_chunks = gains_in.shape[0]
    gains_copy = [None] * 6
    gains_copy[0] = exchange(
        gains_in.at[pl.ds((1 - core) * (gain_chunks // 2), gain_chunks // 2)],
        gains_landed[0],
        gains_send.at[0],
        gains_recv.at[0],
        partners["core"],
    )
    gains_copy[0].start()
    for s in range(streams):
        product(s, held, core * half)
    gains_held[...] = gains_in[pl.ds(core * (gain_chunks // 2), gain_chunks // 2)]

    base = [0] * streams
    gains_base = 0
    for step in range(6):
        rows = half >> step
        for s in range(streams):
            copies[s, step].wait()
            if step == 5:
                mine = pl.multiple_of(base[s], CHUNK)
                outs[s][...] = held[s, pl.ds(mine, CHUNK), :].astype(jnp.float32) + landed[5][
                    s
                ].astype(jnp.float32)
                continue
            tile = min(rows, 64)

            def add(i, _, s=s, step=step, tile=tile):
                start = pl.multiple_of(i * tile, tile)
                here = pl.multiple_of(base[s] + start, tile)
                held[s, pl.ds(here, tile), :] = (
                    held[s, pl.ds(here, tile), :] + landed[step][s, pl.ds(start, tile), :]
                )
                return 0

            lax.fori_loop(0, rows // tile, add, 0)
            dim = orders[s][step + 1]
            bit = bits[dim]
            away = pl.multiple_of(base[s] + (1 - bit) * (rows // 2), CHUNK)
            copies[s, step + 1] = exchange(
                held.at[s, pl.ds(away, rows // 2), :],
                landed[step + 1].at[s],
                send_sem.at[s, step + 1],
                recv_sem.at[s, step + 1],
                partners[dim],
            )
            copies[s, step + 1].start()
            base[s] = base[s] + bit * (rows // 2)
        chunks = gain_chunks >> (step + 1)
        gains_copy[step].wait()
        gains_held[pl.ds(gains_base, chunks)] = (
            gains_held[pl.ds(gains_base, chunks)] + gains_landed[step][...]
        )
        if step < 5:
            dim = orders[0][step + 1]
            bit = bits[dim]
            gains_copy[step + 1] = exchange(
                gains_held.at[pl.ds(gains_base + (1 - bit) * (chunks // 2), chunks // 2)],
                gains_landed[step + 1],
                gains_send.at[step + 1],
                gains_recv.at[step + 1],
                partners[dim],
            )
            gains_copy[step + 1].start()
            gains_base = gains_base + bit * (chunks // 2)
    gains_last[...] = gains_held[pl.ds(gains_base, 1)]
    last = exchange(gains_last, gains_sum, pair_send.at[1], pair_recv.at[1], partners["tensor"])
    last.start()
    last.wait()
    gains_out[...] = gains_last[0] + gains_sum[0]
    partial_copy.wait()


def scatter_gradients(pieces, lhs, rhs, gains, partial):
    streams = len(pieces)
    width = sum(columns for _, _, _, columns in pieces[0])
    tokens, features = lhs[0].shape
    half = features // 2
    parts = sum(len(p) for p in pieces)
    chunks = features // CHUNK
    vmem = pl.BlockSpec(memory_space=pltpu.VMEM)
    landed = [pltpu.VMEM((streams, half >> step, width), LOW) for step in range(6)]
    gains_landed = [pltpu.VMEM((chunks >> (step + 1), 8, 128), jnp.float32) for step in range(6)]
    result = pl.pallas_call(
        functools.partial(scatter_kernel, pieces, len(lhs), len(rhs)),
        out_shape=[jax.ShapeDtypeStruct((CHUNK, width), jnp.float32)] * streams
        + [
            jax.ShapeDtypeStruct((8, 128), jnp.float32),
            jax.ShapeDtypeStruct(partial.shape, partial.dtype),
        ],
        in_specs=[vmem] * (len(lhs) + len(rhs) + 2),
        out_specs=[vmem] * (streams + 2),
        scratch_shapes=[
            pltpu.VMEM((parts, features, tokens), LOW),
            pltpu.VMEM((streams, half, width), LOW),
            pltpu.VMEM((streams, half, width), LOW),
            *landed,
            pltpu.VMEM((chunks // 2, 8, 128), jnp.float32),
            *gains_landed,
            pltpu.VMEM((1, 8, 128), jnp.float32),
            pltpu.VMEM((1, 8, 128), jnp.float32),
            pltpu.SemaphoreType.DMA((streams, 6)),
            pltpu.SemaphoreType.DMA((streams, 6)),
            pltpu.SemaphoreType.DMA((6,)),
            pltpu.SemaphoreType.DMA((6,)),
            pltpu.SemaphoreType.DMA((2,)),
            pltpu.SemaphoreType.DMA((2,)),
        ],
        compiler_params=pltpu.CompilerParams(
            collective_id=0, has_side_effects=True, vmem_limit_bytes=60 * 1024 * 1024
        ),
    )(*lhs, *rhs, gains, partial)
    return result[:streams], result[streams], result[streams + 1]


def pack_gains(attention, mlp, query, key):
    chunks = attention.shape[0] // CHUNK
    packed = jnp.concatenate(
        [entry.reshape(chunks, -1) for entry in (attention, mlp, query, key)], axis=1
    )
    ordered = packed[jnp.array(slot_chunks(stream_order(0)))]
    return jnp.pad(ordered[:, None, :], ((0, 0), (0, 7), (0, 128 - ordered.shape[1])))


def mean_rms(entries):
    return lax.rsqrt(jnp.mean(entries * entries, axis=-1, keepdims=True) + EPS)


def norm_back(entries, gain_vec, gradient):
    inverse = mean_rms(entries)
    scaled = gradient * gain_vec
    gain_grad = jnp.sum((gradient * entries * inverse).reshape(-1, entries.shape[-1]), axis=0)
    entries_grad = inverse * scaled - entries * inverse**3 * jnp.mean(
        scaled * entries, axis=-1, keepdims=True
    )
    return (entries_grad, gain_grad)


def rope_tables(token_place, head_dim):
    half_dim = head_dim // 2
    inverse = 1.0 / ROPE_BASE ** (jnp.arange(half_dim, dtype=jnp.float32) * 2.0 / head_dim)
    angles = token_place.astype(jnp.float32)[:, None] * inverse[None, :]
    return (jnp.cos(angles), jnp.sin(angles))


def rotate(entries, cosine_table, sine_table):
    half_dim = entries.shape[-1] // 2
    front_half = entries[..., :half_dim]
    back_half = entries[..., half_dim:]
    cosine = cosine_table[:, None, :]
    sine = sine_table[:, None, :]
    return jnp.concatenate(
        [front_half * cosine - back_half * sine, back_half * cosine + front_half * sine], axis=-1
    )


def unrotate(gradient, cosine_table, sine_table):
    half_dim = gradient.shape[-1] // 2
    front_half = gradient[..., :half_dim]
    back_half = gradient[..., half_dim:]
    cosine = cosine_table[:, None, :]
    sine = sine_table[:, None, :]
    return jnp.concatenate(
        [front_half * cosine + back_half * sine, back_half * cosine - front_half * sine], axis=-1
    )


def dense(left, right):
    return jnp.dot(left, right, preferred_element_type=jnp.float32)


def shards(
    tokens,
    cotangent,
    positions,
    segments,
    attention_gain,
    query_weight,
    key_weight,
    value_weight,
    query_gain,
    key_gain,
    out_weight,
    mlp_gain,
    gate_weight,
    up_weight,
    down_weight,
):
    head_dim = query_gain.shape[0]
    local_rows = tokens.shape[1]
    key_heads = key_weight.shape[1] // head_dim
    query_heads = query_weight.shape[1] // head_dim
    groups = query_heads // key_heads
    block_rows = min(512, local_rows)
    block_count = local_rows // block_rows
    score_scale = 1.0 / math.sqrt(head_dim)
    attention_gain = attention_gain.astype(jnp.float32)
    mlp_gain = mlp_gain.astype(jnp.float32)
    query_gain = query_gain.astype(jnp.float32)
    key_gain = key_gain.astype(jnp.float32)
    inputs = tokens[0].astype(jnp.float32)
    token_place = positions[0]
    segment = segments[0]
    cosine_table, sine_table = rope_tables(token_place, head_dim)
    normed = (inputs * mean_rms(inputs) * attention_gain).astype(jnp.bfloat16)
    query_raw = dense(normed, query_weight).reshape(local_rows, query_heads, head_dim)
    key_raw = dense(normed, key_weight).reshape(local_rows, key_heads, head_dim)
    value_low = (
        dense(normed, value_weight).astype(jnp.bfloat16).reshape(local_rows, key_heads, head_dim)
    )
    query_low = rotate(
        query_raw * mean_rms(query_raw) * query_gain, cosine_table, sine_table
    ).astype(jnp.bfloat16)
    key_low = rotate(key_raw * mean_rms(key_raw) * key_gain, cosine_table, sine_table).astype(
        jnp.bfloat16
    )
    key_local = key_low.transpose(1, 0, 2)
    value_local = value_low.transpose(1, 0, 2)
    key_all, value_all, place_all, segment_all = (
        lax.all_gather(key_local, "seq", axis=1, tiled=True),
        lax.all_gather(value_local, "seq", axis=1, tiled=True),
        lax.all_gather(token_place, "seq", axis=0, tiled=True),
        lax.all_gather(segment, "seq", axis=0, tiled=True),
    )
    query_blocks = query_low.reshape(
        block_count, block_rows, key_heads, groups, head_dim
    ).transpose(2, 0, 3, 1, 4)
    place_blocks = token_place.reshape(block_count, block_rows)
    segment_blocks = segment.reshape(block_count, block_rows)

    def block_mask(query_place, query_segment, key_place, key_segment):
        return (key_place[None, :] <= query_place[:, None]) & (
            key_segment[None, :] == query_segment[:, None]
        )

    def forward_head(element):
        query_head, key_head, value_head = element

        def forward_block(pieces):
            query_block, query_place, query_segment = pieces
            scores = (
                jnp.einsum("gbd,td->gbt", query_block, key_head, preferred_element_type=jnp.float32)
                * score_scale
            )
            allowed = block_mask(query_place, query_segment, place_all, segment_all)[None]
            scores = jnp.where(allowed, scores, NEGATIVE)
            largest = jnp.max(scores, axis=-1, keepdims=True)
            exponent = jnp.exp(scores - largest)
            row_total = jnp.sum(exponent, axis=-1, keepdims=True)
            attend = (exponent / row_total).astype(jnp.bfloat16)
            attended = jnp.einsum(
                "gbt,td->gbd", attend, value_head, preferred_element_type=jnp.float32
            )
            return (attended, largest[..., 0] + jnp.log(row_total[..., 0]))

        return lax.map(forward_block, (query_head, place_blocks, segment_blocks))

    attended, log_total = lax.map(forward_head, (query_blocks, key_all, value_all))
    attended_low = (
        attended.transpose(1, 3, 0, 2, 4)
        .reshape(local_rows, query_heads * head_dim)
        .astype(jnp.bfloat16)
    )
    attention_out = lax.psum(dense(attended_low, out_weight), "tensor")
    middle = inputs + attention_out
    normed_mlp = (middle * mean_rms(middle) * mlp_gain).astype(jnp.bfloat16)
    gate_value = dense(normed_mlp, gate_weight)
    up_value = dense(normed_mlp, up_weight)
    sigmoid_gate = jax.nn.sigmoid(gate_value)
    activated = (gate_value * sigmoid_gate * up_value).astype(jnp.bfloat16)
    mlp_out = lax.psum(dense(activated, down_weight).astype(jnp.bfloat16), "tensor").astype(
        jnp.float32
    )
    output = (middle + mlp_out).astype(jnp.bfloat16)[None]
    upstream = cotangent[0]
    grad_act = dense(upstream, down_weight.T)
    gate_grad_low = (
        grad_act * up_value * sigmoid_gate * (1.0 + gate_value * (1.0 - sigmoid_gate))
    ).astype(jnp.bfloat16)
    up_grad_low = (grad_act * gate_value * sigmoid_gate).astype(jnp.bfloat16)
    mlp_partial = dense(gate_grad_low, gate_weight.T) + dense(up_grad_low, up_weight.T)
    mlp_normed_grad = lax.psum(mlp_partial.astype(jnp.bfloat16), "tensor").astype(jnp.float32)
    middle_part, mlp_gain_grad = norm_back(middle, mlp_gain, mlp_normed_grad)
    grad_middle = upstream.astype(jnp.float32) + middle_part
    middle_low = grad_middle.astype(jnp.bfloat16)
    attended_grad_low = dense(middle_low, out_weight.T).astype(jnp.bfloat16)
    grad_blocks = attended_grad_low.reshape(
        block_count, block_rows, key_heads, groups, head_dim
    ).transpose(2, 0, 3, 1, 4)
    key_use, value_use, place_use, segment_use = (key_all, value_all, place_all, segment_all)

    def backward_head(element):
        query_head, grad_head, total_head, key_head, value_head = element

        def backward_block(carried, pieces):
            key_sum, value_sum = carried
            query_block, grad_block, total_block, query_place, query_segment = pieces
            scores = (
                jnp.einsum("gbd,td->gbt", query_block, key_head, preferred_element_type=jnp.float32)
                * score_scale
            )
            allowed = block_mask(query_place, query_segment, place_use, segment_use)[None]
            attend = jnp.where(allowed, jnp.exp(scores - total_block[..., None]), 0.0)
            attend_low = attend.astype(jnp.bfloat16)
            grad_attend = jnp.einsum(
                "gbd,td->gbt", grad_block, value_head, preferred_element_type=jnp.float32
            )
            inner_sum = jnp.sum(attend * grad_attend, axis=-1, keepdims=True)
            scores_grad = (attend * (grad_attend - inner_sum)).astype(jnp.bfloat16)
            query_grad = (
                jnp.einsum("gbt,td->gbd", scores_grad, key_head, preferred_element_type=jnp.float32)
                * score_scale
            )
            key_sum = (
                key_sum
                + jnp.einsum(
                    "gbt,gbd->td", scores_grad, query_block, preferred_element_type=jnp.float32
                )
                * score_scale
            )
            value_sum = value_sum + jnp.einsum(
                "gbt,gbd->td", attend_low, grad_block, preferred_element_type=jnp.float32
            )
            return ((key_sum, value_sum), query_grad)

        initial = jnp.zeros(key_head.shape, jnp.float32)
        sums, query_grad = lax.scan(
            backward_block,
            (initial, initial),
            (query_head, grad_head, total_head, place_blocks, segment_blocks),
        )
        return (query_grad, sums[0], sums[1])

    query_grad_blocks, key_grad_all, value_grad_all = lax.map(
        backward_head, (query_blocks, grad_blocks, log_total, key_use, value_use)
    )
    key_grad, value_grad = (
        lax.psum_scatter(
            key_grad_all.astype(jnp.bfloat16), "seq", scatter_dimension=1, tiled=True
        ).astype(jnp.float32),
        lax.psum_scatter(
            value_grad_all.astype(jnp.bfloat16), "seq", scatter_dimension=1, tiled=True
        ).astype(jnp.float32),
    )
    query_rot_grad = query_grad_blocks.transpose(1, 3, 0, 2, 4).reshape(
        local_rows, query_heads, head_dim
    )
    query_raw_grad, query_gain_part = norm_back(
        query_raw, query_gain, unrotate(query_rot_grad, cosine_table, sine_table)
    )
    key_raw_grad, key_gain_part = norm_back(
        key_raw, key_gain, unrotate(key_grad.transpose(1, 0, 2), cosine_table, sine_table)
    )
    query_grad_low = query_raw_grad.reshape(local_rows, query_heads * head_dim).astype(jnp.bfloat16)
    key_grad_low = key_raw_grad.reshape(local_rows, key_heads * head_dim).astype(jnp.bfloat16)
    value_grad_low = (
        value_grad.transpose(1, 0, 2).reshape(local_rows, key_heads * head_dim).astype(jnp.bfloat16)
    )
    attention_partial = (
        dense(query_grad_low, query_weight.T)
        + dense(key_grad_low, key_weight.T)
        + dense(value_grad_low, value_weight.T)
    )
    attention_gain_part = jnp.sum(attention_partial * inputs * mean_rms(inputs), axis=0)
    width = gate_weight.shape[1]
    q_width, k_width = query_weight.shape[1], key_weight.shape[1]
    pieces = (
        ((0, 0, 0, width),),
        ((0, 1, 0, width),),
        ((1, 2, 0, width),),
        ((2, 3, 0, q_width), (2, 4, q_width, k_width)),
        ((2, 5, 0, k_width), (3, 6, k_width, q_width)),
    )
    shares, gains, partial_other = scatter_gradients(
        pieces,
        (normed_mlp, upstream, normed, middle_low),
        (
            gate_grad_low,
            up_grad_low,
            activated,
            query_grad_low,
            key_grad_low,
            value_grad_low,
            attended_low,
        ),
        pack_gains(attention_gain_part, 0.5 * mlp_gain_grad, query_gain_part, key_gain_part),
        attention_partial.astype(jnp.bfloat16),
    )
    normed_grad = attention_partial + partial_other.astype(jnp.float32)
    input_part, _ = norm_back(inputs, attention_gain, normed_grad)
    input_grad = (grad_middle + input_part).astype(jnp.bfloat16)[None]
    return (
        output,
        input_grad,
        shares[3][:, :q_width],
        shares[3][:, q_width:],
        shares[4][:, :k_width],
        shares[4][:, k_width:].T,
        shares[0],
        shares[1],
        shares[2].T,
        gains[0, 0:16],
        gains[0, 16:32],
        gains[0, 32:34],
        gains[0, 34:36],
    )


def solution(mesh):
    return jax.shard_map(
        shards,
        mesh=mesh,
        in_specs=(
            P("dp", "seq", None),
            P("dp", "seq", None),
            P("dp", "seq"),
            P("dp", "seq"),
            P(),
            P(None, "tensor"),
            P(None, "tensor"),
            P(None, "tensor"),
            P(),
            P(),
            P("tensor", None),
            P(),
            P(None, "tensor"),
            P(None, "tensor"),
            P("tensor", None),
        ),
        out_specs=(
            P("dp", "seq", None),
            P("dp", "seq", None),
            P(("dp", "seq"), "tensor"),
            P(("dp", "seq"), "tensor"),
            P(("dp", "seq"), "tensor"),
            P("tensor", ("dp", "seq")),
            P(("dp", "seq"), "tensor"),
            P(("dp", "seq"), "tensor"),
            P("tensor", ("dp", "seq")),
            P(("dp", "seq")),
            P(("dp", "seq")),
            P(("dp", "seq")),
            P(("dp", "seq")),
        ),
        check_vma=False,
    )
```

```python
import functools
import math

import jax
import jax.numpy as jnp
from jax import lax
from jax.experimental import pallas as pl
from jax.experimental.pallas import tpu as pltpu
from jax.sharding import PartitionSpec as P

EPS = 1e-06
ROPE_BASE = 1000000.0
NEGATIVE = -1e30


MESH = pl.DeviceIdType.MESH
CHUNK = 16
DIMS = ("x3", "x1", "y3", "y1", "z")
LOW = jnp.bfloat16


def place():
    dp = lax.axis_index("dp")
    seq = lax.axis_index("seq")
    tensor = lax.axis_index("tensor")
    x, z = dp // 2, dp % 2
    y, core = seq // 2, seq % 2
    x_near = x + 1 - 2 * (x % 2)
    y_near = y + 1 - 2 * (y % 2)
    bits = {
        "core": core,
        "x3": x // 2,
        "x1": (x // 2 + x % 2) % 2,
        "y3": y // 2,
        "y1": (y // 2 + y % 2) % 2,
        "z": z,
    }
    partners = {
        "core": (dp, seq + 1 - 2 * core, tensor),
        "x3": ((3 - x) * 2 + z, seq, tensor),
        "x1": (x_near * 2 + z, seq, tensor),
        "y3": (dp, (3 - y) * 2 + core, tensor),
        "y1": (dp, y_near * 2 + core, tensor),
        "z": (dp + 1 - 2 * z, seq, tensor),
        "tensor": (dp, seq, 1 - tensor),
    }
    return bits, partners


def greet(partners):
    barrier = pltpu.get_barrier_semaphore()
    for partner in partners:
        pl.semaphore_signal(barrier, inc=1, device_id=partner, device_id_type=MESH)
    pl.semaphore_wait(barrier, len(partners))


def stream_order(stream):
    return ("core",) + tuple(DIMS[(stream + i) % len(DIMS)] for i in range(len(DIMS)))


def slot_chunks(order):
    chunks = []
    for slot in range(2 ** len(order)):
        bit = {d: (slot >> (len(order) - 1 - i)) & 1 for i, d in enumerate(order)}
        x = 2 * bit["x3"] + (bit["x3"] ^ bit["x1"])
        y = 2 * bit["y3"] + (bit["y3"] ^ bit["y1"])
        chunks.append(((x * 2 + bit["z"]) * 4 + y) * 2 + bit["core"])
    return chunks


def scatter_kernel(pieces, n_lhs, n_rhs, *refs):
    streams = len(pieces)
    lhs = refs[:n_lhs]
    rhs = refs[n_lhs : n_lhs + n_rhs]
    gains_in, partial_in = refs[n_lhs + n_rhs : n_lhs + n_rhs + 2]
    refs = refs[n_lhs + n_rhs + 2 :]
    outs = refs[:streams]
    gains_out, partial_out = refs[streams : streams + 2]
    refs = refs[streams + 2 :]
    turned, sent, held = refs[:3]
    landed = refs[3:9]
    gains_held = refs[9]
    gains_landed = refs[10:16]
    gains_last, gains_sum, send_sem, recv_sem, gains_send, gains_recv, pair_send, pair_recv = refs[16:]
    bits, partners = place()
    greet(list(partners.values()))

    def exchange(source, target, out_sem, in_sem, partner):
        return pltpu.make_async_remote_copy(
            src_ref=source,
            dst_ref=target,
            send_sem=out_sem,
            recv_sem=in_sem,
            device_id=partner,
            device_id_type=MESH,
        )

    partial_copy = exchange(
        partial_in, partial_out, pair_send.at[0], pair_recv.at[0], partners["tensor"]
    )
    partial_copy.start()
    orders = [stream_order(s) for s in range(streams)]
    features = lhs[0].shape[1]
    half = features // 2
    core = bits["core"]
    block = 128
    copies = {}
    used = []
    for s in range(streams):
        for left, right, first, columns in pieces[s]:
            flipped = lhs[left][...].T
            index = len(used)
            used.append((s, left, right, first, columns))
            for slot, chunk in enumerate(slot_chunks(orders[s])):
                turned[index, slot * CHUNK : (slot + 1) * CHUNK, :] = flipped[
                    chunk * CHUNK : (chunk + 1) * CHUNK, :
                ]

    def product(s, target, offset):
        for index, (stream, _, right, first, columns) in enumerate(used):
            if stream != s:
                continue

            def rows(i, _, index=index, right=right, first=first, columns=columns):
                start = pl.multiple_of(i * block, block)
                from_row = pl.multiple_of(offset + start, block)
                target[s, pl.ds(start, block), first : first + columns] = jnp.dot(
                    turned[index, pl.ds(from_row, block), :],
                    rhs[right][...],
                    preferred_element_type=jnp.float32,
                ).astype(LOW)
                return 0

            lax.fori_loop(0, half // block, rows, 0)

    for s in range(streams):
        product(s, sent, (1 - core) * half)
        copies[s, 0] = exchange(
            sent.at[s], landed[0].at[s], send_sem.at[s, 0], recv_sem.at[s, 0], partners["core"]
        )
        copies[s, 0].start()
    gain_chunks = gains_in.shape[0]
    gains_copy = [None] * 6
    gains_copy[0] = exchange(
        gains_in.at[pl.ds((1 - core) * (gain_chunks // 2), gain_chunks // 2)],
        gains_landed[0],
        gains_send.at[0],
        gains_recv.at[0],
        partners["core"],
    )
    gains_copy[0].start()
    for s in range(streams):
        product(s, held, core * half)
    gains_held[...] = gains_in[pl.ds(core * (gain_chunks // 2), gain_chunks // 2)]

    base = [0] * streams
    gains_base = 0
    for step in range(6):
        rows = half >> step
        for s in range(streams):
            copies[s, step].wait()
            if step == 5:
                mine = pl.multiple_of(base[s], CHUNK)
                outs[s][...] = held[s, pl.ds(mine, CHUNK), :].astype(jnp.float32) + landed[5][
                    s
                ].astype(jnp.float32)
                continue
            tile = min(rows, 64)

            def add(i, _, s=s, step=step, tile=tile):
                start = pl.multiple_of(i * tile, tile)
                here = pl.multiple_of(base[s] + start, tile)
                held[s, pl.ds(here, tile), :] = (
                    held[s, pl.ds(here, tile), :] + landed[step][s, pl.ds(start, tile), :]
                )
                return 0

            lax.fori_loop(0, rows // tile, add, 0)
            dim = orders[s][step + 1]
            bit = bits[dim]
            away = pl.multiple_of(base[s] + (1 - bit) * (rows // 2), CHUNK)
            copies[s, step + 1] = exchange(
                held.at[s, pl.ds(away, rows // 2), :],
                landed[step + 1].at[s],
                send_sem.at[s, step + 1],
                recv_sem.at[s, step + 1],
                partners[dim],
            )
            copies[s, step + 1].start()
            base[s] = base[s] + bit * (rows // 2)
        chunks = gain_chunks >> (step + 1)
        gains_copy[step].wait()
        gains_held[pl.ds(gains_base, chunks)] = (
            gains_held[pl.ds(gains_base, chunks)] + gains_landed[step][...]
        )
        if step < 5:
            dim = orders[0][step + 1]
            bit = bits[dim]
            gains_copy[step + 1] = exchange(
                gains_held.at[pl.ds(gains_base + (1 - bit) * (chunks // 2), chunks // 2)],
                gains_landed[step + 1],
                gains_send.at[step + 1],
                gains_recv.at[step + 1],
                partners[dim],
            )
            gains_copy[step + 1].start()
            gains_base = gains_base + bit * (chunks // 2)
    gains_last[...] = gains_held[pl.ds(gains_base, 1)]
    last = exchange(gains_last, gains_sum, pair_send.at[1], pair_recv.at[1], partners["tensor"])
    last.start()
    last.wait()
    gains_out[...] = gains_last[0] + gains_sum[0]
    partial_copy.wait()


def scatter_gradients(pieces, lhs, rhs, gains, partial):
    streams = len(pieces)
    width = sum(columns for _, _, _, columns in pieces[0])
    tokens, features = lhs[0].shape
    half = features // 2
    parts = sum(len(p) for p in pieces)
    chunks = features // CHUNK
    vmem = pl.BlockSpec(memory_space=pltpu.VMEM)
    landed = [pltpu.VMEM((streams, half >> step, width), LOW) for step in range(6)]
    gains_landed = [pltpu.VMEM((chunks >> (step + 1), 8, 128), jnp.float32) for step in range(6)]
    result = pl.pallas_call(
        functools.partial(scatter_kernel, pieces, len(lhs), len(rhs)),
        out_shape=[jax.ShapeDtypeStruct((CHUNK, width), jnp.float32)] * streams
        + [
            jax.ShapeDtypeStruct((8, 128), jnp.float32),
            jax.ShapeDtypeStruct(partial.shape, partial.dtype),
        ],
        in_specs=[vmem] * (len(lhs) + len(rhs) + 2),
        out_specs=[vmem] * (streams + 2),
        scratch_shapes=[
            pltpu.VMEM((parts, features, tokens), LOW),
            pltpu.VMEM((streams, half, width), LOW),
            pltpu.VMEM((streams, half, width), LOW),
            *landed,
            pltpu.VMEM((chunks // 2, 8, 128), jnp.float32),
            *gains_landed,
            pltpu.VMEM((1, 8, 128), jnp.float32),
            pltpu.VMEM((1, 8, 128), jnp.float32),
            pltpu.SemaphoreType.DMA((streams, 6)),
            pltpu.SemaphoreType.DMA((streams, 6)),
            pltpu.SemaphoreType.DMA((6,)),
            pltpu.SemaphoreType.DMA((6,)),
            pltpu.SemaphoreType.DMA((2,)),
            pltpu.SemaphoreType.DMA((2,)),
        ],
        compiler_params=pltpu.CompilerParams(
            collective_id=0, has_side_effects=True, vmem_limit_bytes=60 * 1024 * 1024
        ),
    )(*lhs, *rhs, gains, partial)
    return result[:streams], result[streams], result[streams + 1]


def pack_gains(attention, mlp, query, key):
    chunks = attention.shape[0] // CHUNK
    packed = jnp.concatenate(
        [entry.reshape(chunks, -1) for entry in (attention, mlp, query, key)], axis=1
    )
    ordered = packed[jnp.array(slot_chunks(stream_order(0)))]
    return jnp.pad(ordered[:, None, :], ((0, 0), (0, 7), (0, 128 - ordered.shape[1])))


def remote(source, target, out_sem, in_sem, partner):
    return pltpu.make_async_remote_copy(
        src_ref=source,
        dst_ref=target,
        send_sem=out_sem,
        recv_sem=in_sem,
        device_id=partner,
        device_id_type=MESH,
    )


def over_tiles(count, body):
    def step(i, _):
        body(i)
        return 0

    lax.fori_loop(0, count, step, 0)


def at_tile(i, size):
    return pl.ds(pl.multiple_of(i * size, size), size)


def times(left, right):
    return jnp.dot(left, right, preferred_element_type=jnp.float32)


def times_turned(left, right):
    return lax.dot_general(
        left, right, (((1,), (1,)), ((), ())), preferred_element_type=jnp.float32
    )


def inverse_rms(entries):
    return lax.rsqrt(jnp.mean(entries * entries, axis=-1, keepdims=True) + EPS)


def forward_kernel(
    tokens,
    cotangent,
    positions,
    segments,
    frequencies,
    attention_gain,
    query_gain,
    key_gain,
    mlp_gain,
    wq_far,
    wk_far,
    wv_far,
    wo_far,
    wg_far,
    wu_far,
    wd_far,
    normed,
    query_raw,
    key_raw,
    query,
    kv,
    meta,
    cosine,
    sine,
    attended,
    middle,
    normed_mlp,
    activated,
    gate_grad,
    up_grad,
    mlp_out,
    grad_middle,
    middle_low,
    attended_grad,
    inner,
    mlp_gain_grad,
    wq,
    wk,
    wv,
    wo,
    wg,
    wu,
    wd,
    bias,
    total,
    weight_sum,
    act_grad,
    part_out,
    part_in,
    weight_sem,
    kv_send,
    kv_recv,
    meta_send,
    meta_recv,
    pair_send,
    pair_recv,
):
    dp, seq, tensor = lax.axis_index("dp"), lax.axis_index("seq"), lax.axis_index("tensor")
    core, y = seq % 2, seq // 2
    after, before, across = (y + 1) % 4, (y + 3) % 4, (y + 2) % 4
    near = (dp, y * 2 + 1 - core, tensor)
    ahead = (dp, after * 2 + core, tensor)
    behind = (dp, before * 2 + core, tensor)
    pair = (dp, seq, 1 - tensor)
    others = [(dp, (seq + step) % 8, tensor) for step in range(1, 8)]
    rows = tokens.shape[0]
    heads = kv.shape[2]
    hd = kv.shape[4]
    greet(others + [pair])
    fetches = [
        pltpu.make_async_copy(far, held, weight_sem.at[i])
        for i, (far, held) in enumerate(
            zip(
                (wk_far, wv_far, wq_far, wo_far, wd_far, wg_far, wu_far),
                (wk, wv, wq, wo, wd, wg, wu),
            )
        )
    ]
    for fetch in fetches:
        fetch.start()
    got_wk, got_wv, got_wq, got_wo, got_wd, got_wg, got_wu = fetches

    meta[seq] = jnp.zeros_like(meta[seq])
    meta[seq, 0:1, :] = positions[...]
    meta[seq, 1:2, :] = segments[...]
    metas = [
        remote(meta.at[seq], meta.at[seq], meta_send.at[i], meta_recv.at[i], other)
        for i, other in enumerate(others)
    ]
    for copy in metas:
        copy.start()

    place_rows = jnp.broadcast_to(positions[...].astype(jnp.float32), (rows, rows)).T
    segment_rows = jnp.broadcast_to(segments[...].astype(jnp.float32), (rows, rows)).T
    angle = place_rows[:, :hd] * frequencies[...]
    cosine[...] = jnp.cos(angle)
    lane = lax.broadcasted_iota(jnp.int32, (rows, hd), 1)
    sine[...] = jnp.where(lane < hd // 2, -1.0, 1.0) * jnp.sin(angle)

    def turn(entries):
        return entries * cosine[...] + pltpu.roll(entries, hd // 2, 1) * sine[...]

    x = tokens[...].astype(jnp.float32)
    normed[...] = (x * inverse_rms(x) * attention_gain[...].astype(jnp.float32)).astype(LOW)

    tile = 2 * hd
    got_wk.wait()

    def key_tile(i):
        raw = times(normed[...], wk[:, at_tile(i, tile)])
        key_raw[:, at_tile(i, tile)] = raw
        for g in range(2):
            head = raw[:, g * hd : (g + 1) * hd]
            scaled = head * inverse_rms(head) * key_gain[...].astype(jnp.float32)
            kv[seq, 0, 2 * i + g] = turn(scaled).astype(LOW)

    over_tiles(heads // 2, key_tile)

    def own(half, kind, target, index):
        copy = remote(
            kv.at[seq, half], kv.at[seq, half], kv_send.at[index], kv_recv.at[kind, half], target
        )
        copy.start()
        return copy

    sends = [own(0, 1, ahead, 0), own(0, 2, behind, 1), own(0, 0, near, 2)]
    got_wv.wait()

    def value_tile(i):
        raw = times(normed[...], wv[:, at_tile(i, tile)]).astype(LOW)
        for g in range(2):
            kv[seq, 1, 2 * i + g] = raw[:, g * hd : (g + 1) * hd]

    over_tiles(heads // 2, value_tile)
    sends += [own(1, 1, ahead, 3), own(1, 2, behind, 4), own(1, 0, near, 5)]
    got_wq.wait()
    scale = math.log2(math.e) / math.sqrt(hd)

    def query_tile(i):
        raw = times(normed[...], wq[:, at_tile(i, tile)])
        query_raw[:, at_tile(i, tile)] = raw
        for g in range(2):
            head = raw[:, g * hd : (g + 1) * hd]
            scaled = head * inverse_rms(head) * (query_gain[...].astype(jnp.float32) * scale)
            query[i, g * rows : (g + 1) * rows, :] = turn(scaled).astype(LOW)

    over_tiles(heads, query_tile)
    total[...] = jnp.zeros_like(total)
    weight_sum[...] = jnp.zeros_like(weight_sum)
    for copy in metas:
        copy.wait()

    def attend(slot):
        key_place = meta[slot, 0:1, :].astype(jnp.float32)
        key_segment = meta[slot, 1:2, :].astype(jnp.float32)
        allowed = (key_place <= place_rows) & (key_segment == segment_rows)
        bias[...] = jnp.where(allowed, 0.0, NEGATIVE)

        def head(j):
            scores = times_turned(query[j], kv[slot, 0, j])
            weights = jnp.concatenate(
                [jnp.exp2(scores[g * rows : (g + 1) * rows] + bias[...]) for g in range(2)], axis=0
            )
            weight_sum[j] += weights[:, :hd] + weights[:, hd:]
            total[j] += times(weights.astype(LOW), kv[slot, 1, j])

        over_tiles(heads, head)

    def arrived(slot, kind, half):
        remote(
            kv.at[slot, half], kv.at[slot, half], kv_send.at[0], kv_recv.at[kind, half], near
        ).wait_recv()

    def pass_on(slot, half, kind, target, index):
        copy = remote(
            kv.at[slot, half], kv.at[slot, half], kv_send.at[index], kv_recv.at[kind, half], target
        )
        copy.start()
        sends.append(copy)

    attend(seq)
    near_slot = y * 2 + 1 - core
    arrived(near_slot, 0, 0)
    arrived(near_slot, 0, 1)
    attend(near_slot)
    before_slot, after_slot, across_slot = before * 2 + core, after * 2 + core, across * 2 + core
    arrived(before_slot, 1, 0)
    pass_on(before_slot, 0, 3, ahead, 6)
    pass_on(before_slot, 0, 4, near, 7)
    arrived(after_slot, 2, 0)
    pass_on(after_slot, 0, 5, near, 8)
    arrived(after_slot, 2, 1)
    pass_on(after_slot, 1, 3, behind, 9)
    pass_on(after_slot, 1, 5, near, 10)
    arrived(before_slot, 1, 1)
    pass_on(before_slot, 1, 4, near, 11)
    attend(before_slot)
    attend(after_slot)
    for far_y, kind in ((before, 4), (after, 5)):
        slot = far_y * 2 + 1 - core
        arrived(slot, kind, 0)
        arrived(slot, kind, 1)
        attend(slot)
    arrived(across_slot, 3, 0)
    pass_on(across_slot, 0, 6, near, 12)
    arrived(across_slot, 3, 1)
    pass_on(across_slot, 1, 6, near, 13)
    attend(across_slot)
    far_slot = across * 2 + 1 - core
    arrived(far_slot, 6, 0)
    arrived(far_slot, 6, 1)
    attend(far_slot)

    def finish(j):
        inverse = 1.0 / jnp.sum(weight_sum[j], axis=-1, keepdims=True)
        result = total[j] * inverse
        total[j] = result
        weight_sum[j] = jnp.broadcast_to(inverse, result.shape)
        for g in range(2):
            attended[:, at_tile(2 * j + g, hd)] = result[g * rows : (g + 1) * rows].astype(LOW)

    over_tiles(heads, finish)
    got_wo.wait()
    wide = 256
    features = tokens.shape[1]
    hidden = wg.shape[1]

    def out_tile(i):
        part_out[0, :, at_tile(i, wide)] = times(attended[...], wo[:, at_tile(i, wide)]).astype(LOW)

    over_tiles(features // wide, out_tile)
    first = remote(part_out.at[0], part_in.at[0], pair_send.at[0], pair_recv.at[0], pair)
    first.start()
    got_wd.wait()

    def act_grad_tile(i):
        act_grad[:, at_tile(i, wide)] = times_turned(cotangent[...], wd[at_tile(i, wide), :])

    over_tiles(hidden // wide, act_grad_tile)
    got_wg.wait()
    got_wu.wait()
    first.wait()
    mid = (
        tokens[...].astype(jnp.float32)
        + (part_out[0].astype(jnp.float32) + part_in[0].astype(jnp.float32))
    )
    middle[...] = mid
    normed_mlp[...] = (mid * inverse_rms(mid) * mlp_gain[...].astype(jnp.float32)).astype(LOW)

    def hidden_tile(i):
        here = at_tile(i, wide)
        gate_here = times(normed_mlp[...], wg[:, here])
        up_here = times(normed_mlp[...], wu[:, here])
        sigmoid = 1.0 / (1.0 + jnp.exp(-gate_here))
        silu = gate_here * sigmoid
        grad = act_grad[:, here]
        activated[:, here] = (silu * up_here).astype(LOW)
        gate_grad[:, here] = (
            grad * up_here * sigmoid * (1.0 + gate_here * (1.0 - sigmoid))
        ).astype(LOW)
        up_grad[:, here] = (grad * silu).astype(LOW)

    over_tiles(hidden // wide, hidden_tile)

    def back_tile(i):
        here = at_tile(i, wide)
        part_out[1, :, here] = (
            times_turned(gate_grad[...], wg[here, :]) + times_turned(up_grad[...], wu[here, :])
        ).astype(LOW)

    over_tiles(features // wide, back_tile)
    second = remote(part_out.at[1], part_in.at[1], pair_send.at[1], pair_recv.at[1], pair)
    second.start()

    def down_tile(i):
        mlp_out[:, at_tile(i, wide)] = times(activated[...], wd[:, at_tile(i, wide)]).astype(LOW)

    over_tiles(features // wide, down_tile)
    for copy in sends:
        copy.wait_send()
    second.wait()
    mid = middle[...]
    inverse = inverse_rms(mid)
    dy = part_out[1].astype(jnp.float32) + part_in[1].astype(jnp.float32)
    mlp_gain_grad[...] = jnp.sum(dy * mid * inverse, axis=0, keepdims=True)
    scaled = dy * mlp_gain[...].astype(jnp.float32)
    grad = (
        cotangent[...].astype(jnp.float32)
        + inverse * scaled
        - mid * (inverse * inverse * inverse) * jnp.mean(scaled * mid, axis=-1, keepdims=True)
    )
    grad_middle[...] = grad
    middle_low[...] = grad.astype(LOW)

    def attended_grad_tile(j):
        both = times_turned(middle_low[...], wo[at_tile(j, 2 * hd), :]).astype(LOW)
        both = both.astype(jnp.float32)
        for g in range(2):
            here = slice(g * rows, (g + 1) * rows)
            normal = both[:, g * hd : (g + 1) * hd] * weight_sum[j, here, :]
            attended_grad[j, here, :] = normal.astype(LOW)
            inner[j, here, :] = jnp.broadcast_to(
                jnp.sum(normal * total[j, here, :], axis=-1, keepdims=True), (rows, hd)
            )

    over_tiles(heads, attended_grad_tile)


def forward(
    tokens, cotangent, positions, segments, attention_gain, query_weight, key_weight, value_weight,
    query_gain, key_gain, out_weight, mlp_gain, gate_weight, up_weight, down_weight,
):
    rows, features = tokens.shape
    hd = query_gain.shape[1]
    heads = key_weight.shape[1] // hd
    q_width, k_width, hidden = query_weight.shape[1], key_weight.shape[1], gate_weight.shape[1]
    half = jnp.arange(hd // 2, dtype=jnp.float32)
    inverse = 1.0 / ROPE_BASE ** (half * 2.0 / hd)
    frequencies = jnp.concatenate([inverse, inverse])[None]
    vmem = pl.BlockSpec(memory_space=pltpu.VMEM)
    far = pl.BlockSpec(memory_space=pl.ANY)
    f32 = jnp.float32
    outs = dict(
        normed=((rows, features), LOW),
        query_raw=((rows, q_width), f32),
        key_raw=((rows, k_width), f32),
        query=((heads, 2 * rows, hd), LOW),
        kv=((8, 2, heads, rows, hd), LOW),
        meta=((8, 8, rows), jnp.int32),
        cosine=((rows, hd), f32),
        sine=((rows, hd), f32),
        attended=((rows, q_width), LOW),
        middle=((rows, features), f32),
        normed_mlp=((rows, features), LOW),
        activated=((rows, hidden), LOW),
        gate_grad=((rows, hidden), LOW),
        up_grad=((rows, hidden), LOW),
        mlp_out=((rows, features), LOW),
        grad_middle=((rows, features), f32),
        middle_low=((rows, features), LOW),
        attended_grad=((heads, 2 * rows, hd), LOW),
        inner=((heads, 2 * rows, hd), f32),
        mlp_gain_grad=((1, features), f32),
    )
    weights = (
        query_weight, key_weight, value_weight, out_weight, gate_weight, up_weight, down_weight,
    )
    results = pl.pallas_call(
        forward_kernel,
        out_shape=[jax.ShapeDtypeStruct(shape, kind) for shape, kind in outs.values()],
        in_specs=[vmem] * 9 + [far] * 7,
        out_specs=[vmem] * len(outs),
        scratch_shapes=[pltpu.VMEM(w.shape, LOW) for w in weights]
        + [
            pltpu.VMEM((rows, rows), f32),
            pltpu.VMEM((heads, 2 * rows, hd), f32),
            pltpu.VMEM((heads, 2 * rows, hd), f32),
            pltpu.VMEM((rows, hidden), f32),
            pltpu.VMEM((2, rows, features), LOW),
            pltpu.VMEM((2, rows, features), LOW),
            pltpu.SemaphoreType.DMA((7,)),
            pltpu.SemaphoreType.DMA((14,)),
            pltpu.SemaphoreType.DMA((7, 2)),
            pltpu.SemaphoreType.DMA((7,)),
            pltpu.SemaphoreType.DMA((7,)),
            pltpu.SemaphoreType.DMA((2,)),
            pltpu.SemaphoreType.DMA((2,)),
        ],
        compiler_params=pltpu.CompilerParams(
            collective_id=1, has_side_effects=True, vmem_limit_bytes=60 * 1024 * 1024
        ),
    )(
        tokens,
        cotangent,
        positions,
        segments,
        frequencies,
        attention_gain,
        query_gain,
        key_gain,
        mlp_gain,
        *weights,
    )
    return dict(zip(outs, results))


def backward_kernel(query, kv, meta, positions, segments, attended_grad, inner, query_grad, kv_grad, bias):
    rows = positions.shape[1]
    heads, hd = kv.shape[2], kv.shape[4]
    place_rows = jnp.broadcast_to(positions[...].astype(jnp.float32), (rows, rows)).T
    segment_rows = jnp.broadcast_to(segments[...].astype(jnp.float32), (rows, rows)).T
    query_grad[...] = jnp.zeros_like(query_grad)

    def block(slot):
        key_place = meta[slot, 0:1, :].astype(jnp.float32)
        key_segment = meta[slot, 1:2, :].astype(jnp.float32)
        allowed = (key_place <= place_rows) & (key_segment == segment_rows)
        bias[...] = jnp.where(allowed, 0.0, NEGATIVE)

        def head(j):
            key, value = kv[slot, 0, j], kv[slot, 1, j]
            scores = times_turned(query[j], key)
            grad = times_turned(attended_grad[j], value)
            weights, scores_grad = [], []
            for g in range(2):
                here = slice(g * rows, (g + 1) * rows)
                weight = jnp.exp2(scores[here] + bias[...])
                inside = jnp.concatenate([inner[j, here, :]] * 2, axis=1)
                weights.append(weight.astype(LOW))
                scores_grad.append((weight * (grad[here] - inside)).astype(LOW))
            weights = jnp.concatenate(weights, axis=0)
            scores_grad = jnp.concatenate(scores_grad, axis=0)
            query_grad[j] += times(scores_grad, key)
            kv_grad[slot, 0, j] = (
                lax.dot_general(
                    scores_grad, query[j], (((0,), (0,)), ((), ())),
                    preferred_element_type=jnp.float32,
                )
                * math.log(2)
            ).astype(LOW)
            kv_grad[slot, 1, j] = lax.dot_general(
                weights, attended_grad[j], (((0,), (0,)), ((), ())),
                preferred_element_type=jnp.float32,
            ).astype(LOW)

        over_tiles(heads, head)

    over_tiles(8, block)


def attention_backward(f, positions, segments):
    vmem = pl.BlockSpec(memory_space=pltpu.VMEM)
    return pl.pallas_call(
        backward_kernel,
        out_shape=[
            jax.ShapeDtypeStruct(f["query"].shape, jnp.float32),
            jax.ShapeDtypeStruct(f["kv"].shape, LOW),
        ],
        in_specs=[vmem] * 7,
        out_specs=[vmem] * 2,
        scratch_shapes=[pltpu.VMEM((positions.shape[1], positions.shape[1]), jnp.float32)],
        compiler_params=pltpu.CompilerParams(vmem_limit_bytes=60 * 1024 * 1024),
    )(f["query"], f["kv"], f["meta"], positions, segments, f["attended_grad"], f["inner"])


def mean_rms(entries):
    return lax.rsqrt(jnp.mean(entries * entries, axis=-1, keepdims=True) + EPS)


def norm_back(entries, gain_vec, gradient):
    inverse = mean_rms(entries)
    scaled = gradient * gain_vec
    gain_grad = jnp.sum((gradient * entries * inverse).reshape(-1, entries.shape[-1]), axis=0)
    entries_grad = inverse * scaled - entries * inverse**3 * jnp.mean(
        scaled * entries, axis=-1, keepdims=True
    )
    return (entries_grad, gain_grad)


def dense(left, right):
    return jnp.dot(left, right, preferred_element_type=jnp.float32)


def shards(
    tokens,
    cotangent,
    positions,
    segments,
    attention_gain,
    query_weight,
    key_weight,
    value_weight,
    query_gain,
    key_gain,
    out_weight,
    mlp_gain,
    gate_weight,
    up_weight,
    down_weight,
):
    head_dim = query_gain.shape[0]
    local_rows = tokens.shape[1]
    key_heads = key_weight.shape[1] // head_dim
    query_heads = query_weight.shape[1] // head_dim
    f = forward(
        tokens[0], cotangent[0], positions, segments, attention_gain[None], query_weight,
        key_weight, value_weight, query_gain[None], key_gain[None], out_weight, mlp_gain[None],
        gate_weight, up_weight, down_weight,
    )
    score_scale = 1.0 / math.sqrt(head_dim)
    attention_gain = attention_gain.astype(jnp.float32)
    query_gain = query_gain.astype(jnp.float32)
    key_gain = key_gain.astype(jnp.float32)
    inputs = tokens[0].astype(jnp.float32)
    query_grad_blocks, kv_grad_all = attention_backward(f, positions, segments)
    mlp_other = lax.ppermute(f["mlp_out"], "tensor", ((0, 1), (1, 0)))
    output = (
        f["middle"] + (f["mlp_out"].astype(jnp.float32) + mlp_other.astype(jnp.float32))
    ).astype(jnp.bfloat16)[None]
    kv_grad = lax.psum_scatter(kv_grad_all, "seq", scatter_dimension=0, tiled=True)[0]
    cosine_table, sine_table = f["cosine"][:, None, :], f["sine"][:, None, :]

    def unrotate(gradient):
        half_dim = head_dim // 2
        turned = jnp.concatenate([gradient[..., half_dim:], gradient[..., :half_dim]], axis=-1)
        return gradient * cosine_table - turned * sine_table

    query_rot_grad = (
        query_grad_blocks.reshape(key_heads, 2, local_rows, head_dim)
        .transpose(2, 0, 1, 3)
        .reshape(local_rows, query_heads, head_dim)
        * score_scale
    )
    query_raw_grad, query_gain_part = norm_back(
        f["query_raw"].reshape(local_rows, query_heads, head_dim),
        query_gain,
        unrotate(query_rot_grad),
    )
    key_raw_grad, key_gain_part = norm_back(
        f["key_raw"].reshape(local_rows, key_heads, head_dim),
        key_gain,
        unrotate(kv_grad[0].astype(jnp.float32).transpose(1, 0, 2)),
    )
    query_grad_low = query_raw_grad.reshape(local_rows, -1).astype(jnp.bfloat16)
    key_grad_low = key_raw_grad.reshape(local_rows, -1).astype(jnp.bfloat16)
    value_grad_low = kv_grad[1].transpose(1, 0, 2).reshape(local_rows, -1)
    normed, normed_mlp, middle_low = f["normed"], f["normed_mlp"], f["middle_low"]
    attended_low, grad_middle = f["attended"], f["grad_middle"]
    gate_grad_low, up_grad_low, activated = f["gate_grad"], f["up_grad"], f["activated"]
    upstream = cotangent[0]
    mlp_gain_grad = f["mlp_gain_grad"][0]
    attention_partial = (
        dense(query_grad_low, query_weight.T)
        + dense(key_grad_low, key_weight.T)
        + dense(value_grad_low, value_weight.T)
    )
    partial_low = attention_partial.astype(jnp.bfloat16)
    attention_gain_part = jnp.sum(attention_partial * inputs * mean_rms(inputs), axis=0)
    width = gate_weight.shape[1]
    q_width, k_width = query_weight.shape[1], key_weight.shape[1]
    pieces = (
        ((0, 0, 0, width),),
        ((0, 1, 0, width),),
        ((1, 2, 0, width),),
        ((2, 3, 0, q_width), (2, 4, q_width, k_width)),
        ((2, 5, 0, k_width), (3, 6, k_width, q_width)),
    )
    shares, gains, partial_other = scatter_gradients(
        pieces,
        (normed_mlp, upstream, normed, middle_low),
        (
            gate_grad_low,
            up_grad_low,
            activated,
            query_grad_low,
            key_grad_low,
            value_grad_low,
            attended_low,
        ),
        pack_gains(attention_gain_part, 0.5 * mlp_gain_grad, query_gain_part, key_gain_part),
        partial_low,
    )
    normed_grad = partial_low.astype(jnp.float32) + partial_other.astype(jnp.float32)
    input_part, _ = norm_back(inputs, attention_gain, normed_grad)
    input_grad = (grad_middle + input_part).astype(jnp.bfloat16)[None]
    return (
        output,
        input_grad,
        shares[3][:, :q_width],
        shares[3][:, q_width:],
        shares[4][:, :k_width],
        shares[4][:, k_width:].T,
        shares[0],
        shares[1],
        shares[2].T,
        gains[0, 0:16],
        gains[0, 16:32],
        gains[0, 32:34],
        gains[0, 34:36],
    )


def solution(mesh):
    return jax.shard_map(
        shards,
        mesh=mesh,
        in_specs=(
            P("dp", "seq", None),
            P("dp", "seq", None),
            P("dp", "seq"),
            P("dp", "seq"),
            P(),
            P(None, "tensor"),
            P(None, "tensor"),
            P(None, "tensor"),
            P(),
            P(),
            P("tensor", None),
            P(),
            P(None, "tensor"),
            P(None, "tensor"),
            P("tensor", None),
        ),
        out_specs=(
            P("dp", "seq", None),
            P("dp", "seq", None),
            P(("dp", "seq"), "tensor"),
            P(("dp", "seq"), "tensor"),
            P(("dp", "seq"), "tensor"),
            P("tensor", ("dp", "seq")),
            P(("dp", "seq"), "tensor"),
            P(("dp", "seq"), "tensor"),
            P("tensor", ("dp", "seq")),
            P(("dp", "seq")),
            P(("dp", "seq")),
            P(("dp", "seq")),
            P(("dp", "seq")),
        ),
        check_vma=False,
    )
```

```python
import functools
import math

import jax
import jax.numpy as jnp
from jax import lax
from jax.experimental import pallas as pl
from jax.experimental.pallas import tpu as pltpu
from jax.sharding import PartitionSpec as P

EPS = 1e-06
ROPE_BASE = 1000000.0
NEGATIVE = -1e30


MESH = pl.DeviceIdType.MESH
CHUNK = 16
DIMS = ("x3", "x1", "y3", "y1", "z")
LOW = jnp.bfloat16


def place():
    dp = lax.axis_index("dp")
    seq = lax.axis_index("seq")
    tensor = lax.axis_index("tensor")
    x, z = dp // 2, dp % 2
    y, core = seq // 2, seq % 2
    x_near = x + 1 - 2 * (x % 2)
    y_near = y + 1 - 2 * (y % 2)
    bits = {
        "core": core,
        "x3": x // 2,
        "x1": (x // 2 + x % 2) % 2,
        "y3": y // 2,
        "y1": (y // 2 + y % 2) % 2,
        "z": z,
    }
    partners = {
        "core": (dp, seq + 1 - 2 * core, tensor),
        "x3": ((3 - x) * 2 + z, seq, tensor),
        "x1": (x_near * 2 + z, seq, tensor),
        "y3": (dp, (3 - y) * 2 + core, tensor),
        "y1": (dp, y_near * 2 + core, tensor),
        "z": (dp + 1 - 2 * z, seq, tensor),
        "tensor": (dp, seq, 1 - tensor),
    }
    return bits, partners


def greet(partners):
    barrier = pltpu.get_barrier_semaphore()
    for partner in partners:
        pl.semaphore_signal(barrier, inc=1, device_id=partner, device_id_type=MESH)
    pl.semaphore_wait(barrier, len(partners))


def stream_order(stream):
    return ("core",) + tuple(DIMS[(stream + i) % len(DIMS)] for i in range(len(DIMS)))


def slot_chunks(order):
    chunks = []
    for slot in range(2 ** len(order)):
        bit = {d: (slot >> (len(order) - 1 - i)) & 1 for i, d in enumerate(order)}
        x = 2 * bit["x3"] + (bit["x3"] ^ bit["x1"])
        y = 2 * bit["y3"] + (bit["y3"] ^ bit["y1"])
        chunks.append(((x * 2 + bit["z"]) * 4 + y) * 2 + bit["core"])
    return chunks


def remote(source, target, out_sem, in_sem, partner):
    return pltpu.make_async_remote_copy(
        src_ref=source,
        dst_ref=target,
        send_sem=out_sem,
        recv_sem=in_sem,
        device_id=partner,
        device_id_type=MESH,
    )


def over_tiles(count, body):
    def step(i, _):
        body(i)
        return 0

    lax.fori_loop(0, count, step, 0)


def at_tile(i, size):
    return pl.ds(pl.multiple_of(i * size, size), size)


def times(left, right):
    return jnp.dot(left, right, preferred_element_type=jnp.float32)


def times_turned(left, right):
    return lax.dot_general(
        left, right, (((1,), (1,)), ((), ())), preferred_element_type=jnp.float32
    )


def inverse_rms(entries):
    return lax.rsqrt(jnp.mean(entries * entries, axis=-1, keepdims=True) + EPS)


def forward_kernel(
    tokens,
    cotangent,
    positions,
    segments,
    frequencies,
    attention_gain,
    query_gain,
    key_gain,
    mlp_gain,
    wq_far,
    wk_far,
    wv_far,
    wo_far,
    wg_far,
    wu_far,
    wd_far,
    normed,
    query_raw,
    key_raw,
    query,
    kv,
    meta,
    cosine,
    sine,
    attended,
    middle,
    normed_mlp,
    activated,
    gate_grad,
    up_grad,
    mlp_out,
    grad_middle,
    middle_low,
    attended_grad,
    inner,
    mlp_gain_grad,
    wq,
    wk,
    wv,
    wo,
    wg,
    wu,
    wd,
    bias,
    total,
    weight_sum,
    act_grad,
    part_out,
    part_in,
    weight_sem,
    kv_send,
    kv_recv,
    meta_send,
    meta_recv,
    pair_send,
    pair_recv,
):
    dp, seq, tensor = lax.axis_index("dp"), lax.axis_index("seq"), lax.axis_index("tensor")
    core, y = seq % 2, seq // 2
    after, before, across = (y + 1) % 4, (y + 3) % 4, (y + 2) % 4
    near = (dp, y * 2 + 1 - core, tensor)
    ahead = (dp, after * 2 + core, tensor)
    behind = (dp, before * 2 + core, tensor)
    pair = (dp, seq, 1 - tensor)
    others = [(dp, (seq + step) % 8, tensor) for step in range(1, 8)]
    rows = tokens.shape[0]
    heads = kv.shape[2]
    hd = kv.shape[4]
    greet(others + [pair])
    fetches = [
        pltpu.make_async_copy(far, held, weight_sem.at[i])
        for i, (far, held) in enumerate(
            zip(
                (wk_far, wv_far, wq_far, wo_far, wd_far, wg_far, wu_far),
                (wk, wv, wq, wo, wd, wg, wu),
            )
        )
    ]
    for fetch in fetches:
        fetch.start()
    got_wk, got_wv, got_wq, got_wo, got_wd, got_wg, got_wu = fetches

    meta[seq] = jnp.zeros_like(meta[seq])
    meta[seq, 0:1, :] = positions[...]
    meta[seq, 1:2, :] = segments[...]
    metas = [
        remote(meta.at[seq], meta.at[seq], meta_send.at[i], meta_recv.at[i], other)
        for i, other in enumerate(others)
    ]
    for copy in metas:
        copy.start()

    place_rows = jnp.broadcast_to(positions[...].astype(jnp.float32), (rows, rows)).T
    segment_rows = jnp.broadcast_to(segments[...].astype(jnp.float32), (rows, rows)).T
    angle = place_rows[:, :hd] * frequencies[...]
    cosine[...] = jnp.cos(angle)
    lane = lax.broadcasted_iota(jnp.int32, (rows, hd), 1)
    sine[...] = jnp.where(lane < hd // 2, -1.0, 1.0) * jnp.sin(angle)

    def turn(entries):
        return entries * cosine[...] + pltpu.roll(entries, hd // 2, 1) * sine[...]

    x = tokens[...].astype(jnp.float32)
    normed[...] = (x * inverse_rms(x) * attention_gain[...].astype(jnp.float32)).astype(LOW)

    tile = 2 * hd
    got_wk.wait()

    def key_tile(i):
        raw = times(normed[...], wk[:, at_tile(i, tile)])
        key_raw[:, at_tile(i, tile)] = raw
        for g in range(2):
            head = raw[:, g * hd : (g + 1) * hd]
            scaled = head * inverse_rms(head) * key_gain[...].astype(jnp.float32)
            kv[seq, 0, 2 * i + g] = turn(scaled).astype(LOW)

    over_tiles(heads // 2, key_tile)

    def own(half, kind, target, index):
        copy = remote(
            kv.at[seq, half], kv.at[seq, half], kv_send.at[index], kv_recv.at[kind, half], target
        )
        copy.start()
        return copy

    sends = [own(0, 1, ahead, 0), own(0, 2, behind, 1), own(0, 0, near, 2)]
    got_wv.wait()

    def value_tile(i):
        raw = times(normed[...], wv[:, at_tile(i, tile)]).astype(LOW)
        for g in range(2):
            kv[seq, 1, 2 * i + g] = raw[:, g * hd : (g + 1) * hd]

    over_tiles(heads // 2, value_tile)
    sends += [own(1, 1, ahead, 3), own(1, 2, behind, 4), own(1, 0, near, 5)]
    got_wq.wait()
    scale = math.log2(math.e) / math.sqrt(hd)

    def query_tile(i):
        raw = times(normed[...], wq[:, at_tile(i, tile)])
        query_raw[:, at_tile(i, tile)] = raw
        for g in range(2):
            head = raw[:, g * hd : (g + 1) * hd]
            scaled = head * inverse_rms(head) * (query_gain[...].astype(jnp.float32) * scale)
            query[i, g * rows : (g + 1) * rows, :] = turn(scaled).astype(LOW)

    over_tiles(heads, query_tile)
    total[...] = jnp.zeros_like(total)
    weight_sum[...] = jnp.zeros_like(weight_sum)
    for copy in metas:
        copy.wait()

    def attend(slot):
        key_place = meta[slot, 0:1, :].astype(jnp.float32)
        key_segment = meta[slot, 1:2, :].astype(jnp.float32)
        allowed = (key_place <= place_rows) & (key_segment == segment_rows)
        bias[...] = jnp.where(allowed, 0.0, NEGATIVE)

        def head(j):
            scores = times_turned(query[j], kv[slot, 0, j])
            weights = jnp.concatenate(
                [jnp.exp2(scores[g * rows : (g + 1) * rows] + bias[...]) for g in range(2)], axis=0
            )
            weight_sum[j] += weights[:, :hd] + weights[:, hd:]
            total[j] += times(weights.astype(LOW), kv[slot, 1, j])

        over_tiles(heads, head)

    def arrived(slot, kind, half):
        remote(
            kv.at[slot, half], kv.at[slot, half], kv_send.at[0], kv_recv.at[kind, half], near
        ).wait_recv()

    def pass_on(slot, half, kind, target, index):
        copy = remote(
            kv.at[slot, half], kv.at[slot, half], kv_send.at[index], kv_recv.at[kind, half], target
        )
        copy.start()
        sends.append(copy)

    attend(seq)
    near_slot = y * 2 + 1 - core
    arrived(near_slot, 0, 0)
    arrived(near_slot, 0, 1)
    attend(near_slot)
    before_slot, after_slot, across_slot = before * 2 + core, after * 2 + core, across * 2 + core
    arrived(before_slot, 1, 0)
    pass_on(before_slot, 0, 3, ahead, 6)
    pass_on(before_slot, 0, 4, near, 7)
    arrived(after_slot, 2, 0)
    pass_on(after_slot, 0, 5, near, 8)
    arrived(after_slot, 2, 1)
    pass_on(after_slot, 1, 3, behind, 9)
    pass_on(after_slot, 1, 5, near, 10)
    arrived(before_slot, 1, 1)
    pass_on(before_slot, 1, 4, near, 11)
    attend(before_slot)
    attend(after_slot)
    for far_y, kind in ((before, 4), (after, 5)):
        slot = far_y * 2 + 1 - core
        arrived(slot, kind, 0)
        arrived(slot, kind, 1)
        attend(slot)
    arrived(across_slot, 3, 0)
    pass_on(across_slot, 0, 6, near, 12)
    arrived(across_slot, 3, 1)
    pass_on(across_slot, 1, 6, near, 13)
    attend(across_slot)
    far_slot = across * 2 + 1 - core
    arrived(far_slot, 6, 0)
    arrived(far_slot, 6, 1)
    attend(far_slot)

    def finish(j):
        inverse = 1.0 / jnp.sum(weight_sum[j], axis=-1, keepdims=True)
        result = total[j] * inverse
        total[j] = result
        weight_sum[j] = jnp.broadcast_to(inverse, result.shape)
        for g in range(2):
            attended[:, at_tile(2 * j + g, hd)] = result[g * rows : (g + 1) * rows].astype(LOW)

    over_tiles(heads, finish)
    got_wo.wait()
    wide = 256
    features = tokens.shape[1]
    hidden = wg.shape[1]

    def out_tile(i):
        part_out[0, :, at_tile(i, wide)] = times(attended[...], wo[:, at_tile(i, wide)]).astype(LOW)

    over_tiles(features // wide, out_tile)
    first = remote(part_out.at[0], part_in.at[0], pair_send.at[0], pair_recv.at[0], pair)
    first.start()
    got_wd.wait()

    def act_grad_tile(i):
        act_grad[:, at_tile(i, wide)] = times_turned(cotangent[...], wd[at_tile(i, wide), :])

    over_tiles(hidden // wide, act_grad_tile)
    got_wg.wait()
    got_wu.wait()
    first.wait()
    mid = (
        tokens[...].astype(jnp.float32)
        + (part_out[0].astype(jnp.float32) + part_in[0].astype(jnp.float32))
    )
    middle[...] = mid
    normed_mlp[...] = (mid * inverse_rms(mid) * mlp_gain[...].astype(jnp.float32)).astype(LOW)

    def hidden_tile(i):
        here = at_tile(i, wide)
        gate_here = times(normed_mlp[...], wg[:, here])
        up_here = times(normed_mlp[...], wu[:, here])
        sigmoid = 1.0 / (1.0 + jnp.exp(-gate_here))
        silu = gate_here * sigmoid
        grad = act_grad[:, here]
        activated[:, here] = (silu * up_here).astype(LOW)
        gate_grad[:, here] = (
            grad * up_here * sigmoid * (1.0 + gate_here * (1.0 - sigmoid))
        ).astype(LOW)
        up_grad[:, here] = (grad * silu).astype(LOW)

    over_tiles(hidden // wide, hidden_tile)

    def back_tile(i):
        here = at_tile(i, wide)
        part_out[1, :, here] = (
            times_turned(gate_grad[...], wg[here, :]) + times_turned(up_grad[...], wu[here, :])
        ).astype(LOW)

    over_tiles(features // wide, back_tile)
    second = remote(part_out.at[1], part_in.at[1], pair_send.at[1], pair_recv.at[1], pair)
    second.start()

    def down_tile(i):
        mlp_out[:, at_tile(i, wide)] = times(activated[...], wd[:, at_tile(i, wide)]).astype(LOW)

    over_tiles(features // wide, down_tile)
    for copy in sends:
        copy.wait_send()
    second.wait()
    mid = middle[...]
    inverse = inverse_rms(mid)
    dy = part_out[1].astype(jnp.float32) + part_in[1].astype(jnp.float32)
    mlp_gain_grad[...] = jnp.sum(dy * mid * inverse, axis=0, keepdims=True)
    scaled = dy * mlp_gain[...].astype(jnp.float32)
    grad = (
        cotangent[...].astype(jnp.float32)
        + inverse * scaled
        - mid * (inverse * inverse * inverse) * jnp.mean(scaled * mid, axis=-1, keepdims=True)
    )
    grad_middle[...] = grad
    middle_low[...] = grad.astype(LOW)

    def attended_grad_tile(j):
        both = times_turned(middle_low[...], wo[at_tile(j, 2 * hd), :]).astype(LOW)
        both = both.astype(jnp.float32)
        for g in range(2):
            here = slice(g * rows, (g + 1) * rows)
            normal = both[:, g * hd : (g + 1) * hd] * weight_sum[j, here, :]
            attended_grad[j, here, :] = normal.astype(LOW)
            summed = jnp.sum((normal * total[j, here, :]).T, axis=0, keepdims=True)
            inner[j, :, here] = jnp.broadcast_to(summed, (8, rows))

    over_tiles(heads, attended_grad_tile)


def forward(
    tokens, cotangent, positions, segments, attention_gain, query_weight, key_weight, value_weight,
    query_gain, key_gain, out_weight, mlp_gain, gate_weight, up_weight, down_weight,
):
    rows, features = tokens.shape
    hd = query_gain.shape[1]
    heads = key_weight.shape[1] // hd
    q_width, k_width, hidden = query_weight.shape[1], key_weight.shape[1], gate_weight.shape[1]
    half = jnp.arange(hd // 2, dtype=jnp.float32)
    inverse = 1.0 / ROPE_BASE ** (half * 2.0 / hd)
    frequencies = jnp.concatenate([inverse, inverse])[None]
    vmem = pl.BlockSpec(memory_space=pltpu.VMEM)
    far = pl.BlockSpec(memory_space=pl.ANY)
    f32 = jnp.float32
    outs = dict(
        normed=((rows, features), LOW),
        query_raw=((rows, q_width), f32),
        key_raw=((rows, k_width), f32),
        query=((heads, 2 * rows, hd), LOW),
        kv=((8, 2, heads, rows, hd), LOW),
        meta=((8, 8, rows), jnp.int32),
        cosine=((rows, hd), f32),
        sine=((rows, hd), f32),
        attended=((rows, q_width), LOW),
        middle=((rows, features), f32),
        normed_mlp=((rows, features), LOW),
        activated=((rows, hidden), LOW),
        gate_grad=((rows, hidden), LOW),
        up_grad=((rows, hidden), LOW),
        mlp_out=((rows, features), LOW),
        grad_middle=((rows, features), f32),
        middle_low=((rows, features), LOW),
        attended_grad=((heads, 2 * rows, hd), LOW),
        inner=((heads, 8, 2 * rows), f32),
        mlp_gain_grad=((1, features), f32),
    )
    weights = (
        query_weight, key_weight, value_weight, out_weight, gate_weight, up_weight, down_weight,
    )
    results = pl.pallas_call(
        forward_kernel,
        out_shape=[jax.ShapeDtypeStruct(shape, kind) for shape, kind in outs.values()],
        in_specs=[vmem] * 9 + [far] * 7,
        out_specs=[vmem] * len(outs),
        scratch_shapes=[pltpu.VMEM(w.shape, LOW) for w in weights]
        + [
            pltpu.VMEM((rows, rows), f32),
            pltpu.VMEM((heads, 2 * rows, hd), f32),
            pltpu.VMEM((heads, 2 * rows, hd), f32),
            pltpu.VMEM((rows, hidden), f32),
            pltpu.VMEM((2, rows, features), LOW),
            pltpu.VMEM((2, rows, features), LOW),
            pltpu.SemaphoreType.DMA((7,)),
            pltpu.SemaphoreType.DMA((14,)),
            pltpu.SemaphoreType.DMA((7, 2)),
            pltpu.SemaphoreType.DMA((7,)),
            pltpu.SemaphoreType.DMA((7,)),
            pltpu.SemaphoreType.DMA((2,)),
            pltpu.SemaphoreType.DMA((2,)),
        ],
        compiler_params=pltpu.CompilerParams(
            collective_id=1, has_side_effects=True, vmem_limit_bytes=60 * 1024 * 1024
        ),
    )(
        tokens,
        cotangent,
        positions,
        segments,
        frequencies,
        attention_gain,
        query_gain,
        key_gain,
        mlp_gain,
        *weights,
    )
    return dict(zip(outs, results))


EARLY = (("normed_mlp", "gate_grad"), ("normed_mlp", "up_grad"), ("cotangent", "activated"), ("middle_low", "attended"))
EARLY_TILES = (6, 5, 4, 4, 3)
LATE_TILES = (2, 2, 2, 1, 1)
WIDE = 256


def split_streams(sizes, tiles):
    bounds, start = [], 0
    for size in sizes:
        bounds.append((start, start + size))
        start += size
    streams, first = [], 0
    for count in tiles:
        last = first + count * WIDE
        pieces = []
        for matrix, (low, high) in enumerate(bounds):
            begin, end = max(first, low), min(last, high)
            if begin < end:
                pieces.append((matrix, begin - low, begin, end - begin))
        streams.append((first, last - first, pieces))
        first = last
    assert first == start
    return streams


class Scatter:
    def __init__(self, streams, lhs, rhs, turned, sent, held, held_first, landed, send_sem, recv_sem, bits, partners):
        self.streams, self.lhs, self.rhs = streams, lhs, rhs
        self.turned, self.sent, self.held, self.held_first = turned, sent, held, held_first
        self.landed, self.send_sem, self.recv_sem = landed, send_sem, recv_sem
        self.bits, self.partners = bits, partners
        self.orders = [stream_order(s) for s in range(len(streams))]
        self.half = landed[0].shape[0]
        self.copies = {}
        self.base = [0] * len(streams)

    def turn(self):
        self.pairs = []
        flipped = {}
        for s, (_, _, pieces) in enumerate(self.streams):
            for matrix, _, _, _ in pieces:
                ref = self.lhs[matrix]
                if (s, id(ref)) in self.pairs:
                    continue
                if id(ref) not in flipped:
                    flipped[id(ref)] = ref[...].T
                index = len(self.pairs)
                self.pairs.append((s, id(ref)))
                for slot, chunk in enumerate(slot_chunks(self.orders[s])):
                    self.turned[index, slot * CHUNK : (slot + 1) * CHUNK, :] = flipped[id(ref)][
                        chunk * CHUNK : (chunk + 1) * CHUNK, :
                    ]

    def product(self, s, target, target_first, offset):
        for matrix, column, first, columns in self.streams[s][2]:
            index = self.pairs.index((s, id(self.lhs[matrix])))
            right = self.rhs[matrix]

            def tile(i, index=index, right=right, column=column, first=first):
                here = pl.multiple_of(i * WIDE, WIDE)
                target[:, pl.ds(target_first + first + here, WIDE)] = times(
                    self.turned[index, pl.ds(pl.multiple_of(offset, CHUNK), self.half), :],
                    right[:, pl.ds(column + here, WIDE)],
                ).astype(LOW)

            over_tiles(columns // WIDE, tile)

    def send(self, step, s, source):
        first, columns, _ = self.streams[s]
        copy = remote(
            source,
            self.landed[step].at[:, pl.ds(first, columns)],
            self.send_sem.at[s, step],
            self.recv_sem.at[s, step],
            self.partners[self.orders[s][step]],
        )
        copy.start()
        self.copies[s, step] = copy

    def open(self):
        core = self.bits["core"]
        for s, (first, columns, _) in enumerate(self.streams):
            self.product(s, self.sent, 0, (1 - core) * self.half)
            self.send(0, s, self.sent.at[:, pl.ds(first, columns)])
        for s in range(len(self.streams)):
            self.product(s, self.held, self.held_first, core * self.half)

    def step(self, step, out=None):
        rows = self.half >> step
        for s, (first, columns, _) in enumerate(self.streams):
            self.copies[s, step].wait()
            mine = pl.ds(self.held_first + first, columns)
            if step == 5:
                out[:, pl.ds(first, columns)] = self.held[
                    pl.ds(pl.multiple_of(self.base[s], CHUNK), CHUNK), mine
                ].astype(jnp.float32) + self.landed[5][:, pl.ds(first, columns)].astype(jnp.float32)
                continue
            tile = min(rows, 64)

            def add(i, s=s, tile=tile, first=first, columns=columns, mine=mine):
                start = pl.multiple_of(i * tile, tile)
                here = pl.ds(pl.multiple_of(self.base[s] + start, tile), tile)
                self.held[here, mine] = (
                    self.held[here, mine]
                    + self.landed[step][pl.ds(start, tile), pl.ds(first, columns)]
                )

            over_tiles(rows // tile, add)
            bit = self.bits[self.orders[s][step + 1]]
            away = pl.multiple_of(self.base[s] + (1 - bit) * (rows // 2), CHUNK)
            self.send(step + 1, s, self.held.at[pl.ds(away, rows // 2), mine])
            self.base[s] = self.base[s] + bit * (rows // 2)


def backward_kernel(early_streams, late_streams, *refs):
    (
        tokens, cotangent, positions, segments, query_gain, key_gain, wq_far, wk_far, wv_far,
        normed, normed_mlp, middle_low, gate_grad, up_grad, activated, attended, query, kv, meta,
        attended_grad, inner, query_raw, key_raw, cosine, sine, mlp_out, mlp_gain_grad,
        early_out, late_out, mlp_other, partial, partial_other, gains,
        turned, sent, held, bias, query_turned, away_grad, near_grad, core_grad, far_grad,
        query_low, key_low, value_low, gains_sent, gains_landed,
    ) = refs[:47]
    early_landed, late_landed = refs[47:53], refs[53:59]
    (
        early_send, early_recv, late_send, late_recv, pair_send, pair_recv, core_send, core_recv,
        far_send, far_recv, gains_send, gains_recv, weight_sem,
    ) = refs[59:]
    bits, partners = place()
    dp, seq, tensor = lax.axis_index("dp"), lax.axis_index("seq"), lax.axis_index("tensor")
    core, y = seq % 2, seq // 2
    rows = tokens.shape[0]
    heads, hd = kv.shape[2], kv.shape[4]
    features = tokens.shape[1]
    half = features // 2
    across = (dp, (y + 2) % 4 * 2 + core, tensor)
    greet(list(partners.values()) + [across])
    pair = partners["tensor"]
    outward = remote(mlp_out, mlp_other, pair_send.at[0], pair_recv.at[0], pair)
    outward.start()
    by_name = dict(
        normed_mlp=normed_mlp, cotangent=cotangent, middle_low=middle_low, gate_grad=gate_grad,
        up_grad=up_grad, activated=activated, attended=attended,
    )
    early = Scatter(
        early_streams, [by_name[l] for l, _ in EARLY], [by_name[r] for _, r in EARLY],
        turned, sent, held, 0, early_landed, early_send, early_recv, bits, partners,
    )
    early.turn()
    early.open()

    place_rows = positions[...].astype(jnp.float32)
    segment_rows = segments[...].astype(jnp.float32)
    query_turned[...] = jnp.zeros_like(query_turned)

    def block(slot, target):
        def column(row):
            return jnp.broadcast_to(row.astype(jnp.float32), (rows, rows)).T

        allowed = (column(meta[slot, 0:1, :]) <= place_rows) & (
            column(meta[slot, 1:2, :]) == segment_rows
        )
        one = jnp.where(allowed, 0.0, NEGATIVE)
        bias[:, :rows] = one
        bias[:, rows:] = one

        def head(j):
            key, value = kv[slot, 0, j], kv[slot, 1, j]
            weight = jnp.exp2(times_turned(key, query[j]) + bias[...])
            grad = times_turned(value, attended_grad[j])
            scores_grad = (weight * (grad - inner[j, 0:1, :])).astype(LOW)
            target[1, j] = times(weight.astype(LOW), attended_grad[j]).astype(LOW)
            target[0, j] = (times(scores_grad, query[j]) * math.log(2)).astype(LOW)
            query_turned[j] += lax.dot_general(
                key, scores_grad, (((0,), (0,)), ((), ())), preferred_element_type=jnp.float32
            )

        over_tiles(heads, head)

    sends = []
    for i, shift in enumerate((2, 1, 3, 0)):
        chip = (y + shift) % 4
        block(chip * 2 + 1 - core, away_grad.at[i])
        copy = remote(
            away_grad.at[i], core_grad.at[i], core_send.at[i], core_recv.at[i], partners["core"]
        )
        copy.start()
        block(chip * 2 + core, near_grad.at[i])
        if i < 4:
            early.step(i)
        copy.wait()
        near_grad[i] = near_grad[i] + core_grad[i]
        if shift:
            copy = remote(
                near_grad.at[i],
                far_grad.at[i],
                far_send.at[i],
                far_recv.at[i],
                (dp, chip * 2 + core, tensor),
            )
            copy.start()
            sends.append(copy)

    q_width, k_width = wq_far.shape[1], wk_far.shape[1]
    key_first, value_first = 2 * q_width, 2 * q_width + 2 * k_width
    fetches = []
    for i, (far, first) in enumerate(((wq_far, 0), (wk_far, key_first), (wv_far, value_first))):
        width = far.shape[1]
        for part in range(2):
            fetches.append(
                pltpu.make_async_copy(
                    far.at[pl.ds(part * half, half), :],
                    sent.at[:, pl.ds(first + part * width, width)],
                    weight_sem.at[i, part],
                )
            )
            fetches[-1].start()
    early.step(4)

    def back(raw, gain, gradient):
        turned_back = gradient * cosine[...] - pltpu.roll(gradient, hd // 2, 1) * sine[...]
        inverse = inverse_rms(raw)
        scaled = turned_back * gain
        raw_grad = inverse * scaled - raw * (inverse * inverse * inverse) * jnp.mean(
            scaled * raw, axis=-1, keepdims=True
        )
        return raw_grad, jnp.sum(turned_back * raw * inverse, axis=0, keepdims=True)

    gains_sent[0] = jnp.zeros_like(gains_sent[0])
    query_gain_row = query_gain[...].astype(jnp.float32)
    key_gain_row = key_gain[...].astype(jnp.float32)

    def query_head(j):
        gradient = query_turned[j].T * (1.0 / math.sqrt(hd))
        for g in range(2):
            here = at_tile(2 * j + g, hd)
            raw_grad, part = back(
                query_raw[:, here], query_gain_row, gradient[g * rows : (g + 1) * rows]
            )
            query_low[:, here] = raw_grad.astype(LOW)
            gains_sent[0, 2:3, :hd] += part

    over_tiles(heads, query_head)
    for copy in sends:
        copy.wait()

    def key_head(j):
        key_sum = near_grad[3, 0, j].astype(jnp.float32)
        value_sum = near_grad[3, 1, j].astype(jnp.float32)
        for i in range(3):
            key_sum = key_sum + far_grad[i, 0, j].astype(jnp.float32)
            value_sum = value_sum + far_grad[i, 1, j].astype(jnp.float32)
        here = at_tile(j, hd)
        raw_grad, part = back(key_raw[:, here], key_gain_row, key_sum)
        key_low[:, here] = raw_grad.astype(LOW)
        value_low[:, here] = value_sum.astype(LOW)
        gains_sent[0, 3:4, :hd] += part

    over_tiles(heads, key_head)
    for fetch in fetches:
        fetch.wait()
    x = tokens[...].astype(jnp.float32)
    inverse = inverse_rms(x)

    def partial_tile(part):
        def tile(i):
            here = at_tile(i, WIDE)

            def weight(first, width):
                return sent[here, pl.ds(first + part * width, width)]

            result = (
                times_turned(query_low[...], weight(0, q_width))
                + times_turned(key_low[...], weight(key_first, k_width))
                + times_turned(value_low[...], weight(value_first, k_width))
            )
            there = pl.ds(pl.multiple_of(part * half + i * WIDE, WIDE), WIDE)
            partial[:, there] = result.astype(LOW)
            across_x = tokens[:, there].astype(jnp.float32) * inverse
            gains_sent[0, 0:1, there] = jnp.sum(result * across_x, axis=0, keepdims=True)

        return tile

    for part in range(2):
        over_tiles(half // WIDE, partial_tile(part))
    outward_partial = remote(partial, partial_other, pair_send.at[1], pair_recv.at[1], pair)
    outward_partial.start()
    gains_sent[0, 1:2, :] = 0.5 * mlp_gain_grad[...]
    gain_dims = ("core",) + DIMS + ("tensor",)

    def send_gains(step):
        copy = remote(
            gains_sent.at[step], gains_landed.at[step], gains_send.at[step], gains_recv.at[step],
            partners[gain_dims[step]],
        )
        copy.start()
        return copy

    def next_gains(step, copy):
        copy.wait()
        total = gains_sent[step] + gains_landed[step]
        if step == len(gain_dims) - 1:
            gains[...] = total
            return None
        gains_sent[step + 1] = total
        return send_gains(step + 1)

    gains_copy = send_gains(0)
    early.step(5, early_out)
    late = Scatter(
        late_streams, [normed] * 3, [query_low, key_low, value_low],
        turned, early_landed[0], early_landed[0], 2 * features, late_landed, late_send, late_recv,
        bits, partners,
    )
    late.turn()
    late.open()
    for step in range(6):
        late.step(step, late_out)
        gains_copy = next_gains(step, gains_copy)
    next_gains(6, gains_copy)
    outward.wait()
    outward_partial.wait()


def backward(f, tokens, cotangent, positions, segments, query_gain, key_gain, weights):
    rows, features = tokens.shape
    heads, hd = f["kv"].shape[2], f["kv"].shape[4]
    q_width, k_width = weights[0].shape[1], weights[1].shape[1]
    hidden = f["gate_grad"].shape[1]
    early_streams = split_streams((hidden, hidden, hidden, q_width), EARLY_TILES)
    late_streams = split_streams((q_width, k_width, k_width), LATE_TILES)
    early_width = 3 * hidden + q_width
    late_width = q_width + 2 * k_width
    half = features // 2
    vmem = pl.BlockSpec(memory_space=pltpu.VMEM)
    far = pl.BlockSpec(memory_space=pl.ANY)
    f32 = jnp.float32
    outs = [
        jax.ShapeDtypeStruct((CHUNK, early_width), f32),
        jax.ShapeDtypeStruct((CHUNK, late_width), f32),
        jax.ShapeDtypeStruct((rows, features), LOW),
        jax.ShapeDtypeStruct((rows, features), LOW),
        jax.ShapeDtypeStruct((rows, features), LOW),
        jax.ShapeDtypeStruct((8, features), f32),
    ]
    kept = [
        f[name]
        for name in (
            "normed", "normed_mlp", "middle_low", "gate_grad", "up_grad", "activated", "attended",
            "query", "kv", "meta", "attended_grad", "inner", "query_raw", "key_raw", "cosine",
            "sine", "mlp_out", "mlp_gain_grad",
        )
    ]
    dma = pltpu.SemaphoreType.DMA
    return pl.pallas_call(
        functools.partial(backward_kernel, early_streams, late_streams),
        out_shape=outs,
        in_specs=[vmem] * 6 + [far] * 3 + [vmem] * len(kept),
        out_specs=[vmem] * len(outs),
        scratch_shapes=[
            pltpu.VMEM((7, features, rows), LOW),
            pltpu.VMEM((half, early_width), LOW),
            pltpu.VMEM((half, early_width), LOW),
            pltpu.VMEM((rows, 2 * rows), f32),
            pltpu.VMEM((heads, hd, 2 * rows), f32),
            pltpu.VMEM((4, 2, heads, rows, hd), LOW),
            pltpu.VMEM((4, 2, heads, rows, hd), LOW),
            pltpu.VMEM((4, 2, heads, rows, hd), LOW),
            pltpu.VMEM((3, 2, heads, rows, hd), LOW),
            pltpu.VMEM((rows, q_width), LOW),
            pltpu.VMEM((rows, k_width), LOW),
            pltpu.VMEM((rows, k_width), LOW),
            pltpu.VMEM((7, 8, features), f32),
            pltpu.VMEM((7, 8, features), f32),
        ]
        + [pltpu.VMEM((half >> step, early_width), LOW) for step in range(6)]
        + [pltpu.VMEM((half >> step, late_width), LOW) for step in range(6)]
        + [
            dma((5, 6)), dma((5, 6)), dma((5, 6)), dma((5, 6)), dma((2,)), dma((2,)), dma((4,)),
            dma((4,)), dma((3,)), dma((3,)), dma((7,)), dma((7,)), dma((3, 2)),
        ],
        compiler_params=pltpu.CompilerParams(
            collective_id=0, has_side_effects=True, vmem_limit_bytes=62 * 1024 * 1024
        ),
    )(tokens, cotangent, positions, segments, query_gain, key_gain, *weights, *kept)


def finish_kernel(
    tokens, attention_gain, middle, mlp_out, mlp_other, grad_middle, partial, partial_other, early,
    late, gains, output, input_grad, grad_query, grad_key, grad_value, grad_out, grad_gate,
    grad_up, grad_down, gains_out,
):
    hidden, q_width, k_width = grad_gate.shape[1], grad_query.shape[1], grad_key.shape[1]
    output[...] = (
        middle[...] + (mlp_out[...].astype(jnp.float32) + mlp_other[...].astype(jnp.float32))
    ).astype(LOW)
    x = tokens[...].astype(jnp.float32)
    inverse = inverse_rms(x)
    scaled = (
        partial[...].astype(jnp.float32) + partial_other[...].astype(jnp.float32)
    ) * attention_gain[...].astype(jnp.float32)
    input_grad[...] = (
        grad_middle[...]
        + inverse * scaled
        - x * (inverse * inverse * inverse) * jnp.mean(scaled * x, axis=-1, keepdims=True)
    ).astype(LOW)
    grad_gate[...] = early[:, :hidden]
    grad_up[...] = early[:, hidden : 2 * hidden]
    grad_down[...] = early[:, 2 * hidden : 3 * hidden].T
    grad_out[...] = early[:, 3 * hidden :].T
    grad_query[...] = late[:, :q_width]
    grad_key[...] = late[:, q_width : q_width + k_width]
    grad_value[...] = late[:, q_width + k_width :]
    chunk = lax.axis_index("dp") * 8 + lax.axis_index("seq")
    features = gains.shape[1]
    wide = pltpu.roll(gains[0:8, :], lax.rem(features - chunk * CHUNK, features), 1)
    thin = pltpu.roll(gains[0:8, :128], lax.rem(128 - chunk * 2, 128), 1)
    gains_out[0:2, :] = wide[0:2, :128]
    gains_out[2:4, :] = thin[2:4, :]


def finish(tokens, attention_gain, f, mlp_other, partial, partial_other, early, late, gains, widths):
    q_width, k_width, hidden = widths
    rows, features = tokens.shape
    f32 = jnp.float32
    vmem = pl.BlockSpec(memory_space=pltpu.VMEM)
    shapes = (
        ((rows, features), LOW), ((rows, features), LOW), ((CHUNK, q_width), f32),
        ((CHUNK, k_width), f32), ((CHUNK, k_width), f32), ((q_width, CHUNK), f32),
        ((CHUNK, hidden), f32), ((CHUNK, hidden), f32), ((hidden, CHUNK), f32), ((8, 128), f32),
    )
    return pl.pallas_call(
        finish_kernel,
        out_shape=[jax.ShapeDtypeStruct(shape, kind) for shape, kind in shapes],
        in_specs=[vmem] * 11,
        out_specs=[vmem] * len(shapes),
        compiler_params=pltpu.CompilerParams(vmem_limit_bytes=40 * 1024 * 1024),
    )(
        tokens, attention_gain, f["middle"], f["mlp_out"], mlp_other, f["grad_middle"], partial,
        partial_other, early, late, gains,
    )


def shards(
    tokens,
    cotangent,
    positions,
    segments,
    attention_gain,
    query_weight,
    key_weight,
    value_weight,
    query_gain,
    key_gain,
    out_weight,
    mlp_gain,
    gate_weight,
    up_weight,
    down_weight,
):
    f = forward(
        tokens[0], cotangent[0], positions, segments, attention_gain[None], query_weight,
        key_weight, value_weight, query_gain[None], key_gain[None], out_weight, mlp_gain[None],
        gate_weight, up_weight, down_weight,
    )
    early, late, mlp_other, partial, partial_other, gains = backward(
        f, tokens[0], cotangent[0], positions, segments, query_gain[None], key_gain[None],
        (query_weight, key_weight, value_weight),
    )
    results = finish(
        tokens[0], attention_gain[None], f, mlp_other, partial, partial_other, early, late, gains,
        (query_weight.shape[1], key_weight.shape[1], gate_weight.shape[1]),
    )
    gains = results[-1]
    return (
        results[0][None],
        results[1][None],
        *results[2:-1],
        gains[0, :CHUNK],
        gains[1, :CHUNK],
        gains[2, :2],
        gains[3, :2],
    )


def solution(mesh):
    return jax.shard_map(
        shards,
        mesh=mesh,
        in_specs=(
            P("dp", "seq", None),
            P("dp", "seq", None),
            P("dp", "seq"),
            P("dp", "seq"),
            P(),
            P(None, "tensor"),
            P(None, "tensor"),
            P(None, "tensor"),
            P(),
            P(),
            P("tensor", None),
            P(),
            P(None, "tensor"),
            P(None, "tensor"),
            P("tensor", None),
        ),
        out_specs=(
            P("dp", "seq", None),
            P("dp", "seq", None),
            P(("dp", "seq"), "tensor"),
            P(("dp", "seq"), "tensor"),
            P(("dp", "seq"), "tensor"),
            P("tensor", ("dp", "seq")),
            P(("dp", "seq"), "tensor"),
            P(("dp", "seq"), "tensor"),
            P("tensor", ("dp", "seq")),
            P(("dp", "seq")),
            P(("dp", "seq")),
            P(("dp", "seq")),
            P(("dp", "seq")),
        ),
        check_vma=False,
    )
```

```python
import functools
import math

import jax
import jax.numpy as jnp
from jax import lax
from jax.experimental import pallas as pl
from jax.experimental.pallas import tpu as pltpu
from jax.sharding import PartitionSpec as P

EPS = 1e-06
ROPE_BASE = 1000000.0
NEGATIVE = -1e30


MESH = pl.DeviceIdType.MESH
CHUNK = 16
DIMS = ("x3", "x1", "y3", "y1", "z")
LOW = jnp.bfloat16


def place():
    dp = lax.axis_index("dp")
    seq = lax.axis_index("seq")
    tensor = lax.axis_index("tensor")
    x, z = dp // 2, dp % 2
    y, core = seq // 2, seq % 2
    x_near = x + 1 - 2 * (x % 2)
    y_near = y + 1 - 2 * (y % 2)
    bits = {
        "core": core,
        "x3": x // 2,
        "x1": (x // 2 + x % 2) % 2,
        "y3": y // 2,
        "y1": (y // 2 + y % 2) % 2,
        "z": z,
    }
    partners = {
        "core": (dp, seq + 1 - 2 * core, tensor),
        "x3": ((3 - x) * 2 + z, seq, tensor),
        "x1": (x_near * 2 + z, seq, tensor),
        "y3": (dp, (3 - y) * 2 + core, tensor),
        "y1": (dp, y_near * 2 + core, tensor),
        "z": (dp + 1 - 2 * z, seq, tensor),
        "tensor": (dp, seq, 1 - tensor),
    }
    return bits, partners


def greet(partners):
    barrier = pltpu.get_barrier_semaphore()
    for partner in partners:
        pl.semaphore_signal(barrier, inc=1, device_id=partner, device_id_type=MESH)
    pl.semaphore_wait(barrier, len(partners))


ORDERS = (
    ("core", "x3", "x1", "z", "y3", "y1"),
    ("core", "x1", "x3", "z", "y1", "y3"),
    ("core", "y3", "z", "x1", "x3", "y1"),
    ("core", "y1", "z", "x3", "x1", "y3"),
    ("core", "z", "x1", "x3", "y3", "y1"),
)


def slot_chunks(order):
    chunks = []
    for slot in range(2 ** len(order)):
        bit = {d: (slot >> (len(order) - 1 - i)) & 1 for i, d in enumerate(order)}
        x = 2 * bit["x3"] + (bit["x3"] ^ bit["x1"])
        y = 2 * bit["y3"] + (bit["y3"] ^ bit["y1"])
        chunks.append(((x * 2 + bit["z"]) * 4 + y) * 2 + bit["core"])
    return chunks


def remote(source, target, out_sem, in_sem, partner):
    return pltpu.make_async_remote_copy(
        src_ref=source,
        dst_ref=target,
        send_sem=out_sem,
        recv_sem=in_sem,
        device_id=partner,
        device_id_type=MESH,
    )


def over_tiles(count, body):
    def step(i, _):
        body(i)
        return 0

    lax.fori_loop(0, count, step, 0)


def at_tile(i, size):
    return pl.ds(pl.multiple_of(i * size, size), size)


def times(left, right):
    return jnp.dot(left, right, preferred_element_type=jnp.float32)


def times_turned(left, right):
    return lax.dot_general(
        left, right, (((1,), (1,)), ((), ())), preferred_element_type=jnp.float32
    )


def inverse_rms(entries):
    return lax.rsqrt(jnp.mean(entries * entries, axis=-1, keepdims=True) + EPS)


EARLY_TILES = (6, 6, 4, 2, 4)
LATE_TILES = (2, 2, 2, 1, 1)
SHIFTS = (2, 1, 3, 0)
WIDE = 256


def split_streams(sizes, tiles):
    bounds, start = [], 0
    for size in sizes:
        bounds.append((start, start + size))
        start += size
    streams, first = [], 0
    for count in tiles:
        last = first + count * WIDE
        pieces = []
        for matrix, (low, high) in enumerate(bounds):
            begin, end = max(first, low), min(last, high)
            if begin < end:
                pieces.append((matrix, begin - low, begin, end - begin))
        streams.append((first, last - first, pieces))
        first = last
    assert first == start
    return streams


class Panels:
    def __init__(self, rows, panels):
        self.rows = rows
        self.panels = panels

    def find(self, first):
        start = 0
        for ref, row, columns in self.panels:
            if first < start + columns:
                return ref, row, first - start
            start += columns
        raise ValueError


class Scatter:
    def __init__(self, streams, lhs, rhs, turned, sent, held, landed, send_sem, recv_sem, bits, partners):
        self.streams, self.lhs, self.rhs = streams, lhs, rhs
        self.turned, self.sent, self.held = turned, sent, held
        self.landed, self.send_sem, self.recv_sem = landed, send_sem, recv_sem
        self.bits, self.partners = bits, partners
        self.half = sent.rows
        self.copies = {}
        self.base = [0] * len(streams)

    def open(self, s):
        first, columns, pieces = self.streams[s]
        core = self.bits["core"]
        chunks = slot_chunks(ORDERS[s])
        for kept in (False, True):
            ref, row, column = (self.held if kept else self.sent).find(first)
            offset = core * self.half if kept else (1 - core) * self.half
            for index, (matrix, left_column, begin, width) in enumerate(pieces):
                if not kept:
                    flipped = self.lhs[matrix][...].T
                    for slot, chunk in enumerate(chunks):
                        self.turned[index, slot * CHUNK : (slot + 1) * CHUNK, :] = flipped[
                            chunk * CHUNK : (chunk + 1) * CHUNK, :
                        ]
                target = column + begin - first
                right = self.rhs[matrix]

                def tile(i, index=index, right=right, left_column=left_column, target=target):
                    here = pl.multiple_of(i * WIDE, WIDE)
                    ref[row : row + self.half, pl.ds(target + here, WIDE)] = times(
                        self.turned[index, pl.ds(pl.multiple_of(offset, CHUNK), self.half), :],
                        right[:, pl.ds(left_column + here, WIDE)],
                    ).astype(LOW)

                over_tiles(width // WIDE, tile)
            if not kept:
                self.send(
                    0, s, ref.at[pl.ds(row, self.half), pl.ds(column, columns)]
                )

    def send(self, step, s, source):
        first, columns, _ = self.streams[s]
        ref, column = self.landed[step]
        copy = remote(
            source,
            ref.at[:, pl.ds(column + first, columns)],
            self.send_sem.at[s, step],
            self.recv_sem.at[s, step],
            self.partners[ORDERS[s][step]],
        )
        copy.start()
        self.copies[s, step] = copy

    def step(self, step, out=None, streams=range(5)):
        rows = self.half >> step
        for s in streams:
            first, columns, _ = self.streams[s]
            self.copies[s, step].wait()
            ref, row, column = self.held.find(first)
            mine = pl.ds(column, columns)
            landed, from_column = self.landed[step]
            theirs = pl.ds(from_column + first, columns)
            if step == 5:
                out[:, pl.ds(first, columns)] = ref[
                    pl.ds(pl.multiple_of(row + self.base[s], CHUNK), CHUNK), mine
                ].astype(jnp.float32) + landed[:, theirs].astype(jnp.float32)
                continue
            tile = min(rows, 64)

            def add(i, s=s, tile=tile, ref=ref, row=row, mine=mine, landed=landed, theirs=theirs):
                start = pl.multiple_of(i * tile, tile)
                here = pl.ds(pl.multiple_of(row + self.base[s] + start, tile), tile)
                ref[here, mine] = ref[here, mine] + landed[pl.ds(start, tile), theirs]

            over_tiles(rows // tile, add)
            bit = self.bits[ORDERS[s][step + 1]]
            away = pl.multiple_of(row + self.base[s] + (1 - bit) * (rows // 2), CHUNK)
            self.send(step + 1, s, ref.at[pl.ds(away, rows // 2), mine])
            self.base[s] = self.base[s] + bit * (rows // 2)


def layer_kernel(early_streams, late_streams, *refs):
    (
        tokens, cotangent, positions, segments, frequencies, attention_gain, query_gain,
        key_gain, mlp_gain, wq_far, wk_far, wv_far, wo_far, wg_far, wu_far, wd_far, middle,
        mlp_out, mlp_other, grad_middle, partial, partial_other, early_out, late_out, gains,
        normed, query_raw, key_raw, query, kv, meta, cosine, sine, attended, normed_mlp,
        activated, gate_grad, up_grad, middle_low, attended_grad, inner, mlp_gain_grad, wq, wk,
        wv, wo, wg, wu, wd, bias, total, weight_sum, act_grad, part_out, part_in, turned, held,
        far_grad, gains_sent, gains_landed, weight_sem, kv_send, kv_recv, meta_send, meta_recv,
        pair_send, pair_recv, early_send, early_recv, late_send, late_recv, core_send,
        core_recv, far_send, far_recv, gains_send, gains_recv,
    ) = refs[: -11]
    early_landed, late_landed = refs[-11:-5], refs[-5:]
    bits, partners = place()
    dp, seq, tensor = lax.axis_index("dp"), lax.axis_index("seq"), lax.axis_index("tensor")
    core, y = seq % 2, seq // 2
    after, before, across = (y + 1) % 4, (y + 3) % 4, (y + 2) % 4
    near = (dp, y * 2 + 1 - core, tensor)
    ahead = (dp, after * 2 + core, tensor)
    behind = (dp, before * 2 + core, tensor)
    pair = (dp, seq, 1 - tensor)
    others = [(dp, (seq + step) % 8, tensor) for step in range(1, 8)]
    rows = tokens.shape[0]
    heads = kv.shape[2]
    hd = kv.shape[4]
    greet(others + [partners[name] for name in ("x3", "x1", "z", "tensor")])
    fetches = [
        pltpu.make_async_copy(far, held, weight_sem.at[i])
        for i, (far, held) in enumerate(
            zip(
                (wk_far, wv_far, wq_far, wo_far, wd_far, wg_far, wu_far),
                (wk, wv, wq, wo, wd, wg, wu),
            )
        )
    ]
    for fetch in fetches:
        fetch.start()
    got_wk, got_wv, got_wq, got_wo, got_wd, got_wg, got_wu = fetches

    meta[seq] = jnp.zeros_like(meta[seq])
    meta[seq, 0:1, :] = positions[...]
    meta[seq, 1:2, :] = segments[...]
    metas = [
        remote(meta.at[seq], meta.at[seq], meta_send.at[i], meta_recv.at[i], other)
        for i, other in enumerate(others)
    ]
    for copy in metas:
        copy.start()

    place_rows = jnp.broadcast_to(positions[...].astype(jnp.float32), (rows, rows)).T
    segment_rows = jnp.broadcast_to(segments[...].astype(jnp.float32), (rows, rows)).T
    angle = place_rows[:, :hd] * frequencies[...]
    cosine[...] = jnp.cos(angle)
    lane = lax.broadcasted_iota(jnp.int32, (rows, hd), 1)
    sine[...] = jnp.where(lane < hd // 2, -1.0, 1.0) * jnp.sin(angle)

    def turn(entries):
        return entries * cosine[...] + pltpu.roll(entries, hd // 2, 1) * sine[...]

    x = tokens[...].astype(jnp.float32)
    normed[...] = (x * inverse_rms(x) * attention_gain[...].astype(jnp.float32)).astype(LOW)

    tile = 2 * hd
    got_wk.wait()

    def key_tile(i):
        raw = times(normed[...], wk[:, at_tile(i, tile)])
        key_raw[:, at_tile(i, tile)] = raw
        for g in range(2):
            head = raw[:, g * hd : (g + 1) * hd]
            scaled = head * inverse_rms(head) * key_gain[...].astype(jnp.float32)
            kv[seq, 0, 2 * i + g] = turn(scaled).astype(LOW)

    over_tiles(heads // 2, key_tile)

    def own(half, kind, target, index):
        copy = remote(
            kv.at[seq, half], kv.at[seq, half], kv_send.at[index], kv_recv.at[kind, half], target
        )
        copy.start()
        return copy

    sends = [own(0, 1, ahead, 0), own(0, 2, behind, 1), own(0, 0, near, 2)]
    got_wv.wait()

    def value_tile(i):
        raw = times(normed[...], wv[:, at_tile(i, tile)]).astype(LOW)
        for g in range(2):
            kv[seq, 1, 2 * i + g] = raw[:, g * hd : (g + 1) * hd]

    over_tiles(heads // 2, value_tile)
    sends += [own(1, 1, ahead, 3), own(1, 2, behind, 4), own(1, 0, near, 5)]
    got_wq.wait()
    scale = math.log2(math.e) / math.sqrt(hd)

    def query_tile(i):
        raw = times(normed[...], wq[:, at_tile(i, tile)])
        query_raw[:, at_tile(i, tile)] = raw
        for g in range(2):
            head = raw[:, g * hd : (g + 1) * hd]
            scaled = head * inverse_rms(head) * (query_gain[...].astype(jnp.float32) * scale)
            query[i, g * rows : (g + 1) * rows, :] = turn(scaled).astype(LOW)

    over_tiles(heads, query_tile)
    total[...] = jnp.zeros_like(total)
    weight_sum[...] = jnp.zeros_like(weight_sum)
    for copy in metas:
        copy.wait()

    def attend(slot):
        key_place = meta[slot, 0:1, :].astype(jnp.float32)
        key_segment = meta[slot, 1:2, :].astype(jnp.float32)
        allowed = (key_place <= place_rows) & (key_segment == segment_rows)
        bias[:, :rows] = jnp.where(allowed, 0.0, NEGATIVE)

        def head(j):
            scores = times_turned(query[j], kv[slot, 0, j])
            weights = jnp.concatenate(
                [jnp.exp2(scores[g * rows : (g + 1) * rows] + bias[:, :rows]) for g in range(2)], axis=0
            )
            weight_sum[j] += weights[:, :hd] + weights[:, hd:]
            total[j] += times(weights.astype(LOW), kv[slot, 1, j])

        over_tiles(heads, head)

    def arrived(slot, kind, half):
        remote(
            kv.at[slot, half], kv.at[slot, half], kv_send.at[0], kv_recv.at[kind, half], near
        ).wait_recv()

    def pass_on(slot, half, kind, target, index):
        copy = remote(
            kv.at[slot, half], kv.at[slot, half], kv_send.at[index], kv_recv.at[kind, half], target
        )
        copy.start()
        sends.append(copy)

    attend(seq)
    near_slot = y * 2 + 1 - core
    arrived(near_slot, 0, 0)
    arrived(near_slot, 0, 1)
    attend(near_slot)
    before_slot, after_slot, across_slot = before * 2 + core, after * 2 + core, across * 2 + core
    arrived(before_slot, 1, 0)
    pass_on(before_slot, 0, 3, ahead, 6)
    pass_on(before_slot, 0, 4, near, 7)
    arrived(after_slot, 2, 0)
    pass_on(after_slot, 0, 5, near, 8)
    arrived(after_slot, 2, 1)
    pass_on(after_slot, 1, 3, behind, 9)
    pass_on(after_slot, 1, 5, near, 10)
    arrived(before_slot, 1, 1)
    pass_on(before_slot, 1, 4, near, 11)
    attend(before_slot)
    attend(after_slot)
    for far_y, kind in ((before, 4), (after, 5)):
        slot = far_y * 2 + 1 - core
        arrived(slot, kind, 0)
        arrived(slot, kind, 1)
        attend(slot)
    arrived(across_slot, 3, 0)
    pass_on(across_slot, 0, 6, near, 12)
    arrived(across_slot, 3, 1)
    pass_on(across_slot, 1, 6, near, 13)
    attend(across_slot)
    far_slot = across * 2 + 1 - core
    arrived(far_slot, 6, 0)
    arrived(far_slot, 6, 1)
    attend(far_slot)

    def finish(j):
        inverse = 1.0 / jnp.sum(weight_sum[j], axis=-1, keepdims=True)
        result = total[j] * inverse
        total[j] = result
        weight_sum[j] = jnp.broadcast_to(inverse, result.shape)
        for g in range(2):
            attended[:, at_tile(2 * j + g, hd)] = result[g * rows : (g + 1) * rows].astype(LOW)

    over_tiles(heads, finish)
    got_wo.wait()
    wide = 256
    features = tokens.shape[1]
    hidden = wg.shape[1]

    def out_tile(i):
        part_out[0, :, at_tile(i, wide)] = times(attended[...], wo[:, at_tile(i, wide)]).astype(LOW)

    over_tiles(features // wide, out_tile)
    first = remote(part_out.at[0], part_in.at[0], pair_send.at[0], pair_recv.at[0], pair)
    first.start()
    got_wd.wait()

    def act_grad_tile(i):
        act_grad[:, at_tile(i, wide)] = times_turned(cotangent[...], wd[at_tile(i, wide), :])

    over_tiles(hidden // wide, act_grad_tile)
    got_wg.wait()
    got_wu.wait()
    first.wait()
    mid = (
        tokens[...].astype(jnp.float32)
        + (part_out[0].astype(jnp.float32) + part_in[0].astype(jnp.float32))
    )
    middle[...] = mid
    normed_mlp[...] = (mid * inverse_rms(mid) * mlp_gain[...].astype(jnp.float32)).astype(LOW)

    def hidden_tile(i):
        here = at_tile(i, wide)
        gate_here = times(normed_mlp[...], wg[:, here])
        up_here = times(normed_mlp[...], wu[:, here])
        sigmoid = 1.0 / (1.0 + jnp.exp(-gate_here))
        silu = gate_here * sigmoid
        grad = act_grad[:, here]
        activated[:, here] = (silu * up_here).astype(LOW)
        gate_grad[:, here] = (
            grad * up_here * sigmoid * (1.0 + gate_here * (1.0 - sigmoid))
        ).astype(LOW)
        up_grad[:, here] = (grad * silu).astype(LOW)

    over_tiles(hidden // wide, hidden_tile)

    def back_tile(i):
        here = at_tile(i, wide)
        part_out[1, :, here] = (
            times_turned(gate_grad[...], wg[here, :]) + times_turned(up_grad[...], wu[here, :])
        ).astype(LOW)

    over_tiles(features // wide, back_tile)
    second = remote(part_out.at[1], part_in.at[1], pair_send.at[1], pair_recv.at[1], pair)
    second.start()

    def down_tile(i):
        mlp_out[:, at_tile(i, wide)] = times(activated[...], wd[:, at_tile(i, wide)]).astype(LOW)

    over_tiles(features // wide, down_tile)
    half = features // 2
    early = Scatter(
        early_streams, [normed_mlp, normed_mlp, cotangent, middle_low],
        [gate_grad, up_grad, activated, attended], turned,
        Panels(half, [(wg, 0, hidden), (wg, half, hidden), (wu, 0, hidden), (wu, half, hidden)]),
        Panels(half, [(held, 0, held.shape[1])]), [(ref, 0) for ref in early_landed],
        early_send, early_recv, bits, partners,
    )
    for s in range(4):
        early.open(s)
    early.step(0, streams=range(4))
    for copy in sends:
        copy.wait_send()
    second.wait()
    outward = remote(mlp_out, mlp_other, pair_send.at[2], pair_recv.at[2], pair)
    outward.start()
    mid = middle[...]
    inverse = inverse_rms(mid)
    dy = part_out[1].astype(jnp.float32) + part_in[1].astype(jnp.float32)
    mlp_gain_grad[...] = jnp.sum(dy * mid * inverse, axis=0, keepdims=True)
    scaled = dy * mlp_gain[...].astype(jnp.float32)
    grad = (
        cotangent[...].astype(jnp.float32)
        + inverse * scaled
        - mid * (inverse * inverse * inverse) * jnp.mean(scaled * mid, axis=-1, keepdims=True)
    )
    grad_middle[...] = grad
    middle_low[...] = grad.astype(LOW)

    def attended_grad_tile(j):
        both = times_turned(middle_low[...], wo[at_tile(j, 2 * hd), :]).astype(LOW)
        both = both.astype(jnp.float32)
        for g in range(2):
            here = slice(g * rows, (g + 1) * rows)
            normal = both[:, g * hd : (g + 1) * hd] * weight_sum[j, here, :]
            attended_grad[j, here, :] = normal.astype(LOW)
            summed = jnp.sum((normal * total[j, here, :]).T, axis=0, keepdims=True)
            inner[j, :, here] = jnp.broadcast_to(summed, (8, rows))

    over_tiles(heads, attended_grad_tile)


    early.open(4)
    place_row = positions[...].astype(jnp.float32)
    segment_row = segments[...].astype(jnp.float32)
    act_grad[...] = jnp.zeros_like(act_grad)

    def query_turned(j):
        return pl.ds(pl.multiple_of(j % 2 * hd, hd), hd), at_tile(j // 2, 2 * rows)

    def block(slot, target, first):
        def column(row):
            return jnp.broadcast_to(row.astype(jnp.float32), (rows, rows)).T

        allowed = (column(meta[slot, 0:1, :]) <= place_row) & (
            column(meta[slot, 1:2, :]) == segment_row
        )
        one = jnp.where(allowed, 0.0, NEGATIVE)
        bias[:, :rows] = one
        bias[:, rows:] = one

        def head(j):
            key, value = kv[slot, 0, j], kv[slot, 1, j]
            weight = jnp.exp2(times_turned(key, query[j]) + bias[...])
            grad = times_turned(value, attended_grad[j])
            scores_grad = (weight * (grad - inner[j, 0:1, :])).astype(LOW)
            down = pl.ds(first, rows)
            target[down, at_tile(heads + j, hd)] = times(
                weight.astype(LOW), attended_grad[j]
            ).astype(LOW)
            target[down, at_tile(j, hd)] = (times(scores_grad, query[j]) * math.log(2)).astype(LOW)
            act_grad[query_turned(j)] += lax.dot_general(
                key, scores_grad, (((0,), (0,)), ((), ())), preferred_element_type=jnp.float32
            )

        over_tiles(heads, head)

    grad_width = 2 * heads * hd
    far_sends, crossing = [], []

    def grad_rows(ref, i):
        return ref.at[pl.ds(i * rows, rows), pl.ds(0, grad_width)]

    for i, shift in enumerate(SHIFTS):
        chip = (y + shift) % 4
        block(chip * 2 + 1 - core, wg, i * rows)
        copy = remote(
            grad_rows(wg, i), grad_rows(wd, i), core_send.at[i], core_recv.at[i], partners["core"]
        )
        copy.start()
        block(chip * 2 + core, wu, i * rows)
        copy.wait()
        down, wide_grad = slice(i * rows, (i + 1) * rows), slice(0, grad_width)
        wu[down, wide_grad] = wu[down, wide_grad] + wd[down, wide_grad]
        if shift:
            copy = remote(
                grad_rows(wu, i),
                far_grad.at[i],
                far_send.at[i],
                far_recv.at[i],
                (dp, chip * 2 + core, tensor),
            )
            copy.start()
            far_sends.append(copy)
        if i == 0:
            early.step(0, streams=range(4, 5))
    early.step(1)

    def back(raw, gain, gradient):
        turned_back = gradient * cosine[...] - pltpu.roll(gradient, hd // 2, 1) * sine[...]
        inverse = inverse_rms(raw)
        scaled = turned_back * gain
        raw_grad = inverse * scaled - raw * (inverse * inverse * inverse) * jnp.mean(
            scaled * raw, axis=-1, keepdims=True
        )
        return raw_grad, jnp.sum(turned_back * raw * inverse, axis=0, keepdims=True)

    gains_sent[0] = jnp.zeros_like(gains_sent[0])
    query_gain_row = query_gain[...].astype(jnp.float32)
    key_gain_row = key_gain[...].astype(jnp.float32)

    def query_head(j):
        gradient = act_grad[query_turned(j)].T * (1.0 / math.sqrt(hd))
        for g in range(2):
            here = at_tile(2 * j + g, hd)
            raw_grad, part = back(
                query_raw[:, here], query_gain_row, gradient[g * rows : (g + 1) * rows]
            )
            attended[:, here] = raw_grad.astype(LOW)
            gains_sent[0, 2:3, :hd] += part

    over_tiles(heads, query_head)
    early.step(2)
    for copy in far_sends:
        copy.wait()

    def key_head(j):
        here, there = at_tile(j, hd), at_tile(heads + j, hd)
        key_sum = wu[3 * rows : 4 * rows, here].astype(jnp.float32)
        value_sum = wu[3 * rows : 4 * rows, there].astype(jnp.float32)
        for i in range(3):
            key_sum = key_sum + far_grad[i, :, here].astype(jnp.float32)
            value_sum = value_sum + far_grad[i, :, there].astype(jnp.float32)
        raw_grad, part = back(key_raw[:, here], key_gain_row, key_sum)
        gate_grad[:, here] = raw_grad.astype(LOW)
        up_grad[:, here] = value_sum.astype(LOW)
        gains_sent[0, 3:4, :hd] += part

    over_tiles(heads, key_head)
    x = tokens[...].astype(jnp.float32)
    inverse = inverse_rms(x)
    k_width = wk.shape[1]

    def partial_tile(i):
        here = at_tile(i, WIDE)
        result = (
            times_turned(attended[...], wq[here, :])
            + times_turned(gate_grad[:, :k_width], wk[here, :])
            + times_turned(up_grad[:, :k_width], wv[here, :])
        )
        partial[:, here] = result.astype(LOW)
        gains_sent[0, 0:1, here] = jnp.sum(
            result * (tokens[:, here].astype(jnp.float32) * inverse), axis=0, keepdims=True
        )

    over_tiles(features // WIDE, partial_tile)
    outward_partial = remote(partial, partial_other, pair_send.at[3], pair_recv.at[3], pair)
    outward_partial.start()
    gains_sent[0, 1:2, :] = 0.5 * mlp_gain_grad[...]
    gain_dims = ("tensor", "core") + DIMS

    def send_gains(step):
        copy = remote(
            gains_sent.at[step], gains_landed.at[step], gains_send.at[step], gains_recv.at[step],
            partners[gain_dims[step]],
        )
        copy.start()
        return copy

    def next_gains(step, copy):
        copy.wait()
        total = gains_sent[step] + gains_landed[step]
        if step == len(gain_dims) - 1:
            gains[...] = total
            return None
        gains_sent[step + 1] = total
        return send_gains(step + 1)

    early.step(3)
    gains_copy = send_gains(0)
    late = Scatter(
        late_streams, [normed] * 3, [attended, gate_grad, up_grad], turned,
        Panels(half, [(wg, 0, hidden), (wg, half, hidden)]),
        Panels(half, [(wu, 0, hidden), (wu, half, hidden)]),
        [(early_landed[0], 0)] + [(ref, 0) for ref in late_landed],
        late_send, late_recv, bits, partners,
    )
    for s in range(5):
        late.open(s)
    early.step(4)
    gains_copy = next_gains(0, gains_copy)
    for step in range(6):
        if step == 1:
            early.step(5, early_out)
        late.step(step, late_out)
        gains_copy = next_gains(step + 1, gains_copy)
    outward.wait()
    outward_partial.wait()


def layer(
    tokens, cotangent, positions, segments, attention_gain, query_weight, key_weight, value_weight,
    query_gain, key_gain, out_weight, mlp_gain, gate_weight, up_weight, down_weight,
):
    rows, features = tokens.shape
    hd = query_gain.shape[1]
    heads = key_weight.shape[1] // hd
    half = features // 2
    q_width, k_width, hidden = query_weight.shape[1], key_weight.shape[1], gate_weight.shape[1]
    early_streams = split_streams((hidden, hidden, hidden, q_width), EARLY_TILES)
    late_streams = split_streams((q_width, k_width, k_width), LATE_TILES)
    early_width = 3 * hidden + q_width
    late_width = q_width + 2 * k_width
    pairs = jnp.arange(hd // 2, dtype=jnp.float32)
    inverse = 1.0 / ROPE_BASE ** (pairs * 2.0 / hd)
    frequencies = jnp.concatenate([inverse, inverse])[None]
    vmem = pl.BlockSpec(memory_space=pltpu.VMEM)
    far = pl.BlockSpec(memory_space=pl.ANY)
    f32 = jnp.float32
    outs = dict(
        middle=((rows, features), f32),
        mlp_out=((rows, features), LOW),
        mlp_other=((rows, features), LOW),
        grad_middle=((rows, features), f32),
        partial=((rows, features), LOW),
        partial_other=((rows, features), LOW),
        early=((CHUNK, early_width), f32),
        late=((CHUNK, late_width), f32),
        gains=((8, features), f32),
    )
    results = pl.pallas_call(
        functools.partial(layer_kernel, early_streams, late_streams),
        out_shape=[jax.ShapeDtypeStruct(shape, kind) for shape, kind in outs.values()],
        in_specs=[vmem] * 9 + [far] * 7,
        out_specs=[vmem] * len(outs),
        scratch_shapes=[
            pltpu.VMEM((rows, features), LOW),
            pltpu.VMEM((rows, q_width), f32),
            pltpu.VMEM((rows, k_width), f32),
            pltpu.VMEM((heads, 2 * rows, hd), LOW),
            pltpu.VMEM((8, 2, heads, rows, hd), LOW),
            pltpu.VMEM((8, 8, rows), jnp.int32),
            pltpu.VMEM((rows, hd), f32),
            pltpu.VMEM((rows, hd), f32),
            pltpu.VMEM((rows, q_width), LOW),
            pltpu.VMEM((rows, features), LOW),
            pltpu.VMEM((rows, hidden), LOW),
            pltpu.VMEM((rows, hidden), LOW),
            pltpu.VMEM((rows, hidden), LOW),
            pltpu.VMEM((rows, features), LOW),
            pltpu.VMEM((heads, 2 * rows, hd), LOW),
            pltpu.VMEM((heads, 8, 2 * rows), f32),
            pltpu.VMEM((1, features), f32),
            pltpu.VMEM(query_weight.shape, LOW),
            pltpu.VMEM(key_weight.shape, LOW),
            pltpu.VMEM(value_weight.shape, LOW),
            pltpu.VMEM(out_weight.shape, LOW),
            pltpu.VMEM(gate_weight.shape, LOW),
            pltpu.VMEM(up_weight.shape, LOW),
            pltpu.VMEM(down_weight.shape, LOW),
            pltpu.VMEM((rows, 2 * rows), f32),
            pltpu.VMEM((heads, 2 * rows, hd), f32),
            pltpu.VMEM((heads, 2 * rows, hd), f32),
            pltpu.VMEM((rows, hidden), f32),
            pltpu.VMEM((2, rows, features), LOW),
            pltpu.VMEM((2, rows, features), LOW),
            pltpu.VMEM((1, features, rows), LOW),
            pltpu.VMEM((half, early_width), LOW),
            pltpu.VMEM((3, rows, 2 * k_width), LOW),
            pltpu.VMEM((7, 8, features), f32),
            pltpu.VMEM((7, 8, features), f32),
            pltpu.SemaphoreType.DMA((7,)),
            pltpu.SemaphoreType.DMA((14,)),
            pltpu.SemaphoreType.DMA((7, 2)),
            pltpu.SemaphoreType.DMA((7,)),
            pltpu.SemaphoreType.DMA((7,)),
            pltpu.SemaphoreType.DMA((4,)),
            pltpu.SemaphoreType.DMA((4,)),
            pltpu.SemaphoreType.DMA((5, 6)),
            pltpu.SemaphoreType.DMA((5, 6)),
            pltpu.SemaphoreType.DMA((5, 6)),
            pltpu.SemaphoreType.DMA((5, 6)),
            pltpu.SemaphoreType.DMA((4,)),
            pltpu.SemaphoreType.DMA((4,)),
            pltpu.SemaphoreType.DMA((3,)),
            pltpu.SemaphoreType.DMA((3,)),
            pltpu.SemaphoreType.DMA((7,)),
            pltpu.SemaphoreType.DMA((7,)),
        ]
        + [pltpu.VMEM((half >> step, early_width), LOW) for step in range(6)]
        + [pltpu.VMEM((half >> step, late_width), LOW) for step in range(1, 6)],
        compiler_params=pltpu.CompilerParams(
            collective_id=0, has_side_effects=True, vmem_limit_bytes=63 * 1024 * 1024
        ),
    )(
        tokens, cotangent, positions, segments, frequencies, attention_gain, query_gain, key_gain,
        mlp_gain, query_weight, key_weight, value_weight, out_weight, gate_weight, up_weight,
        down_weight,
    )
    return dict(zip(outs, results))


def finish_kernel(
    tokens, attention_gain, middle, mlp_out, mlp_other, grad_middle, partial, partial_other, early,
    late, gains, output, input_grad, grad_query, grad_key, grad_value, grad_out, grad_gate,
    grad_up, grad_down, gains_out,
):
    hidden, q_width, k_width = grad_gate.shape[1], grad_query.shape[1], grad_key.shape[1]
    output[...] = (
        middle[...] + (mlp_out[...].astype(jnp.float32) + mlp_other[...].astype(jnp.float32))
    ).astype(LOW)
    x = tokens[...].astype(jnp.float32)
    inverse = inverse_rms(x)
    scaled = (
        partial[...].astype(jnp.float32) + partial_other[...].astype(jnp.float32)
    ) * attention_gain[...].astype(jnp.float32)
    input_grad[...] = (
        grad_middle[...]
        + inverse * scaled
        - x * (inverse * inverse * inverse) * jnp.mean(scaled * x, axis=-1, keepdims=True)
    ).astype(LOW)
    grad_gate[...] = early[:, :hidden]
    grad_up[...] = early[:, hidden : 2 * hidden]
    grad_down[...] = early[:, 2 * hidden : 3 * hidden].T
    grad_out[...] = early[:, 3 * hidden :].T
    grad_query[...] = late[:, :q_width]
    grad_key[...] = late[:, q_width : q_width + k_width]
    grad_value[...] = late[:, q_width + k_width :]
    chunk = lax.axis_index("dp") * 8 + lax.axis_index("seq")
    features = gains.shape[1]
    wide = pltpu.roll(gains[0:8, :], lax.rem(features - chunk * CHUNK, features), 1)
    thin = pltpu.roll(gains[0:8, :128], lax.rem(128 - chunk * 2, 128), 1)
    gains_out[0:2, :] = wide[0:2, :128]
    gains_out[2:4, :] = thin[2:4, :]


def finish(tokens, attention_gain, f, widths):
    q_width, k_width, hidden = widths
    rows, features = tokens.shape
    f32 = jnp.float32
    vmem = pl.BlockSpec(memory_space=pltpu.VMEM)
    shapes = (
        ((rows, features), LOW), ((rows, features), LOW), ((CHUNK, q_width), f32),
        ((CHUNK, k_width), f32), ((CHUNK, k_width), f32), ((q_width, CHUNK), f32),
        ((CHUNK, hidden), f32), ((CHUNK, hidden), f32), ((hidden, CHUNK), f32), ((8, 128), f32),
    )
    return pl.pallas_call(
        finish_kernel,
        out_shape=[jax.ShapeDtypeStruct(shape, kind) for shape, kind in shapes],
        in_specs=[vmem] * 11,
        out_specs=[vmem] * len(shapes),
        compiler_params=pltpu.CompilerParams(vmem_limit_bytes=60 * 1024 * 1024),
    )(
        tokens, attention_gain, f["middle"], f["mlp_out"], f["mlp_other"], f["grad_middle"],
        f["partial"], f["partial_other"], f["early"], f["late"], f["gains"],
    )


def shards(
    tokens,
    cotangent,
    positions,
    segments,
    attention_gain,
    query_weight,
    key_weight,
    value_weight,
    query_gain,
    key_gain,
    out_weight,
    mlp_gain,
    gate_weight,
    up_weight,
    down_weight,
):
    f = layer(
        tokens[0], cotangent[0], positions, segments, attention_gain[None], query_weight,
        key_weight, value_weight, query_gain[None], key_gain[None], out_weight, mlp_gain[None],
        gate_weight, up_weight, down_weight,
    )
    results = finish(
        tokens[0], attention_gain[None], f,
        (query_weight.shape[1], key_weight.shape[1], gate_weight.shape[1]),
    )
    gains = results[-1]
    return (
        results[0][None],
        results[1][None],
        *results[2:-1],
        gains[0, :CHUNK],
        gains[1, :CHUNK],
        gains[2, :2],
        gains[3, :2],
    )


def solution(mesh):
    return jax.shard_map(
        shards,
        mesh=mesh,
        in_specs=(
            P("dp", "seq", None),
            P("dp", "seq", None),
            P("dp", "seq"),
            P("dp", "seq"),
            P(),
            P(None, "tensor"),
            P(None, "tensor"),
            P(None, "tensor"),
            P(),
            P(),
            P("tensor", None),
            P(),
            P(None, "tensor"),
            P(None, "tensor"),
            P("tensor", None),
        ),
        out_specs=(
            P("dp", "seq", None),
            P("dp", "seq", None),
            P(("dp", "seq"), "tensor"),
            P(("dp", "seq"), "tensor"),
            P(("dp", "seq"), "tensor"),
            P("tensor", ("dp", "seq")),
            P(("dp", "seq"), "tensor"),
            P(("dp", "seq"), "tensor"),
            P("tensor", ("dp", "seq")),
            P(("dp", "seq")),
            P(("dp", "seq")),
            P(("dp", "seq")),
            P(("dp", "seq")),
        ),
        check_vma=False,
    )
```

```python
import functools
import math

import jax
import jax.numpy as jnp
from jax import lax
from jax.experimental import pallas as pl
from jax.experimental.pallas import tpu as pltpu
from jax.sharding import PartitionSpec as P

EPS = 1e-06
ROPE_BASE = 1000000.0
NEGATIVE = -1e30


MESH = pl.DeviceIdType.MESH
CHUNK = 16
DIMS = ("x3", "x1", "y3", "y1", "z")
LOW = jnp.bfloat16


def place():
    dp = lax.axis_index("dp")
    seq = lax.axis_index("seq")
    tensor = lax.axis_index("tensor")
    x, z = dp // 2, dp % 2
    y, core = seq // 2, seq % 2
    x_near = x + 1 - 2 * (x % 2)
    y_near = y + 1 - 2 * (y % 2)
    bits = {
        "core": core,
        "x3": x // 2,
        "x1": (x // 2 + x % 2) % 2,
        "y3": y // 2,
        "y1": (y // 2 + y % 2) % 2,
        "z": z,
    }
    def flip(dims):
        far_x = x_near if "x1" in dims else x
        far_x = 3 - far_x if "x3" in dims else far_x
        far_y = y_near if "y1" in dims else y
        far_y = 3 - far_y if "y3" in dims else far_y
        far_z = 1 - z if "z" in dims else z
        return (far_x * 2 + far_z, far_y * 2 + core, tensor)

    partners = {
        "core": (dp, seq + 1 - 2 * core, tensor),
        "x3": ((3 - x) * 2 + z, seq, tensor),
        "x1": (x_near * 2 + z, seq, tensor),
        "y3": (dp, (3 - y) * 2 + core, tensor),
        "y1": (dp, y_near * 2 + core, tensor),
        "z": (dp + 1 - 2 * z, seq, tensor),
        "tensor": (dp, seq, 1 - tensor),
    }
    return bits, partners, flip


def greet(partners):
    barrier = pltpu.get_barrier_semaphore()
    for partner in partners:
        pl.semaphore_signal(barrier, inc=1, device_id=partner, device_id_type=MESH)
    pl.semaphore_wait(barrier, len(partners))


EARLY_ORDERS = (
    ("core", "x3", "x1", "y3", "z", "y1"),
    ("core", "x1", "x3", "y1", "z", "y3"),
    ("core", "y3", "x3", "x1", "z", "y1"),
    ("core", "y1", "x1", "x3", "z", "y3"),
    ("core", "z", "y3", "x1", "x3", "y1"),
)
LATE_ORDERS = (
    ("core", "x3", "x1", "y3", "y1", "z"),
    ("core", "x1", "x3", "y1", "y3", "z"),
    ("core", "y3", "y1", "x3", "x1", "z"),
    ("core", "y1", "y3", "x1", "x3", "z"),
)


def masks(dims):
    return [tuple(d for i, d in enumerate(dims) if m >> (len(dims) - 1 - i) & 1) for m in range(1, 8)]


def slot_chunks(order):
    chunks = []
    for slot in range(2 ** len(order)):
        bit = {d: (slot >> (len(order) - 1 - i)) & 1 for i, d in enumerate(order)}
        x = 2 * bit["x3"] + (bit["x3"] ^ bit["x1"])
        y = 2 * bit["y3"] + (bit["y3"] ^ bit["y1"])
        chunks.append(((x * 2 + bit["z"]) * 4 + y) * 2 + bit["core"])
    return chunks


def remote(source, target, out_sem, in_sem, partner):
    return pltpu.make_async_remote_copy(
        src_ref=source,
        dst_ref=target,
        send_sem=out_sem,
        recv_sem=in_sem,
        device_id=partner,
        device_id_type=MESH,
    )


def over_tiles(count, body):
    def step(i, _):
        body(i)
        return 0

    lax.fori_loop(0, count, step, 0)


def at_tile(i, size):
    return pl.ds(pl.multiple_of(i * size, size), size)


def times(left, right):
    return jnp.dot(left, right, preferred_element_type=jnp.float32)


def times_turned(left, right):
    return lax.dot_general(
        left, right, (((1,), (1,)), ((), ())), preferred_element_type=jnp.float32
    )


def inverse_rms(entries):
    return lax.rsqrt(jnp.mean(entries * entries, axis=-1, keepdims=True) + EPS)


EARLY_TILES = (6, 6, 4, 2, 4)
LATE_TILES = (2, 2, 2, 2)
SHIFTS = (2, 1, 3, 0)
WIDE = 256


def split_streams(sizes, tiles):
    bounds, start = [], 0
    for size in sizes:
        bounds.append((start, start + size))
        start += size
    streams, first = [], 0
    for count in tiles:
        last = first + count * WIDE
        pieces = []
        for matrix, (low, high) in enumerate(bounds):
            begin, end = max(first, low), min(last, high)
            if begin < end:
                pieces.append((matrix, begin - low, begin, end - begin))
        streams.append((first, last - first, pieces))
        first = last
    assert first == start
    return streams


class Fetch:
    def __init__(self, far, near, sem, index):
        rows = far.shape[0] // 4
        self.copies = [
            pltpu.make_async_copy(
                far.at[pl.ds(i * rows, rows), :], near.at[pl.ds(i * rows, rows), :], sem.at[index, i]
            )
            for i in range(4)
        ]
        for copy in self.copies:
            copy.start()

    def wait(self):
        for copy in self.copies:
            copy.wait()


class Panels:
    def __init__(self, rows, panels):
        self.rows = rows
        self.panels = panels

    def find(self, first):
        start = 0
        for ref, row, columns in self.panels:
            if first < start + columns:
                return ref, row, first - start
            start += columns
        raise ValueError


class Scatter:
    def __init__(self, orders, streams, lhs, rhs, flipped, turned, sent, held, landed, send_sem, recv_sem, bits, partners, flip):
        self.streams, self.lhs, self.rhs = streams, lhs, rhs
        self.orders, self.flipped, self.last = orders, flipped, None
        self.turned, self.sent, self.held = turned, sent, held
        self.landed, self.send_sem, self.recv_sem = landed, send_sem, recv_sem
        self.bits, self.partners, self.flip = bits, partners, flip
        self.half = sent.rows
        self.copies = {}
        self.base = [0] * len(streams)

    def open(self, s):
        first, columns, pieces = self.streams[s]
        core = self.bits["core"]
        chunks = slot_chunks(self.orders[s])
        for kept in (False, True):
            ref, row, column = (self.held if kept else self.sent).find(first)
            offset = core * self.half if kept else (1 - core) * self.half
            for index, (matrix, left_column, begin, width) in enumerate(pieces):
                if not kept:
                    if self.last is not self.lhs[matrix]:
                        self.last = self.lhs[matrix]
                        self.flipped[...] = self.last[...].T
                    for slot, chunk in enumerate(chunks):
                        self.turned[index, slot * CHUNK : (slot + 1) * CHUNK, :] = self.flipped[
                            chunk * CHUNK : (chunk + 1) * CHUNK, :
                        ]
                target = column + begin - first
                right = self.rhs[matrix]

                def tile(i, index=index, right=right, left_column=left_column, target=target):
                    here = pl.multiple_of(i * WIDE, WIDE)
                    ref[row : row + self.half, pl.ds(target + here, WIDE)] = times(
                        self.turned[index, pl.ds(pl.multiple_of(offset, CHUNK), self.half), :],
                        right[:, pl.ds(left_column + here, WIDE)],
                    ).astype(LOW)

                over_tiles(width // WIDE, tile)
            if not kept:
                self.send(
                    0, s, ref.at[pl.ds(row, self.half), pl.ds(column, columns)]
                )

    def send(self, step, s, source):
        first, columns, _ = self.streams[s]
        ref, column = self.landed[step]
        copy = remote(
            source,
            ref.at[:, pl.ds(column + first, columns)],
            self.send_sem.at[s, step],
            self.recv_sem.at[s, step],
            self.partners[self.orders[s][step]],
        )
        copy.start()
        self.copies[s, step] = copy

    def step(self, step, streams=range(4)):
        rows = self.half >> step
        for s in streams:
            first, columns, _ = self.streams[s]
            self.copies[s, step].wait()
            ref, row, column = self.held.find(first)
            mine = pl.ds(column, columns)
            landed, from_column = self.landed[step]
            theirs = pl.ds(from_column + first, columns)
            tile = min(rows, 64)

            def add(i, s=s, tile=tile, ref=ref, row=row, mine=mine, landed=landed, theirs=theirs):
                start = pl.multiple_of(i * tile, tile)
                here = pl.ds(pl.multiple_of(row + self.base[s] + start, tile), tile)
                ref[here, mine] = ref[here, mine] + landed[pl.ds(start, tile), theirs]

            over_tiles(rows // tile, add)
            if step == 2:
                self.spread(s)
                continue
            bit = self.bits[self.orders[s][step + 1]]
            away = pl.multiple_of(row + self.base[s] + (1 - bit) * (rows // 2), CHUNK)
            self.send(step + 1, s, ref.at[pl.ds(away, rows // 2), mine])
            self.base[s] = self.base[s] + bit * (rows // 2)

    def landing(self, s, mask):
        step, place_in = ((3, mask - 1), (4, mask - 5), (5, 0))[(mask > 4) + (mask > 6)]
        ref, column = self.landed[step]
        first, columns, _ = self.streams[s]
        return ref.at[pl.ds(place_in * CHUNK, CHUNK), pl.ds(column + first, columns)]

    def spread(self, s):
        first, columns, _ = self.streams[s]
        ref, row, column = self.held.find(first)
        dims = self.orders[s][3:]
        for mask, flipped in enumerate(masks(dims), 1):
            slot = 0
            for d in dims:
                slot = slot * 2 + (1 - self.bits[d] if d in flipped else self.bits[d])
            there = pl.multiple_of(row + self.base[s] + slot * CHUNK, CHUNK)
            copy = remote(
                ref.at[pl.ds(there, CHUNK), pl.ds(column, columns)],
                self.landing(s, mask),
                self.send_sem.at[s, 2 + mask],
                self.recv_sem.at[s, 2 + mask],
                self.flip(flipped),
            )
            copy.start()
            self.copies[s, 2 + mask] = copy

    def finish(self, out, streams=range(4)):
        for s in streams:
            first, columns, _ = self.streams[s]
            ref, row, column = self.held.find(first)
            slot = 0
            for d in self.orders[s][3:]:
                slot = slot * 2 + self.bits[d]
            mine = pl.multiple_of(row + self.base[s] + slot * CHUNK, CHUNK)
            total = ref[pl.ds(mine, CHUNK), pl.ds(column, columns)].astype(jnp.float32)
            for mask in range(1, 8):
                self.copies[s, 2 + mask].wait()
                total = total + self.landing(s, mask)[...].astype(jnp.float32)
            out[:, pl.ds(first, columns)] = total


def layer_kernel(early_streams, late_streams, *refs):
    (
        tokens, cotangent, positions, segments, frequencies, attention_gain, query_gain,
        key_gain, mlp_gain, wq_far, wk_far, wv_far, wo_far, wg_far, wu_far, wd_far, output,
        input_grad, early_out, late_out, gains, middle, grad_middle, partial_other, normed, query_raw, key_raw, query, kv, meta, cosine, sine, attended, normed_mlp,
        activated, gate_grad, up_grad, middle_low, attended_grad, inner, mlp_gain_grad, wq, wk,
        wv, wo, wg, wu, wd, bias, total, weight_sum, act_grad, part_out, part_in, flipped, turned, held,
        far_grad, gains_sent, gains_landed, weight_sem, kv_send, kv_recv, meta_send, meta_recv,
        pair_send, pair_recv, early_send, early_recv, late_send, late_recv, core_send,
        core_recv, far_send, far_recv, gains_send, gains_recv,
    ) = refs[: -11]
    early_landed, late_landed = refs[-11:-5], refs[-5:]
    mlp_out, mlp_other, partial = part_out.at[0], part_in.at[0], part_out.at[1]
    bits, partners, flip = place()
    dp, seq, tensor = lax.axis_index("dp"), lax.axis_index("seq"), lax.axis_index("tensor")
    core, y = seq % 2, seq // 2
    after, before, across = (y + 1) % 4, (y + 3) % 4, (y + 2) % 4
    near = (dp, y * 2 + 1 - core, tensor)
    ahead = (dp, after * 2 + core, tensor)
    behind = (dp, before * 2 + core, tensor)
    pair = (dp, seq, 1 - tensor)
    others = [(dp, (seq + step) % 8, tensor) for step in range(1, 8)]
    rows = tokens.shape[0]
    heads = kv.shape[2]
    hd = kv.shape[4]
    groups = {frozenset(m) for order in EARLY_ORDERS + LATE_ORDERS for m in masks(order[3:])}
    groups |= {frozenset((name,)) for name in ("x3", "x1", "z")}
    groups = sorted(sorted(group) for group in groups if group & {"x3", "x1", "z"})
    greet(others + [partners["tensor"]] + [flip(group) for group in groups])
    got_wk = Fetch(wk_far, wk, weight_sem, 0)
    got_wv = Fetch(wv_far, wv, weight_sem, 1)
    got_wq = Fetch(wq_far, wq, weight_sem, 2)

    meta[seq] = jnp.zeros_like(meta[seq])
    meta[seq, 0:1, :] = positions[...]
    meta[seq, 1:2, :] = segments[...]
    metas = [
        remote(meta.at[seq], meta.at[seq], meta_send.at[i], meta_recv.at[i], other)
        for i, other in enumerate(others)
    ]
    for copy in metas:
        copy.start()

    place_rows = jnp.broadcast_to(positions[...].astype(jnp.float32), (rows, rows)).T
    segment_rows = jnp.broadcast_to(segments[...].astype(jnp.float32), (rows, rows)).T
    angle = place_rows[:, :hd] * frequencies[...]
    cosine[...] = jnp.cos(angle)
    lane = lax.broadcasted_iota(jnp.int32, (rows, hd), 1)
    sine[...] = jnp.where(lane < hd // 2, -1.0, 1.0) * jnp.sin(angle)

    def turn(entries):
        return entries * cosine[...] + pltpu.roll(entries, hd // 2, 1) * sine[...]

    x = tokens[...].astype(jnp.float32)
    normed[...] = (x * inverse_rms(x) * attention_gain[...].astype(jnp.float32)[None, :]).astype(LOW)

    tile = 2 * hd
    got_wk.wait()

    def key_tile(i):
        raw = times(normed[...], wk[:, at_tile(i, tile)])
        key_raw[:, at_tile(i, tile)] = raw
        for g in range(2):
            head = raw[:, g * hd : (g + 1) * hd]
            scaled = head * inverse_rms(head) * key_gain[...].astype(jnp.float32)[None, :]
            kv[seq, 0, 2 * i + g] = turn(scaled).astype(LOW)

    over_tiles(heads // 2, key_tile)

    def own(half, kind, target, index):
        copy = remote(
            kv.at[seq, half], kv.at[seq, half], kv_send.at[index], kv_recv.at[kind, half], target
        )
        copy.start()
        return copy

    sends = [own(0, 1, ahead, 0), own(0, 2, behind, 1), own(0, 0, near, 2)]
    got_wv.wait()

    def value_tile(i):
        raw = times(normed[...], wv[:, at_tile(i, tile)]).astype(LOW)
        for g in range(2):
            kv[seq, 1, 2 * i + g] = raw[:, g * hd : (g + 1) * hd]

    over_tiles(heads // 2, value_tile)
    sends += [own(1, 1, ahead, 3), own(1, 2, behind, 4), own(1, 0, near, 5)]
    got_wq.wait()
    got_wo = Fetch(wo_far, wo, weight_sem, 3)
    got_wd = Fetch(wd_far, wd, weight_sem, 4)
    got_wg = Fetch(wg_far, wg, weight_sem, 5)
    got_wu = Fetch(wu_far, wu, weight_sem, 6)
    scale = math.log2(math.e) / math.sqrt(hd)

    def query_tile(i):
        raw = times(normed[...], wq[:, at_tile(i, tile)])
        query_raw[:, at_tile(i, tile)] = raw
        for g in range(2):
            head = raw[:, g * hd : (g + 1) * hd]
            scaled = head * inverse_rms(head) * (query_gain[...].astype(jnp.float32)[None, :] * scale)
            query[i, g * rows : (g + 1) * rows, :] = turn(scaled).astype(LOW)

    over_tiles(heads, query_tile)
    total[...] = jnp.zeros_like(total)
    weight_sum[...] = jnp.zeros_like(weight_sum)
    for copy in metas:
        copy.wait()

    def attend(slot):
        key_place = meta[slot, 0:1, :].astype(jnp.float32)
        key_segment = meta[slot, 1:2, :].astype(jnp.float32)
        allowed = (key_place <= place_rows) & (key_segment == segment_rows)
        bias[:, :rows] = jnp.where(allowed, 0.0, NEGATIVE)

        def head(j):
            scores = times_turned(query[j], kv[slot, 0, j])
            weights = jnp.concatenate(
                [jnp.exp2(scores[g * rows : (g + 1) * rows] + bias[:, :rows]) for g in range(2)], axis=0
            )
            weight_sum[j] += weights[:, :hd] + weights[:, hd:]
            total[j] += times(weights.astype(LOW), kv[slot, 1, j])

        over_tiles(heads, head)

    def arrived(slot, kind, half):
        remote(
            kv.at[slot, half], kv.at[slot, half], kv_send.at[0], kv_recv.at[kind, half], near
        ).wait_recv()

    def pass_on(slot, half, kind, target, index):
        copy = remote(
            kv.at[slot, half], kv.at[slot, half], kv_send.at[index], kv_recv.at[kind, half], target
        )
        copy.start()
        sends.append(copy)

    attend(seq)
    near_slot = y * 2 + 1 - core
    arrived(near_slot, 0, 0)
    arrived(near_slot, 0, 1)
    attend(near_slot)
    before_slot, after_slot, across_slot = before * 2 + core, after * 2 + core, across * 2 + core
    arrived(before_slot, 1, 0)
    pass_on(before_slot, 0, 3, ahead, 6)
    pass_on(before_slot, 0, 4, near, 7)
    arrived(after_slot, 2, 0)
    pass_on(after_slot, 0, 5, near, 8)
    arrived(after_slot, 2, 1)
    pass_on(after_slot, 1, 3, behind, 9)
    pass_on(after_slot, 1, 5, near, 10)
    arrived(before_slot, 1, 1)
    pass_on(before_slot, 1, 4, near, 11)
    attend(before_slot)
    attend(after_slot)
    for far_y, kind in ((before, 4), (after, 5)):
        slot = far_y * 2 + 1 - core
        arrived(slot, kind, 0)
        arrived(slot, kind, 1)
        attend(slot)
    arrived(across_slot, 3, 0)
    pass_on(across_slot, 0, 6, near, 12)
    arrived(across_slot, 3, 1)
    pass_on(across_slot, 1, 6, near, 13)
    attend(across_slot)
    far_slot = across * 2 + 1 - core
    arrived(far_slot, 6, 0)
    arrived(far_slot, 6, 1)
    attend(far_slot)

    def finish(j):
        inverse = 1.0 / jnp.sum(weight_sum[j], axis=-1, keepdims=True)
        result = total[j] * inverse
        total[j] = result
        weight_sum[j] = jnp.broadcast_to(inverse, result.shape)
        for g in range(2):
            attended[:, at_tile(2 * j + g, hd)] = result[g * rows : (g + 1) * rows].astype(LOW)

    over_tiles(heads, finish)
    got_wo.wait()
    wide = 256
    features = tokens.shape[1]
    hidden = wg.shape[1]

    def out_tile(i):
        part_out[0, :, at_tile(i, wide)] = times(attended[...], wo[:, at_tile(i, wide)]).astype(LOW)

    def in_halves(body, target, source, index):
        copies = []
        for part in range(2):
            count = features // wide // 2

            def tile_of_part(i, part=part):
                body(i + part * count)

            over_tiles(count, tile_of_part)
            here = pl.ds(part * features // 2, features // 2)
            copies.append(
                remote(
                    source.at[:, here],
                    target.at[:, here],
                    pair_send.at[index, part],
                    pair_recv.at[index, part],
                    pair,
                )
            )
            copies[-1].start()
        return copies

    def wait_all(copies):
        for copy in copies:
            copy.wait()

    first = in_halves(out_tile, part_in.at[0], part_out.at[0], 0)
    got_wd.wait()

    def act_grad_tile(i):
        act_grad[:, at_tile(i, wide)] = times_turned(cotangent[...], wd[at_tile(i, wide), :])

    over_tiles(hidden // wide, act_grad_tile)
    got_wg.wait()
    got_wu.wait()
    wait_all(first)
    mid = (
        tokens[...].astype(jnp.float32)
        + (part_out[0].astype(jnp.float32) + part_in[0].astype(jnp.float32))
    )
    middle[...] = mid
    normed_mlp[...] = (mid * inverse_rms(mid) * mlp_gain[...].astype(jnp.float32)[None, :]).astype(LOW)

    def hidden_tile(i):
        here = at_tile(i, wide)
        gate_here = times(normed_mlp[...], wg[:, here])
        up_here = times(normed_mlp[...], wu[:, here])
        sigmoid = 1.0 / (1.0 + jnp.exp(-gate_here))
        silu = gate_here * sigmoid
        grad = act_grad[:, here]
        activated[:, here] = (silu * up_here).astype(LOW)
        gate_grad[:, here] = (
            grad * up_here * sigmoid * (1.0 + gate_here * (1.0 - sigmoid))
        ).astype(LOW)
        up_grad[:, here] = (grad * silu).astype(LOW)

    over_tiles(hidden // wide, hidden_tile)

    def back_tile(i):
        here = at_tile(i, wide)
        part_out[1, :, here] = (
            times_turned(gate_grad[...], wg[here, :]) + times_turned(up_grad[...], wu[here, :])
        ).astype(LOW)

    second = in_halves(back_tile, part_in.at[1], part_out.at[1], 1)

    def down_tile(i):
        mlp_out[:, at_tile(i, wide)] = times(activated[...], wd[:, at_tile(i, wide)]).astype(LOW)

    over_tiles(features // wide, down_tile)
    half = features // 2
    early = Scatter(
        EARLY_ORDERS, early_streams, [normed_mlp, normed_mlp, cotangent, middle_low],
        [gate_grad, up_grad, activated, attended], flipped, turned,
        Panels(half, [(wg, 0, hidden), (wg, half, hidden), (wu, 0, hidden), (wu, half, hidden)]),
        Panels(half, [(held, 0, held.shape[1])]), [(ref, 0) for ref in early_landed],
        early_send, early_recv, bits, partners, flip,
    )
    for s in range(4):
        early.open(s)
    early.step(0, streams=range(4))
    for copy in sends:
        copy.wait_send()
    wait_all(second)
    mid = middle[...]
    inverse = inverse_rms(mid)
    dy = part_out[1].astype(jnp.float32) + part_in[1].astype(jnp.float32)
    mlp_gain_grad[...] = jnp.sum(dy * mid * inverse, axis=0, keepdims=True)
    scaled = dy * mlp_gain[...].astype(jnp.float32)[None, :]
    grad = (
        cotangent[...].astype(jnp.float32)
        + inverse * scaled
        - mid * (inverse * inverse * inverse) * jnp.mean(scaled * mid, axis=-1, keepdims=True)
    )
    grad_middle[...] = grad
    middle_low[...] = grad.astype(LOW)

    def attended_grad_tile(j):
        both = times_turned(middle_low[...], wo[at_tile(j, 2 * hd), :]).astype(LOW)
        both = both.astype(jnp.float32)
        for g in range(2):
            here = slice(g * rows, (g + 1) * rows)
            normal = both[:, g * hd : (g + 1) * hd] * weight_sum[j, here, :]
            attended_grad[j, here, :] = normal.astype(LOW)
            summed = jnp.sum((normal * total[j, here, :]).T, axis=0, keepdims=True)
            inner[j, :, here] = jnp.broadcast_to(summed, (8, rows))

    over_tiles(heads, attended_grad_tile)


    early.open(4)
    place_row = positions[...].astype(jnp.float32)
    segment_row = segments[...].astype(jnp.float32)
    act_grad[...] = jnp.zeros_like(act_grad)

    def query_turned(j):
        return pl.ds(pl.multiple_of(j % 2 * hd, hd), hd), at_tile(j // 2, 2 * rows)

    def block(slot, target, first):
        columns = meta[slot].astype(jnp.float32).T
        allowed = (columns[:, 0:1] <= place_row) & (columns[:, 1:2] == segment_row)
        one = jnp.where(allowed, 0.0, NEGATIVE)
        bias[:, :rows] = one
        bias[:, rows:] = one

        def head(j):
            key, value = kv[slot, 0, j], kv[slot, 1, j]
            weight = jnp.exp2(times_turned(key, query[j]) + bias[...])
            grad = times_turned(value, attended_grad[j])
            scores_grad = (weight * (grad - inner[j, 0:1, :])).astype(LOW)
            down = pl.ds(first, rows)
            target[down, at_tile(heads + j, hd)] = times(
                weight.astype(LOW), attended_grad[j]
            ).astype(LOW)
            target[down, at_tile(j, hd)] = (times(scores_grad, query[j]) * math.log(2)).astype(LOW)
            act_grad[query_turned(j)] += lax.dot_general(
                key, scores_grad, (((0,), (0,)), ((), ())), preferred_element_type=jnp.float32
            )

        over_tiles(heads, head)

    grad_width = 2 * heads * hd
    far_sends, crossing = [], []

    def grad_rows(ref, i):
        return ref.at[pl.ds(i * rows, rows), pl.ds(0, grad_width)]

    for i, shift in enumerate(SHIFTS):
        chip = (y + shift) % 4
        block(chip * 2 + 1 - core, wg, i * rows)
        copy = remote(
            grad_rows(wg, i), grad_rows(wd, i), core_send.at[i], core_recv.at[i], partners["core"]
        )
        copy.start()
        block(chip * 2 + core, wu, i * rows)
        copy.wait()
        down, wide_grad = slice(i * rows, (i + 1) * rows), slice(0, grad_width)
        wu[down, wide_grad] = wu[down, wide_grad] + wd[down, wide_grad]
        if shift:
            copy = remote(
                grad_rows(wu, i),
                far_grad.at[i],
                far_send.at[i],
                far_recv.at[i],
                (dp, chip * 2 + core, tensor),
            )
            copy.start()
            far_sends.append(copy)
        if i == 0:
            early.step(0, streams=range(4, 5))
        if i == 2:
            early.step(1)

    outward = remote(mlp_out, mlp_other, pair_send.at[2, 0], pair_recv.at[2, 0], pair)
    outward.start()

    def back(raw, gain, gradient):
        turned_back = gradient * cosine[...] - pltpu.roll(gradient, hd // 2, 1) * sine[...]
        inverse = inverse_rms(raw)
        scaled = turned_back * gain
        raw_grad = inverse * scaled - raw * (inverse * inverse * inverse) * jnp.mean(
            scaled * raw, axis=-1, keepdims=True
        )
        return raw_grad, jnp.sum(turned_back * raw * inverse, axis=0, keepdims=True)

    gains_sent[0] = jnp.zeros_like(gains_sent[0])
    query_gain_row = query_gain[...].astype(jnp.float32)[None, :]
    key_gain_row = key_gain[...].astype(jnp.float32)[None, :]

    def query_head(j):
        gradient = act_grad[query_turned(j)].T * (1.0 / math.sqrt(hd))
        for g in range(2):
            here = at_tile(2 * j + g, hd)
            raw_grad, part = back(
                query_raw[:, here], query_gain_row, gradient[g * rows : (g + 1) * rows]
            )
            attended[:, here] = raw_grad.astype(LOW)
            gains_sent[0, 2:3, :hd] += part

    over_tiles(heads, query_head)
    early.step(1, streams=range(4, 5))
    for copy in far_sends:
        copy.wait()

    def key_head(j):
        here, there = at_tile(j, hd), at_tile(heads + j, hd)
        key_sum = wu[3 * rows : 4 * rows, here].astype(jnp.float32)
        value_sum = wu[3 * rows : 4 * rows, there].astype(jnp.float32)
        for i in range(3):
            key_sum = key_sum + far_grad[i, :, here].astype(jnp.float32)
            value_sum = value_sum + far_grad[i, :, there].astype(jnp.float32)
        raw_grad, part = back(key_raw[:, here], key_gain_row, key_sum)
        gate_grad[:, here] = raw_grad.astype(LOW)
        up_grad[:, here] = value_sum.astype(LOW)
        gains_sent[0, 3:4, :hd] += part

    over_tiles(heads, key_head)
    late = Scatter(
        LATE_ORDERS, late_streams, [normed] * 3, [attended, gate_grad, up_grad], flipped, turned,
        Panels(half, [(wg, 0, hidden), (wg, half, hidden)]),
        Panels(half, [(wu, 0, hidden), (wu, half, hidden)]),
        [(early_landed[0], 0)] + [(ref, 0) for ref in late_landed],
        late_send, late_recv, bits, partners, flip,
    )
    for s in range(4):
        late.open(s)
    x = tokens[...].astype(jnp.float32)
    inverse = inverse_rms(x)
    k_width = wk.shape[1]

    def partial_tile(i):
        here = at_tile(i, WIDE)
        result = (
            times_turned(attended[...], wq[here, :])
            + times_turned(gate_grad[:, :k_width], wk[here, :])
            + times_turned(up_grad[:, :k_width], wv[here, :])
        )
        partial[:, here] = result.astype(LOW)
        gains_sent[0, 0:1, here] = jnp.sum(
            result * (tokens[:, here].astype(jnp.float32) * inverse), axis=0, keepdims=True
        )

    outward_partial = in_halves(partial_tile, partial_other, partial, 3)
    gains_sent[0, 1:2, :] = 0.5 * mlp_gain_grad[...]
    gain_steps = (
        [(partners["tensor"])],
        [(partners["core"])],
        [flip(m) for m in (("x3",), ("x1",), ("x3", "x1"))],
        [flip(m) for m in masks(("y3", "y1", "z"))],
    )

    def send_gains(step):
        first = (0, 1, 2, 5)[step]
        copies = [
            remote(
                gains_sent.at[step], gains_landed.at[first + i], gains_send.at[first + i],
                gains_recv.at[first + i], partner,
            )
            for i, partner in enumerate(gain_steps[step])
        ]
        for copy in copies:
            copy.start()
        return copies

    def next_gains(step, copies):
        first = (0, 1, 2, 5)[step]
        sum_so_far = gains_sent[step]
        for i, copy in enumerate(copies):
            copy.wait()
            sum_so_far = sum_so_far + gains_landed[first + i]
        if step == 3:
            gains[...] = sum_so_far
            return None
        gains_sent[step + 1] = sum_so_far
        return send_gains(step + 1)

    gains_copy = send_gains(0)
    early.step(2, streams=range(5))
    for step in range(3):
        late.step(step)
        gains_copy = next_gains(step, gains_copy)
        if step == 1:
            early.finish(early_out)
            outward.wait()
            both = mlp_out[...].astype(jnp.float32) + mlp_other[...].astype(jnp.float32)
            output[...] = (middle[...] + both).astype(LOW)
        if step == 2:
            early.finish(early_out, streams=range(4, 5))
            wait_all(outward_partial)
            scaled = (
                partial[...].astype(jnp.float32) + partial_other[...].astype(jnp.float32)
            ) * attention_gain[...].astype(jnp.float32)[None, :]
            across_mean = jnp.mean(scaled * x, axis=-1, keepdims=True)
            input_grad[...] = (
                grad_middle[...] + inverse * scaled - x * (inverse * inverse * inverse) * across_mean
            ).astype(LOW)
    late.finish(late_out)
    next_gains(3, gains_copy)


def layer(
    tokens, cotangent, positions, segments, attention_gain, query_weight, key_weight, value_weight,
    query_gain, key_gain, out_weight, mlp_gain, gate_weight, up_weight, down_weight,
):
    rows, features = tokens.shape
    hd = query_gain.shape[0]
    heads = key_weight.shape[1] // hd
    half = features // 2
    q_width, k_width, hidden = query_weight.shape[1], key_weight.shape[1], gate_weight.shape[1]
    early_streams = split_streams((hidden, hidden, hidden, q_width), EARLY_TILES)
    late_streams = split_streams((q_width, k_width, k_width), LATE_TILES)
    early_width = 3 * hidden + q_width
    late_width = q_width + 2 * k_width
    pairs = jnp.arange(hd // 2, dtype=jnp.float32)
    inverse = 1.0 / ROPE_BASE ** (pairs * 2.0 / hd)
    frequencies = jnp.concatenate([inverse, inverse])[None]
    vmem = pl.BlockSpec(memory_space=pltpu.VMEM)
    far = pl.BlockSpec(memory_space=pl.ANY)
    f32 = jnp.float32
    outs = dict(
        output=((rows, features), LOW),
        input_grad=((rows, features), LOW),
        early=((CHUNK, early_width), f32),
        late=((CHUNK, late_width), f32),
        gains=((8, features), f32),
    )
    results = pl.pallas_call(
        functools.partial(layer_kernel, early_streams, late_streams),
        out_shape=[jax.ShapeDtypeStruct(shape, kind) for shape, kind in outs.values()],
        in_specs=[vmem] * 9 + [far] * 7,
        out_specs=[vmem] * len(outs),
        scratch_shapes=[
            pltpu.VMEM((rows, features), f32),
            pltpu.VMEM((rows, features), f32),
            pltpu.VMEM((rows, features), LOW),
            pltpu.VMEM((rows, features), LOW),
            pltpu.VMEM((rows, q_width), f32),
            pltpu.VMEM((rows, k_width), f32),
            pltpu.VMEM((heads, 2 * rows, hd), LOW),
            pltpu.VMEM((8, 2, heads, rows, hd), LOW),
            pltpu.VMEM((8, 8, rows), jnp.int32),
            pltpu.VMEM((rows, hd), f32),
            pltpu.VMEM((rows, hd), f32),
            pltpu.VMEM((rows, q_width), LOW),
            pltpu.VMEM((rows, features), LOW),
            pltpu.VMEM((rows, hidden), LOW),
            pltpu.VMEM((rows, hidden), LOW),
            pltpu.VMEM((rows, hidden), LOW),
            pltpu.VMEM((rows, features), LOW),
            pltpu.VMEM((heads, 2 * rows, hd), LOW),
            pltpu.VMEM((heads, 8, 2 * rows), f32),
            pltpu.VMEM((1, features), f32),
            pltpu.VMEM(query_weight.shape, LOW),
            pltpu.VMEM(key_weight.shape, LOW),
            pltpu.VMEM(value_weight.shape, LOW),
            pltpu.VMEM(out_weight.shape, LOW),
            pltpu.VMEM(gate_weight.shape, LOW),
            pltpu.VMEM(up_weight.shape, LOW),
            pltpu.VMEM(down_weight.shape, LOW),
            pltpu.VMEM((rows, 2 * rows), f32),
            pltpu.VMEM((heads, 2 * rows, hd), f32),
            pltpu.VMEM((heads, 2 * rows, hd), f32),
            pltpu.VMEM((rows, hidden), f32),
            pltpu.VMEM((2, rows, features), LOW),
            pltpu.VMEM((2, rows, features), LOW),
            pltpu.VMEM((features, rows), LOW),
            pltpu.VMEM((1, features, rows), LOW),
            pltpu.VMEM((half, early_width), LOW),
            pltpu.VMEM((3, rows, 2 * k_width), LOW),
            pltpu.VMEM((4, 8, features), f32),
            pltpu.VMEM((12, 8, features), f32),
            pltpu.SemaphoreType.DMA((7, 4)),
            pltpu.SemaphoreType.DMA((14,)),
            pltpu.SemaphoreType.DMA((7, 2)),
            pltpu.SemaphoreType.DMA((7,)),
            pltpu.SemaphoreType.DMA((7,)),
            pltpu.SemaphoreType.DMA((4, 2)),
            pltpu.SemaphoreType.DMA((4, 2)),
            pltpu.SemaphoreType.DMA((5, 10)),
            pltpu.SemaphoreType.DMA((5, 10)),
            pltpu.SemaphoreType.DMA((5, 10)),
            pltpu.SemaphoreType.DMA((5, 10)),
            pltpu.SemaphoreType.DMA((4,)),
            pltpu.SemaphoreType.DMA((4,)),
            pltpu.SemaphoreType.DMA((3,)),
            pltpu.SemaphoreType.DMA((3,)),
            pltpu.SemaphoreType.DMA((12,)),
            pltpu.SemaphoreType.DMA((12,)),
        ]
        + [pltpu.VMEM((half >> step, early_width), LOW) for step in range(6)]
        + [pltpu.VMEM((half >> step, late_width), LOW) for step in range(1, 6)],
        compiler_params=pltpu.CompilerParams(
            collective_id=0, has_side_effects=True, vmem_limit_bytes=63 * 1024 * 1024
        ),
    )(
        tokens, cotangent, positions, segments, frequencies, attention_gain, query_gain, key_gain,
        mlp_gain, query_weight, key_weight, value_weight, out_weight, gate_weight, up_weight,
        down_weight,
    )
    return dict(zip(outs, results))


def finish_kernel(
    output_in, input_grad_in, early, late, gains, output, input_grad, grad_query, grad_key,
    grad_value, grad_out, grad_gate, grad_up, grad_down, attention_gain, mlp_gain, query_gain,
    key_gain,
):
    hidden, q_width, k_width = grad_gate.shape[1], grad_query.shape[1], grad_key.shape[1]
    output[...] = output_in[...]
    input_grad[...] = input_grad_in[...]
    grad_gate[...] = early[:, :hidden]
    grad_up[...] = early[:, hidden : 2 * hidden]
    grad_down[...] = early[:, 2 * hidden : 3 * hidden]
    grad_out[...] = early[:, 3 * hidden :]
    grad_query[...] = late[:, :q_width]
    grad_key[...] = late[:, q_width : q_width + k_width]
    grad_value[...] = late[:, q_width + k_width :]
    chunk = lax.axis_index("dp") * 8 + lax.axis_index("seq")
    features = gains.shape[1]
    wide = pltpu.roll(gains[0:8, :], lax.rem(features - chunk * CHUNK, features), 1)
    thin = pltpu.roll(gains[0:8, :128], lax.rem(128 - chunk * 2, 128), 1)
    attention_gain[...] = wide[0:1, : attention_gain.shape[1]]
    mlp_gain[...] = wide[1:2, : mlp_gain.shape[1]]
    query_gain[...] = thin[2:3, : query_gain.shape[1]]
    key_gain[...] = thin[3:4, : key_gain.shape[1]]


def finish(f, widths):
    q_width, k_width, hidden = widths
    rows, features = f["output"].shape
    f32 = jnp.float32
    vmem = pl.BlockSpec(memory_space=pltpu.VMEM)
    shapes = (
        ((rows, features), LOW), ((rows, features), LOW), ((CHUNK, q_width), f32),
        ((CHUNK, k_width), f32), ((CHUNK, k_width), f32), ((CHUNK, q_width), f32),
        ((CHUNK, hidden), f32), ((CHUNK, hidden), f32), ((CHUNK, hidden), f32),
        ((1, CHUNK), f32), ((1, CHUNK), f32), ((1, 2), f32), ((1, 2), f32),
    )
    return pl.pallas_call(
        finish_kernel,
        out_shape=[jax.ShapeDtypeStruct(shape, kind) for shape, kind in shapes],
        in_specs=[vmem] * 5,
        out_specs=[vmem] * len(shapes),
        compiler_params=pltpu.CompilerParams(vmem_limit_bytes=60 * 1024 * 1024),
    )(f["output"], f["input_grad"], f["early"], f["late"], f["gains"])


def shards(
    tokens,
    cotangent,
    positions,
    segments,
    attention_gain,
    query_weight,
    key_weight,
    value_weight,
    query_gain,
    key_gain,
    out_weight,
    mlp_gain,
    gate_weight,
    up_weight,
    down_weight,
):
    f = layer(
        tokens[0], cotangent[0], positions, segments, attention_gain, query_weight,
        key_weight, value_weight, query_gain, key_gain, out_weight, mlp_gain,
        gate_weight, up_weight, down_weight,
    )
    results = finish(
        f, (query_weight.shape[1], key_weight.shape[1], gate_weight.shape[1])
    )
    output, input_grad, query, key, value, out, gate, up, down, *gains = results
    return (
        output[None],
        input_grad[None],
        query,
        key,
        value,
        out.T,
        gate,
        up,
        down.T,
        *(gain[0] for gain in gains),
    )


def solution(mesh):
    return jax.shard_map(
        shards,
        mesh=mesh,
        in_specs=(
            P("dp", "seq", None),
            P("dp", "seq", None),
            P("dp", "seq"),
            P("dp", "seq"),
            P(),
            P(None, "tensor"),
            P(None, "tensor"),
            P(None, "tensor"),
            P(),
            P(),
            P("tensor", None),
            P(),
            P(None, "tensor"),
            P(None, "tensor"),
            P("tensor", None),
        ),
        out_specs=(
            P("dp", "seq", None),
            P("dp", "seq", None),
            P(("dp", "seq"), "tensor"),
            P(("dp", "seq"), "tensor"),
            P(("dp", "seq"), "tensor"),
            P("tensor", ("dp", "seq")),
            P(("dp", "seq"), "tensor"),
            P(("dp", "seq"), "tensor"),
            P("tensor", ("dp", "seq")),
            P(("dp", "seq")),
            P(("dp", "seq")),
            P(("dp", "seq")),
            P(("dp", "seq")),
        ),
        check_vma=False,
    )
```

```python
import functools
import math

import jax
import jax.numpy as jnp
from jax import lax
from jax.experimental import pallas as pl
from jax.experimental.pallas import tpu as pltpu
from jax.sharding import PartitionSpec as P

EPS = 1e-06
ROPE_BASE = 1000000.0
NEGATIVE = -1e30


MESH = pl.DeviceIdType.MESH
CHUNK = 16
DIMS = ("x3", "x1", "y3", "y1", "z")
LOW = jnp.bfloat16


def place():
    dp = lax.axis_index("dp")
    seq = lax.axis_index("seq")
    tensor = lax.axis_index("tensor")
    x, z = dp // 2, dp % 2
    y, core = seq // 2, seq % 2
    x_near = x + 1 - 2 * (x % 2)
    y_near = y + 1 - 2 * (y % 2)
    bits = {
        "core": core,
        "x3": x // 2,
        "x1": (x // 2 + x % 2) % 2,
        "y3": y // 2,
        "y1": (y // 2 + y % 2) % 2,
        "z": z,
    }
    def flip(dims):
        far_x = x_near if "x1" in dims else x
        far_x = 3 - far_x if "x3" in dims else far_x
        far_y = y_near if "y1" in dims else y
        far_y = 3 - far_y if "y3" in dims else far_y
        far_z = 1 - z if "z" in dims else z
        return (far_x * 2 + far_z, far_y * 2 + core, tensor)

    partners = {
        "core": (dp, seq + 1 - 2 * core, tensor),
        "x3": ((3 - x) * 2 + z, seq, tensor),
        "x1": (x_near * 2 + z, seq, tensor),
        "y3": (dp, (3 - y) * 2 + core, tensor),
        "y1": (dp, y_near * 2 + core, tensor),
        "z": (dp + 1 - 2 * z, seq, tensor),
        "tensor": (dp, seq, 1 - tensor),
    }
    return bits, partners, flip


def greet(partners):
    barrier = pltpu.get_barrier_semaphore()
    for partner in partners:
        pl.semaphore_signal(barrier, inc=1, device_id=partner, device_id_type=MESH)
    pl.semaphore_wait(barrier, len(partners))


EARLY_ORDERS = (
    ("core", "x3", "x1", "y3", "z", "y1"),
    ("core", "x1", "x3", "y1", "z", "y3"),
    ("core", "y3", "z", "x3", "x1", "y1"),
    ("core", "y1", "x1", "x3", "z", "y3"),
    ("core", "z", "x1", "x3", "y3", "y1"),
)
LATE_ORDERS = (
    ("core", "x3", "x1", "y3", "y1", "z"),
    ("core", "x1", "x3", "y1", "y3", "z"),
    ("core", "y3", "y1", "x3", "x1", "z"),
    ("core", "y1", "y3", "x1", "x3", "z"),
)


def masks(dims):
    return [tuple(d for i, d in enumerate(dims) if m >> (len(dims) - 1 - i) & 1) for m in range(1, 8)]


def slot_chunks(order):
    chunks = []
    for slot in range(2 ** len(order)):
        bit = {d: (slot >> (len(order) - 1 - i)) & 1 for i, d in enumerate(order)}
        x = 2 * bit["x3"] + (bit["x3"] ^ bit["x1"])
        y = 2 * bit["y3"] + (bit["y3"] ^ bit["y1"])
        chunks.append(((x * 2 + bit["z"]) * 4 + y) * 2 + bit["core"])
    return chunks


def remote(source, target, out_sem, in_sem, partner):
    return pltpu.make_async_remote_copy(
        src_ref=source,
        dst_ref=target,
        send_sem=out_sem,
        recv_sem=in_sem,
        device_id=partner,
        device_id_type=MESH,
    )


def over_tiles(count, body):
    def step(i, _):
        body(i)
        return 0

    lax.fori_loop(0, count, step, 0)


def at_tile(i, size):
    return pl.ds(pl.multiple_of(i * size, size), size)


def times(left, right):
    return jnp.dot(left, right, preferred_element_type=jnp.float32)


def times_turned(left, right):
    return lax.dot_general(
        left, right, (((1,), (1,)), ((), ())), preferred_element_type=jnp.float32
    )


def inverse_rms(entries):
    return lax.rsqrt(jnp.mean(entries * entries, axis=-1, keepdims=True) + EPS)


EARLY_TILES = (6, 6, 4, 2, 4)
LATE_TILES = (2, 2, 2, 2)
SHIFTS = (2, 1, 3, 0)
WIDE = 256


def split_streams(sizes, tiles):
    bounds, start = [], 0
    for size in sizes:
        bounds.append((start, start + size))
        start += size
    streams, first = [], 0
    for count in tiles:
        last = first + count * WIDE
        pieces = []
        for matrix, (low, high) in enumerate(bounds):
            begin, end = max(first, low), min(last, high)
            if begin < end:
                pieces.append((matrix, begin - low, begin, end - begin))
        streams.append((first, last - first, pieces))
        first = last
    assert first == start
    return streams


class Fetch:
    def __init__(self, far, near, sem, index):
        rows = far.shape[0] // 4
        self.copies = [
            pltpu.make_async_copy(
                far.at[pl.ds(i * rows, rows), :], near.at[pl.ds(i * rows, rows), :], sem.at[index, i]
            )
            for i in range(4)
        ]
        for copy in self.copies:
            copy.start()

    def wait(self):
        for copy in self.copies:
            copy.wait()


class Panels:
    def __init__(self, rows, panels):
        self.rows = rows
        self.panels = panels

    def find(self, first):
        start = 0
        for ref, row, columns in self.panels:
            if first < start + columns:
                return ref, row, first - start
            start += columns
        raise ValueError


class Scatter:
    def __init__(self, orders, streams, lhs, rhs, flipped, turned, sent, held, landed, send_sem, recv_sem, bits, partners, flip):
        self.streams, self.lhs, self.rhs = streams, lhs, rhs
        self.orders, self.flipped, self.last = orders, flipped, None
        self.turned, self.sent, self.held = turned, sent, held
        self.landed, self.send_sem, self.recv_sem = landed, send_sem, recv_sem
        self.bits, self.partners, self.flip = bits, partners, flip
        self.half = sent.rows
        self.copies = {}
        self.base = [0] * len(streams)

    def open(self, s):
        first, columns, pieces = self.streams[s]
        core = self.bits["core"]
        chunks = slot_chunks(self.orders[s])
        for kept in (False, True):
            ref, row, column = (self.held if kept else self.sent).find(first)
            offset = core * self.half if kept else (1 - core) * self.half
            for index, (matrix, left_column, begin, width) in enumerate(pieces):
                if not kept:
                    if self.last is not self.lhs[matrix]:
                        self.last = self.lhs[matrix]
                        self.flipped[...] = self.last[...].T
                    for slot, chunk in enumerate(chunks):
                        self.turned[index, slot * CHUNK : (slot + 1) * CHUNK, :] = self.flipped[
                            chunk * CHUNK : (chunk + 1) * CHUNK, :
                        ]
                target = column + begin - first
                right = self.rhs[matrix]

                def tile(i, index=index, right=right, left_column=left_column, target=target):
                    here = pl.multiple_of(i * WIDE, WIDE)
                    ref[row : row + self.half, pl.ds(target + here, WIDE)] = times(
                        self.turned[index, pl.ds(pl.multiple_of(offset, CHUNK), self.half), :],
                        right[:, pl.ds(left_column + here, WIDE)],
                    ).astype(LOW)

                over_tiles(width // WIDE, tile)
            if not kept:
                self.send(
                    0, s, ref.at[pl.ds(row, self.half), pl.ds(column, columns)]
                )

    def send(self, step, s, source):
        first, columns, _ = self.streams[s]
        ref, column = self.landed[step]
        copy = remote(
            source,
            ref.at[:, pl.ds(column + first, columns)],
            self.send_sem.at[s, step],
            self.recv_sem.at[s, step],
            self.partners[self.orders[s][step]],
        )
        copy.start()
        self.copies[s, step] = copy

    def step(self, step, streams=range(4)):
        rows = self.half >> step
        for s in streams:
            first, columns, _ = self.streams[s]
            self.copies[s, step].wait()
            ref, row, column = self.held.find(first)
            mine = pl.ds(column, columns)
            landed, from_column = self.landed[step]
            theirs = pl.ds(from_column + first, columns)
            tile = min(rows, 64)

            def add(i, s=s, tile=tile, ref=ref, row=row, mine=mine, landed=landed, theirs=theirs):
                start = pl.multiple_of(i * tile, tile)
                here = pl.ds(pl.multiple_of(row + self.base[s] + start, tile), tile)
                ref[here, mine] = ref[here, mine] + landed[pl.ds(start, tile), theirs]

            over_tiles(rows // tile, add)
            if step == 2:
                self.spread(s)
                continue
            bit = self.bits[self.orders[s][step + 1]]
            away = pl.multiple_of(row + self.base[s] + (1 - bit) * (rows // 2), CHUNK)
            self.send(step + 1, s, ref.at[pl.ds(away, rows // 2), mine])
            self.base[s] = self.base[s] + bit * (rows // 2)

    def landing(self, s, mask):
        step, place_in = ((3, mask - 1), (4, mask - 5), (5, 0))[(mask > 4) + (mask > 6)]
        ref, column = self.landed[step]
        first, columns, _ = self.streams[s]
        return ref.at[pl.ds(place_in * CHUNK, CHUNK), pl.ds(column + first, columns)]

    def spread(self, s):
        first, columns, _ = self.streams[s]
        ref, row, column = self.held.find(first)
        dims = self.orders[s][3:]
        for mask, flipped in enumerate(masks(dims), 1):
            slot = 0
            for d in dims:
                slot = slot * 2 + (1 - self.bits[d] if d in flipped else self.bits[d])
            there = pl.multiple_of(row + self.base[s] + slot * CHUNK, CHUNK)
            copy = remote(
                ref.at[pl.ds(there, CHUNK), pl.ds(column, columns)],
                self.landing(s, mask),
                self.send_sem.at[s, 2 + mask],
                self.recv_sem.at[s, 2 + mask],
                self.flip(flipped),
            )
            copy.start()
            self.copies[s, 2 + mask] = copy

    def finish(self, out, streams=range(4)):
        for s in streams:
            first, columns, _ = self.streams[s]
            ref, row, column = self.held.find(first)
            slot = 0
            for d in self.orders[s][3:]:
                slot = slot * 2 + self.bits[d]
            mine = pl.multiple_of(row + self.base[s] + slot * CHUNK, CHUNK)
            total = ref[pl.ds(mine, CHUNK), pl.ds(column, columns)].astype(jnp.float32)
            for mask in range(1, 8):
                self.copies[s, 2 + mask].wait()
                total = total + self.landing(s, mask)[...].astype(jnp.float32)
            out[:, pl.ds(first, columns)] = total


def layer_kernel(early_streams, late_streams, *refs):
    (
        tokens, cotangent, positions, segments, frequencies, attention_gain, query_gain,
        key_gain, mlp_gain, wq_far, wk_far, wv_far, wo_far, wg_far, wu_far, wd_far, output,
        input_grad, early_out, late_out, gains, middle, grad_middle, partial_other, normed, query_raw, key_raw, query, kv, meta, cosine, sine, attended, normed_mlp,
        activated, gate_grad, up_grad, middle_low, attended_grad, inner, mlp_gain_grad, wq, wk,
        wv, wo, wg, wu, wd, bias, total, weight_sum, act_grad, part_out, part_in, flipped, turned, held,
        far_grad, gains_sent, gains_landed, weight_sem, kv_send, kv_recv, meta_send, meta_recv,
        pair_send, pair_recv, early_send, early_recv, late_send, late_recv, core_send,
        core_recv, far_send, far_recv, gains_send, gains_recv,
    ) = refs[: -11]
    early_landed, late_landed = refs[-11:-5], refs[-5:]
    mlp_out, mlp_other, partial = part_out.at[0], part_in.at[0], part_out.at[1]
    bits, partners, flip = place()
    dp, seq, tensor = lax.axis_index("dp"), lax.axis_index("seq"), lax.axis_index("tensor")
    core, y = seq % 2, seq // 2
    after, before, across = (y + 1) % 4, (y + 3) % 4, (y + 2) % 4
    near = (dp, y * 2 + 1 - core, tensor)
    ahead = (dp, after * 2 + core, tensor)
    behind = (dp, before * 2 + core, tensor)
    pair = (dp, seq, 1 - tensor)
    others = [(dp, (seq + step) % 8, tensor) for step in range(1, 8)]
    rows = tokens.shape[0]
    heads = kv.shape[2]
    hd = kv.shape[4]
    groups = {frozenset(m) for order in EARLY_ORDERS + LATE_ORDERS for m in masks(order[3:])}
    groups |= {frozenset((name,)) for name in ("x3", "x1", "z")}
    groups = sorted(sorted(group) for group in groups if group & {"x3", "x1", "z"})
    greet(others + [partners["tensor"]] + [flip(group) for group in groups])
    got_wk = Fetch(wk_far, wk, weight_sem, 0)
    got_wv = Fetch(wv_far, wv, weight_sem, 1)
    got_wq = Fetch(wq_far, wq, weight_sem, 2)

    meta[seq] = jnp.zeros_like(meta[seq])
    meta[seq, 0:1, :] = positions[...]
    meta[seq, 1:2, :] = segments[...]
    metas = [
        remote(meta.at[seq], meta.at[seq], meta_send.at[i], meta_recv.at[i], other)
        for i, other in enumerate(others)
    ]
    for copy in metas:
        copy.start()

    place_rows = jnp.broadcast_to(positions[...].astype(jnp.float32), (rows, rows)).T
    segment_rows = jnp.broadcast_to(segments[...].astype(jnp.float32), (rows, rows)).T
    angle = place_rows[:, :hd] * frequencies[...]
    cosine[...] = jnp.cos(angle)
    lane = lax.broadcasted_iota(jnp.int32, (rows, hd), 1)
    sine[...] = jnp.where(lane < hd // 2, -1.0, 1.0) * jnp.sin(angle)

    def turn(entries):
        return entries * cosine[...] + pltpu.roll(entries, hd // 2, 1) * sine[...]

    x = tokens[...].astype(jnp.float32)
    normed[...] = (x * inverse_rms(x) * attention_gain[...].astype(jnp.float32)[None, :]).astype(LOW)

    tile = 2 * hd
    got_wk.wait()

    def key_tile(i):
        raw = times(normed[...], wk[:, at_tile(i, tile)])
        key_raw[:, at_tile(i, tile)] = raw
        for g in range(2):
            head = raw[:, g * hd : (g + 1) * hd]
            scaled = head * inverse_rms(head) * key_gain[...].astype(jnp.float32)[None, :]
            kv[seq, 0, 2 * i + g] = turn(scaled).astype(LOW)

    over_tiles(heads // 2, key_tile)

    def own(half, kind, target, index):
        copy = remote(
            kv.at[seq, half], kv.at[seq, half], kv_send.at[index], kv_recv.at[kind, half], target
        )
        copy.start()
        return copy

    sends = [own(0, 1, ahead, 0), own(0, 2, behind, 1), own(0, 0, near, 2)]
    got_wv.wait()

    def value_tile(i):
        raw = times(normed[...], wv[:, at_tile(i, tile)]).astype(LOW)
        for g in range(2):
            kv[seq, 1, 2 * i + g] = raw[:, g * hd : (g + 1) * hd]

    over_tiles(heads // 2, value_tile)
    sends += [own(1, 1, ahead, 3), own(1, 2, behind, 4), own(1, 0, near, 5)]
    got_wq.wait()
    got_wo = Fetch(wo_far, wo, weight_sem, 3)
    got_wd = Fetch(wd_far, wd, weight_sem, 4)
    got_wg = Fetch(wg_far, wg, weight_sem, 5)
    got_wu = Fetch(wu_far, wu, weight_sem, 6)
    scale = math.log2(math.e) / math.sqrt(hd)

    def query_tile(i):
        raw = times(normed[...], wq[:, at_tile(i, tile)])
        query_raw[:, at_tile(i, tile)] = raw
        for g in range(2):
            head = raw[:, g * hd : (g + 1) * hd]
            scaled = head * inverse_rms(head) * (query_gain[...].astype(jnp.float32)[None, :] * scale)
            query[i, g * rows : (g + 1) * rows, :] = turn(scaled).astype(LOW)

    over_tiles(heads, query_tile)
    total[...] = jnp.zeros_like(total)
    weight_sum[...] = jnp.zeros_like(weight_sum)
    for copy in metas:
        copy.wait()

    def attend(slot):
        key_place = meta[slot, 0:1, :].astype(jnp.float32)
        key_segment = meta[slot, 1:2, :].astype(jnp.float32)
        allowed = (key_place <= place_rows) & (key_segment == segment_rows)
        bias[:, :rows] = jnp.where(allowed, 0.0, NEGATIVE)

        def head(j):
            scores = times_turned(query[j], kv[slot, 0, j])
            weights = jnp.concatenate(
                [jnp.exp2(scores[g * rows : (g + 1) * rows] + bias[:, :rows]) for g in range(2)], axis=0
            )
            weight_sum[j] += weights[:, :hd] + weights[:, hd:]
            total[j] += times(weights.astype(LOW), kv[slot, 1, j])

        over_tiles(heads, head)

    def arrived(slot, kind, half):
        remote(
            kv.at[slot, half], kv.at[slot, half], kv_send.at[0], kv_recv.at[kind, half], near
        ).wait_recv()

    def pass_on(slot, half, kind, target, index):
        copy = remote(
            kv.at[slot, half], kv.at[slot, half], kv_send.at[index], kv_recv.at[kind, half], target
        )
        copy.start()
        sends.append(copy)

    attend(seq)
    near_slot = y * 2 + 1 - core
    arrived(near_slot, 0, 0)
    arrived(near_slot, 0, 1)
    attend(near_slot)
    before_slot, after_slot, across_slot = before * 2 + core, after * 2 + core, across * 2 + core
    arrived(before_slot, 1, 0)
    pass_on(before_slot, 0, 3, ahead, 6)
    pass_on(before_slot, 0, 4, near, 7)
    arrived(after_slot, 2, 0)
    pass_on(after_slot, 0, 5, near, 8)
    arrived(after_slot, 2, 1)
    pass_on(after_slot, 1, 3, behind, 9)
    pass_on(after_slot, 1, 5, near, 10)
    arrived(before_slot, 1, 1)
    pass_on(before_slot, 1, 4, near, 11)
    attend(before_slot)
    attend(after_slot)
    for far_y, kind in ((before, 4), (after, 5)):
        slot = far_y * 2 + 1 - core
        arrived(slot, kind, 0)
        arrived(slot, kind, 1)
        attend(slot)
    arrived(across_slot, 3, 0)
    pass_on(across_slot, 0, 6, near, 12)
    arrived(across_slot, 3, 1)
    pass_on(across_slot, 1, 6, near, 13)
    attend(across_slot)
    far_slot = across * 2 + 1 - core
    arrived(far_slot, 6, 0)
    arrived(far_slot, 6, 1)
    attend(far_slot)

    def finish(j):
        inverse = 1.0 / jnp.sum(weight_sum[j], axis=-1, keepdims=True)
        result = total[j] * inverse
        total[j] = result
        weight_sum[j] = jnp.broadcast_to(inverse, result.shape)
        for g in range(2):
            attended[:, at_tile(2 * j + g, hd)] = result[g * rows : (g + 1) * rows].astype(LOW)

    over_tiles(heads, finish)
    got_wo.wait()
    wide = 256
    features = tokens.shape[1]
    hidden = wg.shape[1]

    def out_tile(i):
        part_out[0, :, at_tile(i, wide)] = times(attended[...], wo[:, at_tile(i, wide)]).astype(LOW)

    def in_halves(body, target, source, index):
        copies = []
        for part in range(2):
            count = features // wide // 2

            def tile_of_part(i, part=part):
                body(i + part * count)

            over_tiles(count, tile_of_part)
            here = pl.ds(part * features // 2, features // 2)
            copies.append(
                remote(
                    source.at[:, here],
                    target.at[:, here],
                    pair_send.at[index, part],
                    pair_recv.at[index, part],
                    pair,
                )
            )
            copies[-1].start()
        return copies

    def wait_all(copies):
        for copy in copies:
            copy.wait()

    first = in_halves(out_tile, part_in.at[0], part_out.at[0], 0)
    got_wd.wait()

    def act_grad_tile(i):
        act_grad[:, at_tile(i, wide)] = times_turned(cotangent[...], wd[at_tile(i, wide), :])

    over_tiles(hidden // wide, act_grad_tile)
    got_wg.wait()
    got_wu.wait()
    wait_all(first)
    mid = (
        tokens[...].astype(jnp.float32)
        + (part_out[0].astype(jnp.float32) + part_in[0].astype(jnp.float32))
    )
    middle[...] = mid
    normed_mlp[...] = (mid * inverse_rms(mid) * mlp_gain[...].astype(jnp.float32)[None, :]).astype(LOW)

    def hidden_tile(i):
        here = at_tile(i, wide)
        gate_here = times(normed_mlp[...], wg[:, here])
        up_here = times(normed_mlp[...], wu[:, here])
        sigmoid = 1.0 / (1.0 + jnp.exp(-gate_here))
        silu = gate_here * sigmoid
        grad = act_grad[:, here]
        activated[:, here] = (silu * up_here).astype(LOW)
        gate_grad[:, here] = (
            grad * up_here * sigmoid * (1.0 + gate_here * (1.0 - sigmoid))
        ).astype(LOW)
        up_grad[:, here] = (grad * silu).astype(LOW)

    over_tiles(hidden // wide, hidden_tile)

    def back_tile(i):
        here = at_tile(i, wide)
        part_out[1, :, here] = (
            times_turned(gate_grad[...], wg[here, :]) + times_turned(up_grad[...], wu[here, :])
        ).astype(LOW)

    second = in_halves(back_tile, part_in.at[1], part_out.at[1], 1)

    def down_tile(i):
        mlp_out[:, at_tile(i, wide)] = times(activated[...], wd[:, at_tile(i, wide)]).astype(LOW)

    over_tiles(features // wide, down_tile)
    half = features // 2
    early = Scatter(
        EARLY_ORDERS, early_streams, [normed_mlp, normed_mlp, cotangent, middle_low],
        [gate_grad, up_grad, activated, attended], flipped, turned,
        Panels(half, [(wg, 0, hidden), (wg, half, hidden), (wu, 0, hidden), (wu, half, hidden)]),
        Panels(half, [(held, 0, held.shape[1])]), [(ref, 0) for ref in early_landed],
        early_send, early_recv, bits, partners, flip,
    )
    for s in range(4):
        early.open(s)
    early.step(0, streams=range(4))
    for copy in sends:
        copy.wait_send()
    wait_all(second)
    mid = middle[...]
    inverse = inverse_rms(mid)
    dy = part_out[1].astype(jnp.float32) + part_in[1].astype(jnp.float32)
    mlp_gain_grad[...] = jnp.sum(dy * mid * inverse, axis=0, keepdims=True)
    scaled = dy * mlp_gain[...].astype(jnp.float32)[None, :]
    grad = (
        cotangent[...].astype(jnp.float32)
        + inverse * scaled
        - mid * (inverse * inverse * inverse) * jnp.mean(scaled * mid, axis=-1, keepdims=True)
    )
    grad_middle[...] = grad
    middle_low[...] = grad.astype(LOW)

    def attended_grad_tile(j):
        both = times_turned(middle_low[...], wo[at_tile(j, 2 * hd), :]).astype(LOW)
        both = both.astype(jnp.float32)
        for g in range(2):
            here = slice(g * rows, (g + 1) * rows)
            normal = both[:, g * hd : (g + 1) * hd] * weight_sum[j, here, :]
            attended_grad[j, here, :] = normal.astype(LOW)
            summed = jnp.sum((normal * total[j, here, :]).T, axis=0, keepdims=True)
            inner[j, :, here] = jnp.broadcast_to(summed, (8, rows))

    over_tiles(heads, attended_grad_tile)


    early.open(4)
    place_row = positions[...].astype(jnp.float32)
    segment_row = segments[...].astype(jnp.float32)
    act_grad[...] = jnp.zeros_like(act_grad)

    def query_turned(j):
        return pl.ds(pl.multiple_of(j % 2 * hd, hd), hd), at_tile(j // 2, 2 * rows)

    def block(slot, target, first):
        columns = meta[slot].astype(jnp.float32).T
        allowed = (columns[:, 0:1] <= place_row) & (columns[:, 1:2] == segment_row)
        one = jnp.where(allowed, 0.0, NEGATIVE)
        bias[:, :rows] = one
        bias[:, rows:] = one

        def head(j):
            key, value = kv[slot, 0, j], kv[slot, 1, j]
            weight = jnp.exp2(times_turned(key, query[j]) + bias[...])
            grad = times_turned(value, attended_grad[j])
            scores_grad = (weight * (grad - inner[j, 0:1, :])).astype(LOW)
            down = pl.ds(first, rows)
            target[down, at_tile(heads + j, hd)] = times(
                weight.astype(LOW), attended_grad[j]
            ).astype(LOW)
            target[down, at_tile(j, hd)] = (times(scores_grad, query[j]) * math.log(2)).astype(LOW)
            act_grad[query_turned(j)] += lax.dot_general(
                key, scores_grad, (((0,), (0,)), ((), ())), preferred_element_type=jnp.float32
            )

        over_tiles(heads, head)

    grad_width = 2 * heads * hd
    far_sends, crossing = [], []

    def grad_rows(ref, i):
        return ref.at[pl.ds(i * rows, rows), pl.ds(0, grad_width)]

    for i, shift in enumerate(SHIFTS):
        chip = (y + shift) % 4
        block(chip * 2 + 1 - core, wg, i * rows)
        copy = remote(
            grad_rows(wg, i), grad_rows(wd, i), core_send.at[i], core_recv.at[i], partners["core"]
        )
        copy.start()
        block(chip * 2 + core, wu, i * rows)
        copy.wait()
        down, wide_grad = slice(i * rows, (i + 1) * rows), slice(0, grad_width)
        wu[down, wide_grad] = wu[down, wide_grad] + wd[down, wide_grad]
        if shift:
            copy = remote(
                grad_rows(wu, i),
                far_grad.at[i],
                far_send.at[i],
                far_recv.at[i],
                (dp, chip * 2 + core, tensor),
            )
            copy.start()
            far_sends.append(copy)
        if i == 0:
            early.step(0, streams=range(4, 5))
        if i == 2:
            early.step(1)

    outward = remote(mlp_out, mlp_other, pair_send.at[2, 0], pair_recv.at[2, 0], pair)
    outward.start()

    def back(raw, gain, gradient):
        turned_back = gradient * cosine[...] - pltpu.roll(gradient, hd // 2, 1) * sine[...]
        inverse = inverse_rms(raw)
        scaled = turned_back * gain
        raw_grad = inverse * scaled - raw * (inverse * inverse * inverse) * jnp.mean(
            scaled * raw, axis=-1, keepdims=True
        )
        return raw_grad, jnp.sum(turned_back * raw * inverse, axis=0, keepdims=True)

    gains_sent[0] = jnp.zeros_like(gains_sent[0])
    query_gain_row = query_gain[...].astype(jnp.float32)[None, :]
    key_gain_row = key_gain[...].astype(jnp.float32)[None, :]

    def query_head(j):
        gradient = act_grad[query_turned(j)].T * (1.0 / math.sqrt(hd))
        for g in range(2):
            here = at_tile(2 * j + g, hd)
            raw_grad, part = back(
                query_raw[:, here], query_gain_row, gradient[g * rows : (g + 1) * rows]
            )
            attended[:, here] = raw_grad.astype(LOW)
            gains_sent[0, 2:3, :hd] += part

    over_tiles(heads, query_head)
    early.step(1, streams=range(4, 5))
    for copy in far_sends:
        copy.wait()

    def key_head(j):
        here, there = at_tile(j, hd), at_tile(heads + j, hd)
        key_sum = wu[3 * rows : 4 * rows, here].astype(jnp.float32)
        value_sum = wu[3 * rows : 4 * rows, there].astype(jnp.float32)
        for i in range(3):
            key_sum = key_sum + far_grad[i, :, here].astype(jnp.float32)
            value_sum = value_sum + far_grad[i, :, there].astype(jnp.float32)
        raw_grad, part = back(key_raw[:, here], key_gain_row, key_sum)
        gate_grad[:, here] = raw_grad.astype(LOW)
        up_grad[:, here] = value_sum.astype(LOW)
        gains_sent[0, 3:4, :hd] += part

    over_tiles(heads, key_head)
    late = Scatter(
        LATE_ORDERS, late_streams, [normed] * 3, [attended, gate_grad, up_grad], flipped, turned,
        Panels(half, [(wg, 0, hidden), (wg, half, hidden)]),
        Panels(half, [(wu, 0, hidden), (wu, half, hidden)]),
        [(early_landed[0], 0)] + [(ref, 0) for ref in late_landed],
        late_send, late_recv, bits, partners, flip,
    )
    for s in range(4):
        late.open(s)
    x = tokens[...].astype(jnp.float32)
    inverse = inverse_rms(x)
    k_width = wk.shape[1]

    def partial_tile(i):
        here = at_tile(i, WIDE)
        result = (
            times_turned(attended[...], wq[here, :])
            + times_turned(gate_grad[:, :k_width], wk[here, :])
            + times_turned(up_grad[:, :k_width], wv[here, :])
        )
        partial[:, here] = result.astype(LOW)
        gains_sent[0, 0:1, here] = jnp.sum(
            result * (tokens[:, here].astype(jnp.float32) * inverse), axis=0, keepdims=True
        )

    outward_partial = in_halves(partial_tile, partial_other, partial, 3)
    gains_sent[0, 1:2, :] = 0.5 * mlp_gain_grad[...]
    gain_steps = (
        [(partners["tensor"])],
        [(partners["core"])],
        [flip(m) for m in (("x3",), ("x1",), ("x3", "x1"))],
        [flip(m) for m in masks(("y3", "y1", "z"))],
    )

    def send_gains(step):
        first = (0, 1, 2, 5)[step]
        copies = [
            remote(
                gains_sent.at[step], gains_landed.at[first + i], gains_send.at[first + i],
                gains_recv.at[first + i], partner,
            )
            for i, partner in enumerate(gain_steps[step])
        ]
        for copy in copies:
            copy.start()
        return copies

    def next_gains(step, copies):
        first = (0, 1, 2, 5)[step]
        sum_so_far = gains_sent[step]
        for i, copy in enumerate(copies):
            copy.wait()
            sum_so_far = sum_so_far + gains_landed[first + i]
        if step == 3:
            gains[...] = sum_so_far
            return None
        gains_sent[step + 1] = sum_so_far
        return send_gains(step + 1)

    gains_copy = send_gains(0)
    early.step(2, streams=range(5))
    for step in range(3):
        late.step(step)
        gains_copy = next_gains(step, gains_copy)
        if step == 1:
            early.finish(early_out)
            outward.wait()
            both = mlp_out[...].astype(jnp.float32) + mlp_other[...].astype(jnp.float32)
            output[...] = (middle[...] + both).astype(LOW)
        if step == 2:
            early.finish(early_out, streams=range(4, 5))
            wait_all(outward_partial)
            scaled = (
                partial[...].astype(jnp.float32) + partial_other[...].astype(jnp.float32)
            ) * attention_gain[...].astype(jnp.float32)[None, :]
            across_mean = jnp.mean(scaled * x, axis=-1, keepdims=True)
            input_grad[...] = (
                grad_middle[...] + inverse * scaled - x * (inverse * inverse * inverse) * across_mean
            ).astype(LOW)
    late.finish(late_out)
    next_gains(3, gains_copy)


def layer(
    tokens, cotangent, positions, segments, attention_gain, query_weight, key_weight, value_weight,
    query_gain, key_gain, out_weight, mlp_gain, gate_weight, up_weight, down_weight,
):
    rows, features = tokens.shape
    hd = query_gain.shape[0]
    heads = key_weight.shape[1] // hd
    half = features // 2
    q_width, k_width, hidden = query_weight.shape[1], key_weight.shape[1], gate_weight.shape[1]
    early_streams = split_streams((hidden, hidden, hidden, q_width), EARLY_TILES)
    late_streams = split_streams((q_width, k_width, k_width), LATE_TILES)
    early_width = 3 * hidden + q_width
    late_width = q_width + 2 * k_width
    pairs = jnp.arange(hd // 2, dtype=jnp.float32)
    inverse = 1.0 / ROPE_BASE ** (pairs * 2.0 / hd)
    frequencies = jnp.concatenate([inverse, inverse])[None]
    vmem = pl.BlockSpec(memory_space=pltpu.VMEM)
    far = pl.BlockSpec(memory_space=pl.ANY)
    f32 = jnp.float32
    outs = dict(
        output=((rows, features), LOW),
        input_grad=((rows, features), LOW),
        early=((CHUNK, early_width), f32),
        late=((CHUNK, late_width), f32),
        gains=((8, features), f32),
    )
    results = pl.pallas_call(
        functools.partial(layer_kernel, early_streams, late_streams),
        out_shape=[jax.ShapeDtypeStruct(shape, kind) for shape, kind in outs.values()],
        in_specs=[vmem] * 9 + [far] * 7,
        out_specs=[vmem] * len(outs),
        scratch_shapes=[
            pltpu.VMEM((rows, features), f32),
            pltpu.VMEM((rows, features), f32),
            pltpu.VMEM((rows, features), LOW),
            pltpu.VMEM((rows, features), LOW),
            pltpu.VMEM((rows, q_width), f32),
            pltpu.VMEM((rows, k_width), f32),
            pltpu.VMEM((heads, 2 * rows, hd), LOW),
            pltpu.VMEM((8, 2, heads, rows, hd), LOW),
            pltpu.VMEM((8, 8, rows), jnp.int32),
            pltpu.VMEM((rows, hd), f32),
            pltpu.VMEM((rows, hd), f32),
            pltpu.VMEM((rows, q_width), LOW),
            pltpu.VMEM((rows, features), LOW),
            pltpu.VMEM((rows, hidden), LOW),
            pltpu.VMEM((rows, hidden), LOW),
            pltpu.VMEM((rows, hidden), LOW),
            pltpu.VMEM((rows, features), LOW),
            pltpu.VMEM((heads, 2 * rows, hd), LOW),
            pltpu.VMEM((heads, 8, 2 * rows), f32),
            pltpu.VMEM((1, features), f32),
            pltpu.VMEM(query_weight.shape, LOW),
            pltpu.VMEM(key_weight.shape, LOW),
            pltpu.VMEM(value_weight.shape, LOW),
            pltpu.VMEM(out_weight.shape, LOW),
            pltpu.VMEM(gate_weight.shape, LOW),
            pltpu.VMEM(up_weight.shape, LOW),
            pltpu.VMEM(down_weight.shape, LOW),
            pltpu.VMEM((rows, 2 * rows), f32),
            pltpu.VMEM((heads, 2 * rows, hd), f32),
            pltpu.VMEM((heads, 2 * rows, hd), f32),
            pltpu.VMEM((rows, hidden), f32),
            pltpu.VMEM((2, rows, features), LOW),
            pltpu.VMEM((2, rows, features), LOW),
            pltpu.VMEM((features, rows), LOW),
            pltpu.VMEM((1, features, rows), LOW),
            pltpu.VMEM((half, early_width), LOW),
            pltpu.VMEM((3, rows, 2 * k_width), LOW),
            pltpu.VMEM((4, 8, features), f32),
            pltpu.VMEM((12, 8, features), f32),
            pltpu.SemaphoreType.DMA((7, 4)),
            pltpu.SemaphoreType.DMA((14,)),
            pltpu.SemaphoreType.DMA((7, 2)),
            pltpu.SemaphoreType.DMA((7,)),
            pltpu.SemaphoreType.DMA((7,)),
            pltpu.SemaphoreType.DMA((4, 2)),
            pltpu.SemaphoreType.DMA((4, 2)),
            pltpu.SemaphoreType.DMA((5, 10)),
            pltpu.SemaphoreType.DMA((5, 10)),
            pltpu.SemaphoreType.DMA((5, 10)),
            pltpu.SemaphoreType.DMA((5, 10)),
            pltpu.SemaphoreType.DMA((4,)),
            pltpu.SemaphoreType.DMA((4,)),
            pltpu.SemaphoreType.DMA((3,)),
            pltpu.SemaphoreType.DMA((3,)),
            pltpu.SemaphoreType.DMA((12,)),
            pltpu.SemaphoreType.DMA((12,)),
        ]
        + [pltpu.VMEM((half >> step, early_width), LOW) for step in range(6)]
        + [pltpu.VMEM((half >> step, late_width), LOW) for step in range(1, 6)],
        compiler_params=pltpu.CompilerParams(
            collective_id=0, has_side_effects=True, vmem_limit_bytes=63 * 1024 * 1024
        ),
    )(
        tokens, cotangent, positions, segments, frequencies, attention_gain, query_gain, key_gain,
        mlp_gain, query_weight, key_weight, value_weight, out_weight, gate_weight, up_weight,
        down_weight,
    )
    return dict(zip(outs, results))


def finish_kernel(
    output_in, input_grad_in, early, late, gains, output, input_grad, grad_query, grad_key,
    grad_value, grad_out, grad_gate, grad_up, grad_down, attention_gain, mlp_gain, query_gain,
    key_gain,
):
    hidden, q_width, k_width = grad_gate.shape[1], grad_query.shape[1], grad_key.shape[1]
    output[...] = output_in[...]
    input_grad[...] = input_grad_in[...]
    grad_gate[...] = early[:, :hidden]
    grad_up[...] = early[:, hidden : 2 * hidden]
    grad_down[...] = early[:, 2 * hidden : 3 * hidden]
    grad_out[...] = early[:, 3 * hidden :]
    grad_query[...] = late[:, :q_width]
    grad_key[...] = late[:, q_width : q_width + k_width]
    grad_value[...] = late[:, q_width + k_width :]
    chunk = lax.axis_index("dp") * 8 + lax.axis_index("seq")
    features = gains.shape[1]
    wide = pltpu.roll(gains[0:8, :], lax.rem(features - chunk * CHUNK, features), 1)
    thin = pltpu.roll(gains[0:8, :128], lax.rem(128 - chunk * 2, 128), 1)
    attention_gain[...] = wide[0:1, : attention_gain.shape[1]]
    mlp_gain[...] = wide[1:2, : mlp_gain.shape[1]]
    query_gain[...] = thin[2:3, : query_gain.shape[1]]
    key_gain[...] = thin[3:4, : key_gain.shape[1]]


def finish(f, widths):
    q_width, k_width, hidden = widths
    rows, features = f["output"].shape
    f32 = jnp.float32
    vmem = pl.BlockSpec(memory_space=pltpu.VMEM)
    shapes = (
        ((rows, features), LOW), ((rows, features), LOW), ((CHUNK, q_width), f32),
        ((CHUNK, k_width), f32), ((CHUNK, k_width), f32), ((CHUNK, q_width), f32),
        ((CHUNK, hidden), f32), ((CHUNK, hidden), f32), ((CHUNK, hidden), f32),
        ((1, CHUNK), f32), ((1, CHUNK), f32), ((1, 2), f32), ((1, 2), f32),
    )
    return pl.pallas_call(
        finish_kernel,
        out_shape=[jax.ShapeDtypeStruct(shape, kind) for shape, kind in shapes],
        in_specs=[vmem] * 5,
        out_specs=[vmem] * len(shapes),
        compiler_params=pltpu.CompilerParams(vmem_limit_bytes=60 * 1024 * 1024),
    )(f["output"], f["input_grad"], f["early"], f["late"], f["gains"])


def shards(
    tokens,
    cotangent,
    positions,
    segments,
    attention_gain,
    query_weight,
    key_weight,
    value_weight,
    query_gain,
    key_gain,
    out_weight,
    mlp_gain,
    gate_weight,
    up_weight,
    down_weight,
):
    f = layer(
        tokens[0], cotangent[0], positions, segments, attention_gain, query_weight,
        key_weight, value_weight, query_gain, key_gain, out_weight, mlp_gain,
        gate_weight, up_weight, down_weight,
    )
    results = finish(
        f, (query_weight.shape[1], key_weight.shape[1], gate_weight.shape[1])
    )
    output, input_grad, query, key, value, out, gate, up, down, *gains = results
    return (
        output[None],
        input_grad[None],
        query,
        key,
        value,
        out.T,
        gate,
        up,
        down.T,
        *(gain[0] for gain in gains),
    )


def solution(mesh):
    return jax.shard_map(
        shards,
        mesh=mesh,
        in_specs=(
            P("dp", "seq", None),
            P("dp", "seq", None),
            P("dp", "seq"),
            P("dp", "seq"),
            P(),
            P(None, "tensor"),
            P(None, "tensor"),
            P(None, "tensor"),
            P(),
            P(),
            P("tensor", None),
            P(),
            P(None, "tensor"),
            P(None, "tensor"),
            P("tensor", None),
        ),
        out_specs=(
            P("dp", "seq", None),
            P("dp", "seq", None),
            P(("dp", "seq"), "tensor"),
            P(("dp", "seq"), "tensor"),
            P(("dp", "seq"), "tensor"),
            P("tensor", ("dp", "seq")),
            P(("dp", "seq"), "tensor"),
            P(("dp", "seq"), "tensor"),
            P("tensor", ("dp", "seq")),
            P(("dp", "seq")),
            P(("dp", "seq")),
            P(("dp", "seq")),
            P(("dp", "seq")),
        ),
        check_vma=False,
    )
```
